256 devices in a mesh: dp: 32 (over y_lo, z, core), mp: 8 (over x, y_hi).
Axes of the slice: x: 4, y: 4 (y_hi: 2, y_lo: 2; y = y_hi * 2 + y_lo), z: 8, core: 2. Of those that a mesh axis runs over, the one named last changes fastest.
Arguments:
- img_features: bfloat16 [8192, 1152], P(('dp', 'mp')), may hold values from -8 to 8
- txt_features: bfloat16 [8192, 1152], P(('dp', 'mp')), may hold values from -8 to 8
- img_weight: bfloat16 [1152, 1152], P('mp'), may hold values from -1 to 1
- txt_weight: bfloat16 [1152, 1152], P('mp'), may hold values from -1 to 1
- img_bias: float32 [1152], replicated, may hold values from -2.5 to 2.5
- txt_bias: float32 [1152], replicated, may hold values from -2.5 to 2.5
- log_scale: float32 [1], replicated, may hold values from 1.8 to 2.3
- logit_bias: float32 [1], replicated, may hold values from -8 to -4
Outputs:
- mean_loss: float32 [1], replicated
- scale_grads: float32 [2], replicated
- img_feature_grad: bfloat16 [8192, 1152], P(('dp', 'mp'))
- txt_feature_grad: bfloat16 [8192, 1152], P(('dp', 'mp'))
- img_weight_grad: float32 [1152, 1152], P('mp', 'dp')
- txt_weight_grad: float32 [1152, 1152], P('mp', 'dp')
- bias_grads: float32 [2, 1152], replicated
The draws below stay inside these ranges and needn't reach their ends.
All inputs are finite; a program needn't handle non-finite values.
Results may differ from the reference program's by a relative error of at most 0.0047.
Values may be sent and summed in bfloat16 or wider, within the bound.
A program may use at most 128 MiB of HBM per device.

```python
import math
import jax
import jax.numpy as jnp
from jax import lax

D = 1152
E = 1152
B = 8192


def mixed_noise(key, shape):
    gauss = jax.random.normal(key, shape, jnp.float32)
    return gauss


def pair_latent(key):
    key = jax.random.fold_in(key, 101)
    key_coef, key_basis, key_own = jax.random.split(key, 3)
    coef = jax.random.normal(key_coef, (B, 4), jnp.float32)
    basis = jax.random.normal(key_basis, (4, D), jnp.float32)
    low = 0.5 * (coef[:, 0:1] * basis[0:1, :] + coef[:, 1:2] * basis[1:2, :] + coef[:, 2:3] * basis[2:3, :] + coef[:, 3:4] * basis[3:4, :])
    own = mixed_noise(key_own, (B, D))
    return 0.8 * low + 0.6 * own


def feature_rows(key, shared, scale_lo, scale_hi):
    key_noise, key_scale = jax.random.split(key, 2)
    noise = mixed_noise(key_noise, (B, D))
    scales = jnp.exp(jax.random.uniform(key_scale, (B, 1), jnp.float32, math.log(scale_lo), math.log(scale_hi)))
    return jnp.clip(scales * (0.8 * shared + 0.6 * noise), -8.0, 8.0).astype(jnp.bfloat16)


def head_base(key):
    key = jax.random.fold_in(key, 202)
    return jnp.clip(mixed_noise(key, (D, E)), -4.0, 4.0)


def head_rows(key, base):
    own = jnp.clip(mixed_noise(key, (D, E)), -4.0, 4.0)
    return ((base + 0.4 * own) * (1.16 * D) ** (-0.5)).astype(jnp.bfloat16)


def draw_img_features(key, part):
    scale_lo, scale_hi = (0.7, 1.6)
    shared = pair_latent(key)
    key = jax.random.fold_in(key, 3)
    return feature_rows(key, shared, scale_lo, scale_hi)


def draw_txt_features(key, part):
    scale_lo, scale_hi = (0.7, 1.6)
    shared = pair_latent(key)
    key = jax.random.fold_in(key, 4)
    return feature_rows(key, shared, scale_lo, scale_hi)


def draw_img_weight(key, part):
    base = head_base(key)
    key = jax.random.fold_in(key, 5)
    return head_rows(key, base)


def draw_txt_weight(key, part):
    base = head_base(key)
    key = jax.random.fold_in(key, 6)
    return head_rows(key, base)


def centred(rng, dims, scale, most, kind=jnp.bfloat16):
    result = scale * jax.random.normal(rng, dims, jnp.float32)
    return jnp.clip(result, min=-most, max=most).astype(kind)


def setup_inputs(seed: int = 0) -> dict:
    arg_keys = jax.random.split(jax.random.key(seed), 9)
    return {
        "img_features": draw_img_features(jax.random.fold_in(arg_keys[8], 71), 0),
        "txt_features": draw_txt_features(jax.random.fold_in(arg_keys[8], 71), 0),
        "img_weight": draw_img_weight(jax.random.fold_in(arg_keys[8], 71), 0),
        "txt_weight": draw_txt_weight(jax.random.fold_in(arg_keys[8], 71), 0),
        "img_bias": centred(arg_keys[4], (E,), 0.5, 2.5, jnp.float32),
        "txt_bias": centred(arg_keys[5], (E,), 0.5, 2.5, jnp.float32),
        "log_scale": jnp.clip(jax.random.uniform(arg_keys[6], (1,), jnp.float32, 1.8, 2.3), 1.8, 2.3),
        "logit_bias": jnp.clip(jax.random.uniform(arg_keys[7], (1,), jnp.float32, -8.0, -4.0), -8.0, -4.0),
    }


epsilon = 1e-06
LOSS_FACTOR = 32.0

def project_rows(features, weight, bias):
    pre = jnp.dot(features, weight, preferred_element_type=jnp.float32) + bias
    inverse = lax.rsqrt(lax.optimization_barrier(jnp.sum(pre * pre, axis=1, keepdims=True)) + epsilon)
    unit = pre * inverse
    return (unit, inverse, unit.astype(jnp.bfloat16))

def norm_backward(grad, unit, inverse):
    return inverse * (grad - unit * lax.optimization_barrier(jnp.sum(unit * grad, axis=1, keepdims=True)))

def reference(img_features, txt_features, img_weight, txt_weight, img_bias, txt_bias, log_scale, logit_bias):
    unit_img, inv_img, emb_img = project_rows(img_features, img_weight, img_bias)
    unit_txt, inv_txt, emb_txt = project_rows(txt_features, txt_weight, txt_bias)
    logit_scale = jnp.exp(log_scale[0])
    logit_shift = logit_bias[0]
    batch_rows = img_features.shape[0]
    block_rows = 512 if batch_rows % 512 == 0 else batch_rows
    col_index = jnp.arange(batch_rows, dtype=jnp.int32)[None, :]

    def block_step(loop_state, first_row):
        text_grad, statistics = loop_state
        image_rows = lax.dynamic_slice_in_dim(emb_img, first_row, block_rows, 0)
        logits = logit_scale * jnp.dot(image_rows, emb_txt.T, preferred_element_type=jnp.float32) + logit_shift
        row_index = first_row + jnp.arange(block_rows, dtype=jnp.int32)[:, None]
        target = (col_index == row_index).astype(jnp.float32)
        errors = jax.nn.sigmoid(logits) - target
        weights = (LOSS_FACTOR * errors).astype(jnp.bfloat16)
        image_part = logit_scale * jnp.dot(weights, emb_txt, preferred_element_type=jnp.float32)
        text_grad = text_grad + logit_scale * jnp.dot(weights.T, image_rows, preferred_element_type=jnp.float32)
        pair_loss = jax.nn.softplus(-(2.0 * target - 1.0) * logits)
        stat_part = jnp.stack([jnp.sum(pair_loss), LOSS_FACTOR * jnp.sum(errors * (logits - logit_shift)), LOSS_FACTOR * jnp.sum(errors)])
        return ((text_grad, statistics + stat_part), image_part)
    first_rows = jnp.arange(batch_rows // block_rows, dtype=jnp.int32) * block_rows
    start_state = (jnp.zeros(emb_txt.shape, jnp.float32), jnp.zeros((3,), jnp.float32))
    (text_grad, statistics), image_blocks = lax.scan(block_step, start_state, first_rows)
    image_grad = image_blocks.reshape(batch_rows, emb_img.shape[1])
    delta_img = norm_backward(image_grad, unit_img, inv_img)
    delta_txt = norm_backward(text_grad, unit_txt, inv_txt)
    delta_img16 = delta_img.astype(jnp.bfloat16)
    delta_txt16 = delta_txt.astype(jnp.bfloat16)
    img_feature_grad = jnp.dot(delta_img16, img_weight.T, preferred_element_type=jnp.float32).astype(jnp.bfloat16)
    txt_feature_grad = jnp.dot(delta_txt16, txt_weight.T, preferred_element_type=jnp.float32).astype(jnp.bfloat16)
    img_weight_grad = jnp.dot(img_features.T, delta_img16, preferred_element_type=jnp.float32)
    txt_weight_grad = jnp.dot(txt_features.T, delta_txt16, preferred_element_type=jnp.float32)
    bias_grads = jnp.stack([lax.optimization_barrier(jnp.sum(delta_img, axis=0)), lax.optimization_barrier(jnp.sum(delta_txt, axis=0))])
    mean_loss = statistics[0:1] / batch_rows
    scale_grads = statistics[1:3]
    return (mean_loss, scale_grads, img_feature_grad, txt_feature_grad, img_weight_grad, txt_weight_grad, bias_grads)
```

```python
import functools

import jax
import jax.numpy as jnp
from jax import lax
from jax.experimental import pallas as pl
from jax.experimental.pallas import tpu as pltpu
from jax.sharding import PartitionSpec as P

EPSILON = 1e-06
LOSS_FACTOR = 32.0
NX, NY, NZ = 4, 4, 8
ROWS = 32
D = 1152
E = 1152
SHARD = 144
KX = 2 * SHARD
MESH = pl.DeviceIdType.MESH
F32 = jnp.float32
BF16 = jnp.bfloat16

N_COPIES = 128


class Links:
    def __init__(self, send_sems, recv_sems):
        dp, mp = lax.axis_index("dp"), lax.axis_index("mp")
        self.x, self.y = mp // 2, (mp % 2) * 2 + dp // 16
        self.z, self.c = (dp // 2) % NZ, dp % 2
        self.send_sems, self.recv_sems = send_sems, recv_sems
        self.started = []

    def at(self, dx=0, dy=0, dz=0, dc=0):
        x, y = (self.x + dx) % NX, (self.y + dy) % NY
        z, c = (self.z + dz) % NZ, (self.c + dc) % 2
        return ((y % 2) * 16 + z * 2 + c, x * 2 + y // 2)

    def send(self, src, dst, device):
        k = len(self.started)
        copy = pltpu.make_async_remote_copy(
            src_ref=src,
            dst_ref=dst,
            send_sem=self.send_sems.at[k],
            recv_sem=self.recv_sems.at[k],
            device_id=device,
            device_id_type=MESH,
        )
        copy.start()
        self.started.append(copy)
        return copy


def matmul(a, b):
    return lax.dot_general(a, b, (((1,), (0,)), ((), ())), preferred_element_type=F32)


def matmul_bt(a, b):
    return lax.dot_general(a, b, (((1,), (1,)), ((), ())), preferred_element_type=F32)


def matmul_at(a, b):
    return lax.dot_general(a, b, (((0,), (0,)), ((), ())), preferred_element_type=F32)


def wait_all(copies):
    for copy in copies:
        copy.wait_recv()


def kernel(
    f_img, f_txt, w_img, w_txt, b_img, b_txt, log_scale, logit_bias,
    o_loss, o_scale, o_fi, o_ft, o_wi, o_wt, o_bias,
    fs, fk, wk, po, pk, rp0, rp, unit, inv, ia, ta, wt, tg, tgx, tgs, rt, ig0, igs, ri,
    d16, dk, bp, bx, by, bz, bs, dfs, rf, g32, gy, ry, gz32, gz, rz, fin, ow,
    send_sems, recv_sems,
):
    link = Links(send_sems, recv_sems)
    x, y, z, c = link.x, link.y, link.z, link.c

    peers = [(0, 0, 0, 1)]
    peers += [(i, j, 0, 0) for i in range(NX) for j in range(NY) if (i, j) != (0, 0)]
    peers += [(i, 0, 0, 1) for i in range(1, NX)]
    peers += [(0, 0, k, 0) for k in range(1, NZ)]
    barrier = pltpu.get_barrier_semaphore()
    for p in peers:
        pl.semaphore_signal(barrier, inc=1, device_id=link.at(*p), device_id_type=MESH)

    shard = y // 2

    @pl.when(c == 0)
    def _():
        wk[shard] = w_img[...]

    @pl.when(c == 1)
    def _():
        wk[shard] = w_txt[...]

    for k in range(NX):
        fs[0, k] = f_img[:, KX * k : KX * (k + 1)]
        fs[1, k] = f_txt[:, KX * k : KX * (k + 1)]
    pl.semaphore_wait(barrier, len(peers))

    partner = jnp.where(y % 2 == 1, 1, 3)
    got_w = link.send(wk.at[shard], wk.at[shard], link.at(dy=partner))
    got_f = []
    for r in range(NX):
        for e in range(2):
            if (r, e) == (0, 0):
                fk[0] = fs[c, x]
                continue
            got_f.append(
                link.send(
                    fs.at[(c + e) % 2, (x + r) % NX],
                    fk.at[((NX - r) % NX) * 2 + e],
                    link.at(dx=r, dc=e),
                )
            )
    wait_all(got_f)
    got_w.wait_recv()

    part = matmul(fk[...].reshape(8 * ROWS, KX), wk[...].reshape(KX, E))
    rp0[0] = part[:ROWS]
    po[...] = part[ROWS : 2 * ROWS]
    pk[...] = part[2 * ROWS :].astype(BF16).reshape(6, ROWS, E)
    got_p = [link.send(po, rp0.at[1], link.at(dc=1))]
    for r in range(1, NX):
        for e in range(2):
            got_p.append(
                link.send(pk.at[(r - 1) * 2 + e], rp.at[e, NX - r - 1], link.at(dx=r, dc=e))
            )
    wait_all(got_p)
    for t, bias in enumerate((b_img, b_txt)):
        e = (c + t) % 2
        pre = rp0[e] + bias[...]
        for r in range(NX - 1):
            pre = pre + rp[e, r].astype(F32)
        inverse = lax.rsqrt(jnp.sum(pre * pre, axis=1, keepdims=True) + EPSILON)
        unit[t] = pre * inverse
        inv[t] = jnp.broadcast_to(inverse, (ROWS, 128))
    ia[0] = unit[0].astype(BF16)
    ta[0] = unit[1].astype(BF16)

    got_t = [link.send(ta.at[0], ta.at[NZ - k], link.at(dz=k)) for k in (1, 7, 2, 6, 3, 5, 4)]
    got_s = [link.send(ta.at[0], ta.at[NZ], link.at(dc=1))]
    got_i = []
    for i in range(NX):
        for j in range(NY):
            if (i, j) != (0, 0):
                slot = ((NX - i) % NX) * NY + (NY - j) % NY
                got_i.append(link.send(ia.at[0], ia.at[slot], link.at(dx=i, dy=j)))
    for copy, k in zip(got_t, (1, 7, 2, 6, 3, 5, 4)):
        copy.wait_recv()
        got_s.append(link.send(ta.at[NZ - k], ta.at[NZ + NZ - k], link.at(dc=1)))
    wait_all(got_i)

    half = NZ * ROWS
    scale = jnp.exp(jnp.full((1, 1), log_scale[0], F32))
    shift = logit_bias[0]
    images = ia[...].reshape(16 * ROWS, E)
    stats = []
    for h in range(2):
        if h == 1:
            wait_all(got_s)
        texts = ta[NZ * h : NZ * (h + 1)].reshape(half, E)
        scaled = scale * matmul_bt(texts, images)
        logits = scaled + shift
        signed = logits
        if h == 0:
            row = lax.broadcasted_iota(jnp.int32, logits.shape, 0)
            col = lax.broadcasted_iota(jnp.int32, logits.shape, 1)
            match = jnp.logical_and(row == col, col < ROWS)
            signed = jnp.where(match, -logits, logits)
        small = jnp.exp(-jnp.abs(logits))
        loss = jnp.maximum(signed, 0.0) + jnp.log1p(small)
        errors = jnp.where(logits >= 0.0, 1.0, small) / (1.0 + small)
        if h == 0:
            errors = errors - match.astype(F32)
        weights = (LOSS_FACTOR * errors).astype(BF16)
        sums = (loss, LOSS_FACTOR * errors * scaled, LOSS_FACTOR * errors)
        stats.append([jnp.sum(v, axis=0, keepdims=True) for v in sums])
        wt[:, half * h : half * (h + 1)] = weights.T
        grad = matmul(weights, images)
        if h == 0:
            tg[...] = grad.reshape(NZ, ROWS, E)
        else:
            tgx[...] = grad.reshape(NZ, ROWS, E)
    got_x = link.send(tgx, tgs, link.at(dc=1))

    texts = ta[...].reshape(16 * ROWS, E)
    got_ig = []
    for q in range(4):
        grad = matmul(wt[128 * q : 128 * (q + 1), :], texts).reshape(4, ROWS, E)
        if q == 0:
            ig0[...] = grad[0]
        igs[4 * q : 4 * (q + 1)] = grad.astype(BF16)
        for slot in range(4 * q, 4 * q + 4):
            if slot:
                got_ig.append(
                    link.send(igs.at[slot], ri.at[slot - 1], link.at(dx=slot // 4, dy=slot % 4))
                )
        if q == 0:
            got_x.wait_recv()
            tg[...] = tg[...] + tgs[...]
            tgx16 = tg[1:].astype(BF16)
            rt[1, ...] = tgx16
            got_tg = [
                link.send(rt.at[1, k - 1], rt.at[0, k - 1], link.at(dz=k))
                for k in (4, 3, 5, 2, 6, 1, 7)
            ]

    wait_all(got_tg)
    grad_txt = tg[0]
    for k in range(NZ - 1):
        grad_txt = grad_txt + rt[0, k].astype(F32)
    wait_all(got_ig)
    grad_img = ig0[...]
    for k in range(NX * NY - 1):
        grad_img = grad_img + ri[k].astype(F32)
    for t, grad in enumerate((grad_img, grad_txt)):
        grad = scale * grad
        delta = inv[t, :, 0:1] * (grad - unit[t] * jnp.sum(unit[t] * grad, axis=1, keepdims=True))
        d16[t] = delta.astype(BF16)
        total = jnp.sum(delta, axis=0, keepdims=True)
        for k in range(9):
            bp[9 * t + k : 9 * t + k + 1, :] = total[:, 128 * k : 128 * (k + 1)]
    for k in range(3):
        lanes = stats[0][k] + stats[1][k]
        bp[18 + k : 19 + k, :] = (
            lanes[:, 0:128] + lanes[:, 128:256] + lanes[:, 256:384] + lanes[:, 384:512]
        )
    bp[21:24, :] = jnp.zeros((3, 128), F32)

    got_d = []
    for r in range(NX):
        for e in range(2):
            if (r, e) == (0, 0):
                dk[0] = d16[c]
                continue
            got_d.append(
                link.send(
                    d16.at[(c + e) % 2], dk.at[((NX - r) % NX) * 2 + e], link.at(dx=r, dc=e)
                )
            )
    got_b = [link.send(bp, bx.at[r - 1], link.at(dx=r)) for r in range(1, NX)]
    wait_all(got_d)

    deltas = dk[...].reshape(8 * ROWS, E)
    grad_w = matmul_at(fk[...].reshape(8 * ROWS, KX), deltas)
    for j in range(NY):
        part = grad_w[SHARD * (j // 2) : SHARD * (j // 2 + 1), (E // 2) * (j % 2) : (E // 2) * (j % 2 + 1)]
        g32[j] = part
        gy[j] = part.astype(BF16)
    got_y = [link.send(gy.at[(y + j) % NY], ry.at[j - 1], link.at(dy=j)) for j in (2, 1, 3)]
    wait_all(got_b)
    by[0] = bp[...] + bx[0] + bx[1] + bx[2]
    got_b = [link.send(by.at[0], by.at[j], link.at(dy=j)) for j in range(1, NY)]

    grad_f = matmul_bt(deltas, wk[...].reshape(KX, E)).astype(BF16)
    dfs[...] = grad_f.reshape(8, ROWS, KX)
    got_df = []
    for r in range(NX):
        for e in range(2):
            if (r, e) == (0, 0):
                rf[0, x] = dfs[0]
                continue
            got_df.append(link.send(dfs.at[r * 2 + e], rf.at[e, x], link.at(dx=r, dc=e)))

    wait_all(got_y)
    total = g32[y]
    for j in range(NY - 1):
        total = total + ry[j].astype(F32)
    for k in range(NZ):
        part = total[:, 72 * k : 72 * (k + 1)]
        gz32[k] = part
        gz[k] = part.astype(BF16)
    got_z = [link.send(gz.at[(z + k) % NZ], rz.at[k - 1], link.at(dz=k)) for k in (4, 3, 5, 2, 6, 1, 7)]
    wait_all(got_b)
    bz[0] = by[0] + by[1] + by[2] + by[3]
    got_b = [link.send(bz.at[0], bz.at[k], link.at(dz=k)) for k in range(1, NZ)]

    wait_all(got_df)
    for t, out in enumerate((o_fi, o_ft)):
        for k in range(NX):
            out[:, KX * k : KX * (k + 1)] = rf[(c + t) % 2, k]

    wait_all(got_b)
    bias_sum = bz[0]
    for k in range(1, NZ):
        bias_sum = bias_sum + bz[k]
    bs[0] = bias_sum
    got_b = link.send(bs.at[0], bs.at[1], link.at(dc=1))

    wait_all(got_z)
    total = gz32[z]
    for k in range(NZ - 1):
        total = total + rz[k].astype(F32)
    fin[0] = total[:, :36]
    fin[1] = total[:, 36:]
    got_w = link.send(fin.at[1 - c], ow, link.at(dc=1))
    got_b.wait_recv()
    bias_sum = bs[0] + bs[1]
    for t in range(2):
        for k in range(9):
            o_bias[t : t + 1, 128 * k : 128 * (k + 1)] = bias_sum[9 * t + k : 9 * t + k + 1, :]
    o_loss[0] = jnp.sum(bias_sum[18:19, :]) * (1.0 / 8192.0)
    o_scale[0] = jnp.sum(bias_sum[19:20, :])
    o_scale[1] = jnp.sum(bias_sum[20:21, :])
    got_w.wait_recv()

    @pl.when(c == 0)
    def _():
        o_wi[...] = fin[0]
        o_wt[...] = ow[...]

    @pl.when(c == 1)
    def _():
        o_wi[...] = ow[...]
        o_wt[...] = fin[1]

    for copy in link.started:
        copy.wait_send()


def per_device(f_img, f_txt, w_img, w_txt, b_img, b_txt, log_scale, logit_bias):
    vmem = pl.BlockSpec(memory_space=pltpu.VMEM)
    smem = pl.BlockSpec(memory_space=pltpu.SMEM)
    scratch = [
        ((2, NX, ROWS, KX), BF16),
        ((8, ROWS, KX), BF16),
        ((2, SHARD, E), BF16),
        ((ROWS, E), F32),
        ((6, ROWS, E), BF16),
        ((2, ROWS, E), F32),
        ((2, NX - 1, ROWS, E), BF16),
        ((2, ROWS, E), F32),
        ((2, ROWS, 128), F32),
        ((16, ROWS, E), BF16),
        ((16, ROWS, E), BF16),
        ((512, 512), BF16),
        ((NZ, ROWS, E), F32),
        ((NZ, ROWS, E), F32),
        ((NZ, ROWS, E), F32),
        ((2, NZ - 1, ROWS, E), BF16),
        ((ROWS, E), F32),
        ((16, ROWS, E), BF16),
        ((15, ROWS, E), BF16),
        ((2, ROWS, E), BF16),
        ((8, ROWS, E), BF16),
        ((24, 128), F32),
        ((3, 24, 128), F32),
        ((4, 24, 128), F32),
        ((8, 24, 128), F32),
        ((2, 24, 128), F32),
        ((8, ROWS, KX), BF16),
        ((2, NX, ROWS, KX), BF16),
        ((NY, SHARD, E // 2), F32),
        ((NY, SHARD, E // 2), BF16),
        ((NY - 1, SHARD, E // 2), BF16),
        ((NZ, SHARD, 72), F32),
        ((NZ, SHARD, 72), BF16),
        ((NZ - 1, SHARD, 72), BF16),
        ((2, SHARD, 36), F32),
        ((SHARD, 36), F32),
    ]
    return pl.pallas_call(
        kernel,
        out_shape=(
            jax.ShapeDtypeStruct((1,), F32),
            jax.ShapeDtypeStruct((2,), F32),
            jax.ShapeDtypeStruct((ROWS, D), BF16),
            jax.ShapeDtypeStruct((ROWS, D), BF16),
            jax.ShapeDtypeStruct((SHARD, 36), F32),
            jax.ShapeDtypeStruct((SHARD, 36), F32),
            jax.ShapeDtypeStruct((2, E), F32),
        ),
        in_specs=[vmem] * 6 + [smem] * 2,
        out_specs=(smem, smem, vmem, vmem, vmem, vmem, vmem),
        scratch_shapes=[pltpu.VMEM(shape, dtype) for shape, dtype in scratch]
        + [pltpu.SemaphoreType.DMA((N_COPIES,))] * 2,
        compiler_params=pltpu.CompilerParams(
            collective_id=0, has_side_effects=True, vmem_limit_bytes=56 * 2**20
        ),
    )(f_img, f_txt, w_img, w_txt, b_img.reshape(1, E), b_txt.reshape(1, E), log_scale, logit_bias)


def solution(mesh):
    rows = P(("dp", "mp"), None)
    return jax.shard_map(
        per_device,
        mesh=mesh,
        in_specs=(rows, rows, P("mp", None), P("mp", None), P(), P(), P(), P()),
        out_specs=(P(), P(), rows, rows, P("mp", "dp"), P("mp", "dp"), P()),
        check_vma=False,
    )
```

```python
import functools

import jax
import jax.numpy as jnp
from jax import lax
from jax.experimental import pallas as pl
from jax.experimental.pallas import tpu as pltpu
from jax.sharding import PartitionSpec as P

EPSILON = 1e-06
LOSS_FACTOR = 32.0
NX, NY, NZ = 4, 4, 8
ROWS = 32
D = 1152
E = 1152
SHARD = 144
KX = 2 * SHARD
MESH = pl.DeviceIdType.MESH
F32 = jnp.float32
BF16 = jnp.bfloat16

N_COPIES = 128


def ring(place, size):
    steps = [place + k for k in range(size)]
    return [place] + [jnp.where(v >= size, v - size, v) for v in steps[1:]]


class Links:
    def __init__(self, send_sems, recv_sems):
        dp, mp = lax.axis_index("dp"), lax.axis_index("mp")
        self.x, self.y = mp // 2, (mp % 2) * 2 + dp // 16
        self.z, self.c = (dp // 2) % NZ, dp % 2
        self.send_sems, self.recv_sems = send_sems, recv_sems
        self.started = []
        self.xs = ring(self.x, NX)
        self.ys = ring(self.y, NY)
        self.zs = ring(self.z, NZ)
        self.cs = ring(self.c, 2)
        self.x_mp = [2 * v for v in self.xs]
        self.y_mp = [v // 2 for v in self.ys]
        self.y_dp = [(v - 2 * h) * 16 for v, h in zip(self.ys, self.y_mp)]
        self.z_dp = [2 * v for v in self.zs]

    def at(self, dx=0, dy=0, dz=0, dc=0):
        return (self.y_dp[dy] + self.z_dp[dz] + self.cs[dc], self.x_mp[dx] + self.y_mp[dy])

    def send(self, src, dst, device):
        k = len(self.started)
        copy = pltpu.make_async_remote_copy(
            src_ref=src,
            dst_ref=dst,
            send_sem=self.send_sems.at[k],
            recv_sem=self.recv_sems.at[k],
            device_id=device,
            device_id_type=MESH,
        )
        copy.start()
        self.started.append(copy)
        return copy


def matmul(a, b):
    return lax.dot_general(a, b, (((1,), (0,)), ((), ())), preferred_element_type=F32)


def matmul_bt(a, b):
    return lax.dot_general(a, b, (((1,), (1,)), ((), ())), preferred_element_type=F32)


def matmul_at(a, b):
    return lax.dot_general(a, b, (((0,), (0,)), ((), ())), preferred_element_type=F32)


def wait_all(copies):
    for copy in copies:
        copy.wait_recv()


def kernel(
    f_img, f_txt, w_img, w_txt, b_img, b_txt, log_scale, logit_bias,
    rf, ow, o_sums,
    fs, fk, wk, po, pk, rp0, rp, unit, inv, ia, ta, wt, tg, tgx, tgs, rt, ig0, igs, ri,
    d16, dk, bp, bx, by, bz, bs, dfs, g32, gy, ry, gz32, gz, rz, fin,
    send_sems, recv_sems,
):
    link = Links(send_sems, recv_sems)
    x, y, z, c = link.x, link.y, link.z, link.c

    peers = [(0, 0, 0, 1)]
    peers += [(i, j, 0, 0) for i in range(NX) for j in range(NY) if (i, j) != (0, 0)]
    peers += [(i, 0, 0, 1) for i in range(1, NX)]
    peers += [(0, 0, k, 0) for k in range(1, NZ)]
    barrier = pltpu.get_barrier_semaphore()
    for p in peers:
        pl.semaphore_signal(barrier, inc=1, device_id=link.at(*p), device_id_type=MESH)

    shard = link.y_mp[0]

    @pl.when(c == 0)
    def _():
        wk[shard] = w_img[...]

    @pl.when(c == 1)
    def _():
        wk[shard] = w_txt[...]

    for k in range(NX):
        fs[0, k] = f_img[:, KX * k : KX * (k + 1)]
        fs[1, k] = f_txt[:, KX * k : KX * (k + 1)]
    pl.semaphore_wait(barrier, len(peers))

    odd = y - 2 * shard
    ahead, behind = link.at(dy=1), link.at(dy=3)
    partner = tuple(jnp.where(odd == 1, u, v) for u, v in zip(ahead, behind))
    got_w = link.send(wk.at[shard], wk.at[shard], partner)
    got_f = []
    for r in range(NX):
        for e in range(2):
            if (r, e) == (0, 0):
                fk[0] = fs[c, x]
                continue
            got_f.append(
                link.send(
                    fs.at[link.cs[e], link.xs[r]],
                    fk.at[((NX - r) % NX) * 2 + e],
                    link.at(dx=r, dc=e),
                )
            )
    wait_all(got_f)
    got_w.wait_recv()

    part = matmul(fk[...].reshape(8 * ROWS, KX), wk[...].reshape(KX, E))
    rp0[0] = part[:ROWS]
    po[...] = part[ROWS : 2 * ROWS]
    pk[...] = part[2 * ROWS :].astype(BF16).reshape(6, ROWS, E)
    got_p = [link.send(po, rp0.at[1], link.at(dc=1))]
    for r in range(1, NX):
        for e in range(2):
            got_p.append(
                link.send(pk.at[(r - 1) * 2 + e], rp.at[e, NX - r - 1], link.at(dx=r, dc=e))
            )
    wait_all(got_p)
    for t, bias in enumerate((b_img, b_txt)):
        e = link.cs[t]
        pre = rp0[e] + bias[...].reshape(1, E)
        for r in range(NX - 1):
            pre = pre + rp[e, r].astype(F32)
        inverse = lax.rsqrt(jnp.sum(pre * pre, axis=1, keepdims=True) + EPSILON)
        unit[t] = pre * inverse
        inv[t] = jnp.broadcast_to(inverse, (ROWS, 128))
    ia[0] = unit[0].astype(BF16)
    ta[0] = unit[1].astype(BF16)

    got_t = [link.send(ta.at[0], ta.at[NZ - k], link.at(dz=k)) for k in (1, 7, 2, 6, 3, 5, 4)]
    got_s = [link.send(ta.at[0], ta.at[NZ], link.at(dc=1))]
    got_i = []
    for i in range(NX):
        for j in range(NY):
            if (i, j) != (0, 0):
                slot = ((NX - i) % NX) * NY + (NY - j) % NY
                got_i.append(link.send(ia.at[0], ia.at[slot], link.at(dx=i, dy=j)))
    for copy, k in zip(got_t, (1, 7, 2, 6, 3, 5, 4)):
        copy.wait_recv()
        got_s.append(link.send(ta.at[NZ - k], ta.at[NZ + NZ - k], link.at(dc=1)))
    wait_all(got_i)

    half = NZ * ROWS
    scale = jnp.exp(log_scale[...].reshape(1, 1))
    shift = logit_bias[...].reshape(1, 1)
    images = ia[...].reshape(16 * ROWS, E)
    stats = []
    for h in range(2):
        if h == 1:
            wait_all(got_s)
        texts = ta[NZ * h : NZ * (h + 1)].reshape(half, E)
        scaled = scale * matmul_bt(texts, images)
        logits = scaled + shift
        signed = logits
        if h == 0:
            row = lax.broadcasted_iota(jnp.int32, logits.shape, 0)
            col = lax.broadcasted_iota(jnp.int32, logits.shape, 1)
            match = jnp.logical_and(row == col, col < ROWS)
            signed = jnp.where(match, -logits, logits)
        small = jnp.exp(-jnp.abs(logits))
        loss = jnp.maximum(signed, 0.0) + jnp.log1p(small)
        errors = jnp.where(logits >= 0.0, 1.0, small) / (1.0 + small)
        if h == 0:
            errors = errors - match.astype(F32)
        weights = (LOSS_FACTOR * errors).astype(BF16)
        sums = (loss, LOSS_FACTOR * errors * scaled, LOSS_FACTOR * errors)
        stats.append([jnp.sum(v, axis=0, keepdims=True) for v in sums])
        wt[:, half * h : half * (h + 1)] = weights.T
        grad = matmul(weights, images)
        if h == 0:
            tg[...] = grad.reshape(NZ, ROWS, E)
        else:
            tgx[...] = grad.reshape(NZ, ROWS, E)
    got_x = link.send(tgx, tgs, link.at(dc=1))

    texts = ta[...].reshape(16 * ROWS, E)
    got_ig = []
    for q in range(4):
        grad = matmul(wt[128 * q : 128 * (q + 1), :], texts).reshape(4, ROWS, E)
        if q == 0:
            ig0[...] = grad[0]
        igs[4 * q : 4 * (q + 1)] = grad.astype(BF16)
        for slot in range(4 * q, 4 * q + 4):
            if slot:
                got_ig.append(
                    link.send(igs.at[slot], ri.at[slot - 1], link.at(dx=slot // 4, dy=slot % 4))
                )
        if q == 0:
            got_x.wait_recv()
            tg[...] = tg[...] + tgs[...]
            tgx16 = tg[1:].astype(BF16)
            rt[1, ...] = tgx16
            got_tg = [
                link.send(rt.at[1, k - 1], rt.at[0, k - 1], link.at(dz=k))
                for k in (4, 3, 5, 2, 6, 1, 7)
            ]

    wait_all(got_tg)
    grad_txt = tg[0]
    for k in range(NZ - 1):
        grad_txt = grad_txt + rt[0, k].astype(F32)
    wait_all(got_ig)
    grad_img = ig0[...]
    for k in range(NX * NY - 1):
        grad_img = grad_img + ri[k].astype(F32)
    for t, grad in enumerate((grad_img, grad_txt)):
        grad = scale * grad
        delta = inv[t, :, 0:1] * (grad - unit[t] * jnp.sum(unit[t] * grad, axis=1, keepdims=True))
        d16[t] = delta.astype(BF16)
        total = jnp.sum(delta, axis=0, keepdims=True)
        for k in range(9):
            bp[9 * t + k : 9 * t + k + 1, :] = total[:, 128 * k : 128 * (k + 1)]
    for k in range(3):
        lanes = stats[0][k] + stats[1][k]
        bp[18 + k : 19 + k, :] = (
            lanes[:, 0:128] + lanes[:, 128:256] + lanes[:, 256:384] + lanes[:, 384:512]
        )
    bp[21:24, :] = jnp.zeros((3, 128), F32)

    got_d = []
    for r in range(NX):
        for e in range(2):
            if (r, e) == (0, 0):
                dk[0] = d16[c]
                continue
            got_d.append(
                link.send(
                    d16.at[link.cs[e]], dk.at[((NX - r) % NX) * 2 + e], link.at(dx=r, dc=e)
                )
            )
    got_b = [link.send(bp, bx.at[r - 1], link.at(dx=r)) for r in range(1, NX)]
    wait_all(got_d)

    deltas = dk[...].reshape(8 * ROWS, E)
    grad_w = matmul_at(fk[...].reshape(8 * ROWS, KX), deltas)
    for j in range(NY):
        part = grad_w[SHARD * (j // 2) : SHARD * (j // 2 + 1), (E // 2) * (j % 2) : (E // 2) * (j % 2 + 1)]
        g32[j] = part
        gy[j] = part.astype(BF16)
    got_y = [link.send(gy.at[link.ys[j]], ry.at[j - 1], link.at(dy=j)) for j in (2, 1, 3)]
    wait_all(got_b)
    by[0] = bp[...] + bx[0] + bx[1] + bx[2]
    got_b = [link.send(by.at[0], by.at[j], link.at(dy=j)) for j in range(1, NY)]

    grad_f = matmul_bt(deltas, wk[...].reshape(KX, E)).astype(BF16)
    dfs[...] = grad_f.reshape(8, ROWS, KX)
    got_df = []
    for r in range(NX):
        for e in range(2):
            if (r, e) == (0, 0):
                rf[0, x] = dfs[0]
                continue
            got_df.append(link.send(dfs.at[r * 2 + e], rf.at[e, x], link.at(dx=r, dc=e)))

    wait_all(got_y)
    total = g32[y]
    for j in range(NY - 1):
        total = total + ry[j].astype(F32)
    for k in range(NZ):
        part = total[:, 72 * k : 72 * (k + 1)]
        gz32[k] = part
        gz[k] = part.astype(BF16)
    got_z = [link.send(gz.at[link.zs[k]], rz.at[k - 1], link.at(dz=k)) for k in (4, 3, 5, 2, 6, 1, 7)]
    wait_all(got_b)
    bz[0] = by[0] + by[1] + by[2] + by[3]
    got_b = [link.send(bz.at[0], bz.at[k], link.at(dz=k)) for k in range(1, NZ)]

    wait_all(got_b)
    bias_sum = bz[0]
    for k in range(1, NZ):
        bias_sum = bias_sum + bz[k]
    bs[0] = bias_sum
    got_b = link.send(bs.at[0], bs.at[1], link.at(dc=1))

    wait_all(got_z)
    total = gz32[z]
    for k in range(NZ - 1):
        total = total + rz[k].astype(F32)
    fin[0] = total[:, :36]
    fin[1] = total[:, 36:]
    got_w = link.send(fin.at[1 - c], ow.at[1], link.at(dc=1))
    got_b.wait_recv()
    o_sums[...] = bs[0] + bs[1]
    got_w.wait_recv()
    ow[0] = fin[c]
    wait_all(got_df)

    for copy in link.started:
        copy.wait_send()


def finish(rf, ow, sums, o_loss, o_scale, o_fi, o_ft, o_wi, o_wt, o_bias):
    c = lax.axis_index("dp") % 2
    for t, (out_f, out_w) in enumerate(((o_fi, o_wi), (o_ft, o_wt))):
        e = jnp.where(c == t, 0, 1)
        for k in range(NX):
            out_f[:, KX * k : KX * (k + 1)] = rf[e, k]
        out_w[...] = ow[e].T
        for k in range(9):
            o_bias[t : t + 1, 128 * k : 128 * (k + 1)] = sums[9 * t + k : 9 * t + k + 1, :]
    o_loss[0] = jnp.sum(sums[18:19, :]) * (1.0 / 8192.0)
    o_scale[0] = jnp.sum(sums[19:20, :])
    o_scale[1] = jnp.sum(sums[20:21, :])


def per_device(f_img, f_txt, w_img, w_txt, b_img, b_txt, log_scale, logit_bias):
    vmem = pl.BlockSpec(memory_space=pltpu.VMEM)
    smem = pl.BlockSpec(memory_space=pltpu.SMEM)
    scratch = [
        ((2, NX, ROWS, KX), BF16),
        ((8, ROWS, KX), BF16),
        ((2, SHARD, E), BF16),
        ((ROWS, E), F32),
        ((6, ROWS, E), BF16),
        ((2, ROWS, E), F32),
        ((2, NX - 1, ROWS, E), BF16),
        ((2, ROWS, E), F32),
        ((2, ROWS, 128), F32),
        ((16, ROWS, E), BF16),
        ((16, ROWS, E), BF16),
        ((512, 512), BF16),
        ((NZ, ROWS, E), F32),
        ((NZ, ROWS, E), F32),
        ((NZ, ROWS, E), F32),
        ((2, NZ - 1, ROWS, E), BF16),
        ((ROWS, E), F32),
        ((16, ROWS, E), BF16),
        ((15, ROWS, E), BF16),
        ((2, ROWS, E), BF16),
        ((8, ROWS, E), BF16),
        ((24, 128), F32),
        ((3, 24, 128), F32),
        ((4, 24, 128), F32),
        ((8, 24, 128), F32),
        ((2, 24, 128), F32),
        ((8, ROWS, KX), BF16),
        ((NY, SHARD, E // 2), F32),
        ((NY, SHARD, E // 2), BF16),
        ((NY - 1, SHARD, E // 2), BF16),
        ((NZ, SHARD, 72), F32),
        ((NZ, SHARD, 72), BF16),
        ((NZ - 1, SHARD, 72), BF16),
        ((2, SHARD, 36), F32),
    ]
    parts = pl.pallas_call(
        kernel,
        out_shape=(
            jax.ShapeDtypeStruct((2, NX, ROWS, KX), BF16),
            jax.ShapeDtypeStruct((2, SHARD, 36), F32),
            jax.ShapeDtypeStruct((24, 128), F32),
        ),
        in_specs=[vmem] * 8,
        out_specs=(vmem, vmem, vmem),
        scratch_shapes=[pltpu.VMEM(shape, dtype) for shape, dtype in scratch]
        + [pltpu.SemaphoreType.DMA((N_COPIES,))] * 2,
        compiler_params=pltpu.CompilerParams(
            collective_id=0, has_side_effects=True, vmem_limit_bytes=56 * 2**20
        ),
    )(f_img, f_txt, w_img, w_txt, b_img, b_txt, log_scale, logit_bias)
    loss, scale, fi, ft, wi, wt, bias = pl.pallas_call(
        finish,
        out_shape=(
            jax.ShapeDtypeStruct((1,), F32),
            jax.ShapeDtypeStruct((2,), F32),
            jax.ShapeDtypeStruct((ROWS, D), BF16),
            jax.ShapeDtypeStruct((ROWS, D), BF16),
            jax.ShapeDtypeStruct((36, SHARD), F32),
            jax.ShapeDtypeStruct((36, SHARD), F32),
            jax.ShapeDtypeStruct((2, E), F32),
        ),
        in_specs=[vmem] * 3,
        out_specs=(smem, smem, vmem, vmem, vmem, vmem, vmem),
    )(*parts)
    return loss, scale, fi, ft, wi.T, wt.T, bias


def solution(mesh):
    rows = P(("dp", "mp"), None)
    return jax.shard_map(
        per_device,
        mesh=mesh,
        in_specs=(rows, rows, P("mp", None), P("mp", None), P(), P(), P(), P()),
        out_specs=(P(), P(), rows, rows, P("mp", "dp"), P("mp", "dp"), P()),
        check_vma=False,
    )
```

```python
import functools

import jax
import jax.numpy as jnp
from jax import lax
from jax.experimental import pallas as pl
from jax.experimental.pallas import tpu as pltpu
from jax.sharding import PartitionSpec as P

EPSILON = 1e-06
LOSS_FACTOR = 32.0
NX, NY, NZ = 4, 4, 8
ROWS = 32
HALF = ROWS // 2
D = 1152
E = 1152
SHARD = 144
KX = 2 * SHARD
MESH = pl.DeviceIdType.MESH
F32 = jnp.float32
BF16 = jnp.bfloat16

N_COPIES = 128


def ring(place, size):
    steps = [place + k for k in range(size)]
    return [place] + [jnp.where(v >= size, v - size, v) for v in steps[1:]]


class Links:
    def __init__(self, send_sems, recv_sems):
        dp, mp = lax.axis_index("dp"), lax.axis_index("mp")
        self.x, self.y = mp // 2, (mp % 2) * 2 + dp // 16
        self.z, self.c = (dp // 2) % NZ, dp % 2
        self.send_sems, self.recv_sems = send_sems, recv_sems
        self.started = []
        self.xs = ring(self.x, NX)
        self.ys = ring(self.y, NY)
        self.zs = ring(self.z, NZ)
        self.cs = ring(self.c, 2)
        self.x_mp = [2 * v for v in self.xs]
        self.y_mp = [v // 2 for v in self.ys]
        self.y_dp = [(v - 2 * h) * 16 for v, h in zip(self.ys, self.y_mp)]
        self.z_dp = [2 * v for v in self.zs]

    def at(self, dx=0, dy=0, dz=0, dc=0):
        return (self.y_dp[dy] + self.z_dp[dz] + self.cs[dc], self.x_mp[dx] + self.y_mp[dy])

    def send(self, src, dst, device):
        k = len(self.started)
        copy = pltpu.make_async_remote_copy(
            src_ref=src,
            dst_ref=dst,
            send_sem=self.send_sems.at[k],
            recv_sem=self.recv_sems.at[k],
            device_id=device,
            device_id_type=MESH,
        )
        copy.start()
        self.started.append(copy)
        return copy


def matmul(a, b):
    return lax.dot_general(a, b, (((1,), (0,)), ((), ())), preferred_element_type=F32)


def matmul_bt(a, b):
    return lax.dot_general(a, b, (((1,), (1,)), ((), ())), preferred_element_type=F32)


def matmul_at(a, b):
    return lax.dot_general(a, b, (((0,), (0,)), ((), ())), preferred_element_type=F32)


def wait_all(copies):
    for copy in copies:
        copy.wait_recv()


def gather_z(link, buf, split, on_arrival):
    to_7 = link.send(buf.at[0], buf.at[7], link.at(dz=1))
    to_1 = link.send(buf.at[0], buf.at[1], link.at(dz=7))
    to_6 = link.send(buf.at[0], buf.at[6], link.at(dz=2))
    to_2 = link.send(buf.at[0], buf.at[2], link.at(dz=6))
    yield
    to_7.wait_recv()
    to_5 = link.send(buf.at[7], buf.at[5], link.at(dz=2))
    on_arrival(7)
    yield
    to_1.wait_recv()
    to_3 = link.send(buf.at[1], buf.at[3], link.at(dz=6))
    on_arrival(1)
    yield
    to_6.wait_recv()
    if split is None:
        to_4 = [link.send(buf.at[6], buf.at[4], link.at(dz=2))]
    else:
        to_4 = [link.send(buf.at[6, :split], buf.at[4, :split], link.at(dz=2))]
    on_arrival(6)
    yield
    to_2.wait_recv()
    if split is not None:
        to_4.append(link.send(buf.at[2, split:], buf.at[4, split:], link.at(dz=6)))
    on_arrival(2)
    yield
    to_5.wait_recv()
    on_arrival(5)
    to_3.wait_recv()
    on_arrival(3)
    wait_all(to_4)
    on_arrival(4)


def gather_plane(link, buf):
    steps = (1, 3, 2)
    top, low = pl.ds(0, HALF), pl.ds(HALF, HALF)
    got = []
    got_x = [link.send(buf.at[0, 0], buf.at[NX - i, 0], link.at(dx=i)) for i in steps]
    got_y = [link.send(buf.at[0, 0], buf.at[0, NY - j], link.at(dy=j)) for j in steps]
    yield
    for copy_x, copy_y, k in zip(got_x, got_y, steps):
        a = NX - k
        copy_x.wait_recv()
        for j in steps:
            got.append(link.send(buf.at[a, 0, top], buf.at[a, NY - j, top], link.at(dy=j)))
        copy_y.wait_recv()
        for i in steps:
            got.append(link.send(buf.at[0, a, low], buf.at[NX - i, a, low], link.at(dx=i)))
        yield
    wait_all(got)


def interleave(*parts):
    parts = list(parts)
    while parts:
        for part in list(parts):
            try:
                next(part)
            except StopIteration:
                parts.remove(part)


def reduce_z_start(link, part, sent, got, split):
    for i, k in enumerate((3, 5, 4)):
        sent[i] = part(k).astype(BF16)
    return [
        link.send(sent.at[0], got.at[0], link.at(dz=2)),
        link.send(sent.at[1], got.at[1], link.at(dz=6)),
        link.send(sent.at[2, :split], got.at[2, :split], link.at(dz=2)),
        link.send(sent.at[2, split:], got.at[2, split:], link.at(dz=6)),
    ]


def reduce_z_finish(link, part, sent, got, split, first):
    first[0].wait_recv()
    sent[3] = (part(1) + got[0].astype(F32)).astype(BF16)
    last = [link.send(sent.at[3], got.at[3], link.at(dz=1))]
    first[1].wait_recv()
    sent[4] = (part(7) + got[1].astype(F32)).astype(BF16)
    last.append(link.send(sent.at[4], got.at[4], link.at(dz=7)))
    first[2].wait_recv()
    term = part(2)
    sent[5, :split] = (term[:split] + got[2, :split].astype(F32)).astype(BF16)
    sent[5, split:] = term[split:].astype(BF16)
    last.append(link.send(sent.at[5], got.at[5], link.at(dz=2)))
    first[3].wait_recv()
    term = part(6)
    sent[6, :split] = term[:split].astype(BF16)
    sent[6, split:] = (term[split:] + got[2, split:].astype(F32)).astype(BF16)
    last.append(link.send(sent.at[6], got.at[6], link.at(dz=6)))
    return last


def reduce_z_sum(part, got, last):
    total = part(0)
    for k, copy in enumerate(last):
        copy.wait_recv()
        total = total + got[3 + k].astype(F32)
    return total


def kernel(
    f_img, f_txt, w_img, w_txt, b_img, b_txt, log_scale, logit_bias,
    rf, ow, o_sums,
    fs, fk, wk, po, pk, rp0, rp, unit, inv, ia, ta, wt, tg, tgx, tgs, tz_sent, tz_got,
    ig0, ig_x32, ig_y32, ig_top, ig_low, r_top, r_low, ig2_top, ig2_low, r2_top, r2_low,
    d16, dk, bp, bx, by, bz, bs, dfs, g32, gy, ry, gz32, gz_sent, gz_got, fin,
    send_sems, recv_sems,
):
    link = Links(send_sems, recv_sems)
    x, y, z, c = link.x, link.y, link.z, link.c

    peers = [(0, 0, 0, 1)]
    peers += [(i, 0, 0, e) for i in range(1, NX) for e in range(2)]
    peers += [(0, j, 0, 0) for j in range(1, NY)]
    peers += [(0, 0, k, 0) for k in (1, 2, 6, 7)]
    barrier = pltpu.get_barrier_semaphore()
    for p in peers:
        pl.semaphore_signal(barrier, inc=1, device_id=link.at(*p), device_id_type=MESH)

    shard = link.y_mp[0]

    @pl.when(c == 0)
    def _():
        wk[shard] = w_img[...]

    @pl.when(c == 1)
    def _():
        wk[shard] = w_txt[...]

    for k in range(NX):
        fs[0, k] = f_img[:, KX * k : KX * (k + 1)]
        fs[1, k] = f_txt[:, KX * k : KX * (k + 1)]
    pl.semaphore_wait(barrier, len(peers))

    odd = y - 2 * shard
    ahead, behind = link.at(dy=1), link.at(dy=3)
    partner = tuple(jnp.where(odd == 1, u, v) for u, v in zip(ahead, behind))
    got_w = link.send(wk.at[shard], wk.at[shard], partner)
    got_f = []
    for r in range(NX):
        for e in range(2):
            if (r, e) == (0, 0):
                fk[0] = fs[c, x]
                continue
            got_f.append(
                link.send(
                    fs.at[link.cs[e], link.xs[r]],
                    fk.at[((NX - r) % NX) * 2 + e],
                    link.at(dx=r, dc=e),
                )
            )
    wait_all(got_f)
    got_w.wait_recv()

    part = matmul(fk[...].reshape(8 * ROWS, KX), wk[...].reshape(KX, E))
    rp0[0] = part[:ROWS]
    po[...] = part[ROWS : 2 * ROWS]
    pk[...] = part[2 * ROWS :].astype(BF16).reshape(6, ROWS, E)
    got_p = [link.send(po, rp0.at[1], link.at(dc=1))]
    for r in range(1, NX):
        for e in range(2):
            got_p.append(
                link.send(pk.at[(r - 1) * 2 + e], rp.at[e, NX - r - 1], link.at(dx=r, dc=e))
            )
    wait_all(got_p)
    for t, bias in enumerate((b_img, b_txt)):
        e = link.cs[t]
        pre = rp0[e] + bias[...].reshape(1, E)
        for r in range(NX - 1):
            pre = pre + rp[e, r].astype(F32)
        inverse = lax.rsqrt(jnp.sum(pre * pre, axis=1, keepdims=True) + EPSILON)
        unit[t] = pre * inverse
        inv[t] = jnp.broadcast_to(inverse, (ROWS, 128))
    ia[0, 0] = unit[0].astype(BF16)
    ta[0, 0] = unit[1].astype(BF16)

    got_s = [link.send(ta.at[0, 0], ta.at[1, 0], link.at(dc=1))]

    def forward(k):
        got_s.append(link.send(ta.at[0, k], ta.at[1, k], link.at(dc=1)))

    interleave(gather_z(link, ta.at[0], HALF, forward), gather_plane(link, ia))

    half = NZ * ROWS
    scale = jnp.exp(log_scale[...].reshape(1, 1))
    shift = logit_bias[...].reshape(1, 1)
    images = ia[...].reshape(16 * ROWS, E)
    stats = []
    for h in range(2):
        if h == 1:
            wait_all(got_s)
        texts = ta[h].reshape(half, E)
        scaled = scale * matmul_bt(texts, images)
        logits = scaled + shift
        signed = logits
        if h == 0:
            row = lax.broadcasted_iota(jnp.int32, logits.shape, 0)
            col = lax.broadcasted_iota(jnp.int32, logits.shape, 1)
            match = jnp.logical_and(row == col, col < ROWS)
            signed = jnp.where(match, -logits, logits)
        small = jnp.exp(-jnp.abs(logits))
        loss = jnp.maximum(signed, 0.0) + jnp.log1p(small)
        errors = jnp.where(logits >= 0.0, 1.0, small) / (1.0 + small)
        if h == 0:
            errors = errors - match.astype(F32)
        weights = (LOSS_FACTOR * errors).astype(BF16)
        sums = (loss, LOSS_FACTOR * errors * scaled, LOSS_FACTOR * errors)
        stats.append([jnp.sum(v, axis=0, keepdims=True) for v in sums])
        wt[:, half * h : half * (h + 1)] = weights.T
        grad = matmul(weights, images)
        if h == 0:
            tg[...] = grad.reshape(NZ, ROWS, E)
        else:
            tgx[...] = grad.reshape(NZ, ROWS, E)
    got_x = [
        link.send(tgx.at[k], tgs.at[k], link.at(dc=1))
        for k in (pl.ds(3, 3), pl.ds(0, 3), pl.ds(6, 2))
    ]

    def txt_part(k):
        return tg[k] + tgs[k]

    top, low = pl.ds(0, HALF), pl.ds(HALF, HALF)
    texts = ta[...].reshape(16 * ROWS, E)
    got_low, got_top = [], []
    for i, a in enumerate((2, 1, 3, 0)):
        grad = matmul(wt[128 * a : 128 * (a + 1), :], texts).reshape(NY, ROWS, E)
        ig_top[:, a] = grad[:, :HALF].astype(BF16)
        ig_low[a] = grad[:, HALF:].astype(BF16)
        if a:
            ig_x32[a - 1] = grad[0, :HALF]
            got_low.append(link.send(ig_low.at[a], r_low.at[a - 1], link.at(dx=a)))
        else:
            ig0[...] = grad[0]
            ig_y32[...] = grad[1:, HALF:]
        if i == 0:
            got_x[0].wait_recv()
            first = reduce_z_start(link, txt_part, tz_sent, tz_got, HALF)
    for j in (2, 1, 3):
        got_top.append(link.send(ig_top.at[j], r_top.at[j - 1], link.at(dy=j)))
    wait_all(got_x[1:])
    got_tg = reduce_z_finish(link, txt_part, tz_sent, tz_got, HALF, first)

    wait_all(got_low)
    got_low2 = []
    for j in (2, 1, 3):
        total = ig_y32[j - 1]
        for i in range(NX - 1):
            total = total + r_low[i, j].astype(F32)
        ig2_low[j - 1] = total.astype(BF16)
        got_low2.append(link.send(ig2_low.at[j - 1], r2_low.at[j - 1], link.at(dy=j)))
    wait_all(got_top)
    got_top2 = []
    for i in (2, 1, 3):
        total = ig_x32[i - 1]
        for j in range(NY - 1):
            total = total + r_top[j, i].astype(F32)
        ig2_top[i - 1] = total.astype(BF16)
        got_top2.append(link.send(ig2_top.at[i - 1], r2_top.at[i - 1], link.at(dx=i)))

    grad_txt = reduce_z_sum(txt_part, tz_got, got_tg)
    wait_all(got_low2 + got_top2)
    halves = []
    for rows, first_got, second_got in ((top, r_top, r2_top), (low, r_low, r2_low)):
        total = ig0[rows, :]
        for k in range(3):
            total = total + first_got[k, 0].astype(F32) + second_got[k].astype(F32)
        halves.append(total)
    grad_img = jnp.concatenate(halves, axis=0)
    for t, grad in enumerate((grad_img, grad_txt)):
        grad = scale * grad
        delta = inv[t, :, 0:1] * (grad - unit[t] * jnp.sum(unit[t] * grad, axis=1, keepdims=True))
        d16[t] = delta.astype(BF16)
        total = jnp.sum(delta, axis=0, keepdims=True)
        for k in range(9):
            bp[9 * t + k : 9 * t + k + 1, :] = total[:, 128 * k : 128 * (k + 1)]
    for k in range(3):
        lanes = stats[0][k] + stats[1][k]
        bp[18 + k : 19 + k, :] = (
            lanes[:, 0:128] + lanes[:, 128:256] + lanes[:, 256:384] + lanes[:, 384:512]
        )
    bp[21:24, :] = jnp.zeros((3, 128), F32)

    got_d = []
    for r in range(NX):
        for e in range(2):
            if (r, e) == (0, 0):
                dk[0] = d16[c]
                continue
            got_d.append(
                link.send(
                    d16.at[link.cs[e]], dk.at[((NX - r) % NX) * 2 + e], link.at(dx=r, dc=e)
                )
            )
    got_b = [link.send(bp, bx.at[r - 1], link.at(dx=r)) for r in range(1, NX)]
    wait_all(got_d)

    deltas = dk[...].reshape(8 * ROWS, E)
    grad_w = matmul_at(fk[...].reshape(8 * ROWS, KX), deltas)
    for j in range(NY):
        part = grad_w[SHARD * (j // 2) : SHARD * (j // 2 + 1), (E // 2) * (j % 2) : (E // 2) * (j % 2 + 1)]
        g32[j] = part
        gy[j] = part.astype(BF16)
    got_y = [link.send(gy.at[link.ys[j]], ry.at[j - 1], link.at(dy=j)) for j in (2, 1, 3)]
    wait_all(got_b)
    by[0] = bp[...] + bx[0] + bx[1] + bx[2]
    got_b = [link.send(by.at[0], by.at[j], link.at(dy=j)) for j in range(1, NY)]

    grad_f = matmul_bt(deltas, wk[...].reshape(KX, E)).astype(BF16)
    dfs[...] = grad_f.reshape(8, ROWS, KX)
    got_df = []
    for r in range(NX):
        for e in range(2):
            if (r, e) == (0, 0):
                rf[0, x] = dfs[0]
                continue
            got_df.append(link.send(dfs.at[r * 2 + e], rf.at[e, x], link.at(dx=r, dc=e)))

    wait_all(got_y)
    total = g32[y]
    for j in range(NY - 1):
        total = total + ry[j].astype(F32)
    for k in range(NZ):
        gz32[k] = total[:, 72 * k : 72 * (k + 1)]

    def head_part(k):
        return gz32[link.zs[k]]

    first = reduce_z_start(link, head_part, gz_sent, gz_got, 80)
    wait_all(got_b)
    bz[0] = by[0] + by[1] + by[2] + by[3]
    interleave(gather_z(link, bz, None, lambda k: None))
    got_z = reduce_z_finish(link, head_part, gz_sent, gz_got, 80, first)
    bias_sum = bz[0]
    for k in range(1, NZ):
        bias_sum = bias_sum + bz[k]
    bs[0] = bias_sum
    got_b = link.send(bs.at[0], bs.at[1], link.at(dc=1))

    total = reduce_z_sum(head_part, gz_got, got_z)
    fin[0] = total[:, :36]
    fin[1] = total[:, 36:]
    got_w = link.send(fin.at[1 - c], ow.at[1], link.at(dc=1))
    got_b.wait_recv()
    o_sums[...] = bs[0] + bs[1]
    got_w.wait_recv()
    ow[0] = fin[c]
    wait_all(got_df)

    for copy in link.started:
        copy.wait_send()


def finish(rf, ow, sums, o_loss, o_scale, o_fi, o_ft, o_wi, o_wt, o_bias):
    c = lax.axis_index("dp") % 2
    for t, (out_f, out_w) in enumerate(((o_fi, o_wi), (o_ft, o_wt))):
        e = jnp.where(c == t, 0, 1)
        for k in range(NX):
            out_f[:, KX * k : KX * (k + 1)] = rf[e, k]
        out_w[...] = ow[e].T
        for k in range(9):
            o_bias[t : t + 1, 128 * k : 128 * (k + 1)] = sums[9 * t + k : 9 * t + k + 1, :]
    o_loss[0] = jnp.sum(sums[18:19, :]) * (1.0 / 8192.0)
    o_scale[0] = jnp.sum(sums[19:20, :])
    o_scale[1] = jnp.sum(sums[20:21, :])


def per_device(f_img, f_txt, w_img, w_txt, b_img, b_txt, log_scale, logit_bias):
    vmem = pl.BlockSpec(memory_space=pltpu.VMEM)
    smem = pl.BlockSpec(memory_space=pltpu.SMEM)
    scratch = [
        ((2, NX, ROWS, KX), BF16),
        ((8, ROWS, KX), BF16),
        ((2, SHARD, E), BF16),
        ((ROWS, E), F32),
        ((6, ROWS, E), BF16),
        ((2, ROWS, E), F32),
        ((2, NX - 1, ROWS, E), BF16),
        ((2, ROWS, E), F32),
        ((2, ROWS, 128), F32),
        ((NX, NY, ROWS, E), BF16),
        ((2, NZ, ROWS, E), BF16),
        ((512, 512), BF16),
        ((NZ, ROWS, E), F32),
        ((NZ, ROWS, E), F32),
        ((NZ, ROWS, E), F32),
        ((7, ROWS, E), BF16),
        ((7, ROWS, E), BF16),
        ((ROWS, E), F32),
        ((NX - 1, HALF, E), F32),
        ((NY - 1, HALF, E), F32),
        ((NY, NX, HALF, E), BF16),
        ((NX, NY, HALF, E), BF16),
        ((NY - 1, NX, HALF, E), BF16),
        ((NX - 1, NY, HALF, E), BF16),
        ((NX - 1, HALF, E), BF16),
        ((NY - 1, HALF, E), BF16),
        ((NX - 1, HALF, E), BF16),
        ((NY - 1, HALF, E), BF16),
        ((2, ROWS, E), BF16),
        ((8, ROWS, E), BF16),
        ((24, 128), F32),
        ((3, 24, 128), F32),
        ((4, 24, 128), F32),
        ((8, 24, 128), F32),
        ((2, 24, 128), F32),
        ((8, ROWS, KX), BF16),
        ((NY, SHARD, E // 2), F32),
        ((NY, SHARD, E // 2), BF16),
        ((NY - 1, SHARD, E // 2), BF16),
        ((NZ, SHARD, 72), F32),
        ((7, SHARD, 72), BF16),
        ((7, SHARD, 72), BF16),
        ((2, SHARD, 36), F32),
    ]
    parts = pl.pallas_call(
        kernel,
        out_shape=(
            jax.ShapeDtypeStruct((2, NX, ROWS, KX), BF16),
            jax.ShapeDtypeStruct((2, SHARD, 36), F32),
            jax.ShapeDtypeStruct((24, 128), F32),
        ),
        in_specs=[vmem] * 8,
        out_specs=(vmem, vmem, vmem),
        scratch_shapes=[pltpu.VMEM(shape, dtype) for shape, dtype in scratch]
        + [pltpu.SemaphoreType.DMA((N_COPIES,))] * 2,
        compiler_params=pltpu.CompilerParams(
            collective_id=0, has_side_effects=True, vmem_limit_bytes=56 * 2**20
        ),
    )(f_img, f_txt, w_img, w_txt, b_img, b_txt, log_scale, logit_bias)
    loss, scale, fi, ft, wi, wt, bias = pl.pallas_call(
        finish,
        out_shape=(
            jax.ShapeDtypeStruct((1,), F32),
            jax.ShapeDtypeStruct((2,), F32),
            jax.ShapeDtypeStruct((ROWS, D), BF16),
            jax.ShapeDtypeStruct((ROWS, D), BF16),
            jax.ShapeDtypeStruct((36, SHARD), F32),
            jax.ShapeDtypeStruct((36, SHARD), F32),
            jax.ShapeDtypeStruct((2, E), F32),
        ),
        in_specs=[vmem] * 3,
        out_specs=(smem, smem, vmem, vmem, vmem, vmem, vmem),
    )(*parts)
    return loss, scale, fi, ft, wi.T, wt.T, bias


def solution(mesh):
    rows = P(("dp", "mp"), None)
    return jax.shard_map(
        per_device,
        mesh=mesh,
        in_specs=(rows, rows, P("mp", None), P("mp", None), P(), P(), P(), P()),
        out_specs=(P(), P(), rows, rows, P("mp", "dp"), P("mp", "dp"), P()),
        check_vma=False,
    )
```

```python
import functools

import jax
import jax.numpy as jnp
from jax import lax
from jax.experimental import pallas as pl
from jax.experimental.pallas import tpu as pltpu
from jax.sharding import PartitionSpec as P

EPSILON = 1e-06
LOSS_FACTOR = 32.0
NX, NY, NZ = 4, 4, 8
ROWS = 32
HALF = ROWS // 2
D = 1152
E = 1152
SHARD = 144
KX = 2 * SHARD
CHUNKS = 3
COLS = E // CHUNKS
CUT = SHARD // 3
MESH = pl.DeviceIdType.MESH
F32 = jnp.float32
BF16 = jnp.bfloat16

N_GROUPS = 64


def ring(place, size):
    steps = [place + k for k in range(size)]
    return [place] + [jnp.where(v >= size, v - size, v) for v in steps[1:]]


class Links:
    def __init__(self, send_sems, recv_sems):
        dp, mp = lax.axis_index("dp"), lax.axis_index("mp")
        self.x, self.y = mp // 2, (mp % 2) * 2 + dp // 16
        self.z, self.c = (dp // 2) % NZ, dp % 2
        self.send_sems, self.recv_sems = send_sems, recv_sems
        self.started = []
        self.xs = ring(self.x, NX)
        self.ys = ring(self.y, NY)
        self.zs = ring(self.z, NZ)
        self.cs = ring(self.c, 2)
        self.x_mp = [2 * v for v in self.xs]
        self.y_mp = [v // 2 for v in self.ys]
        self.y_dp = [(v - 2 * h) * 16 for v, h in zip(self.ys, self.y_mp)]
        self.z_dp = [2 * v for v in self.zs]

    def at(self, dx=0, dy=0, dz=0, dc=0):
        return (self.y_dp[dy] + self.z_dp[dz] + self.cs[dc], self.x_mp[dx] + self.y_mp[dy])

    def group(self, region):
        copies = Group(self, len(self.started), region)
        self.started.append(copies)
        return copies

    def send(self, src, dst, device):
        copies = self.group(dst)
        copies.send(src, dst, device)
        return copies


class Group:
    def __init__(self, link, k, region):
        self.link, self.region = link, region
        self.sems = (link.send_sems.at[k], link.recv_sems.at[k])

    def copy(self, src, dst, device):
        return pltpu.make_async_remote_copy(
            src_ref=src,
            dst_ref=dst,
            send_sem=self.sems[0],
            recv_sem=self.sems[1],
            device_id=device,
            device_id_type=MESH,
        )

    def send(self, src, dst, device):
        self.copy(src, dst, device).start()

    def wait_recv(self):
        self.copy(self.region, self.region, self.link.at(dc=1)).wait_recv()

    def wait_send(self):
        self.copy(self.region, self.region, self.link.at(dc=1)).wait_send()


def matmul(a, b):
    return lax.dot_general(a, b, (((1,), (0,)), ((), ())), preferred_element_type=F32)


def matmul_bt(a, b):
    return lax.dot_general(a, b, (((1,), (1,)), ((), ())), preferred_element_type=F32)


def matmul_at(a, b):
    return lax.dot_general(a, b, (((0,), (0,)), ((), ())), preferred_element_type=F32)


def wait_all(copies):
    for copy in copies:
        copy.wait_recv()


def gather_z(link, buf, split, on_arrival):
    to_7 = link.send(buf.at[0], buf.at[7], link.at(dz=1))
    to_1 = link.send(buf.at[0], buf.at[1], link.at(dz=7))
    to_6 = link.send(buf.at[0], buf.at[6], link.at(dz=2))
    to_2 = link.send(buf.at[0], buf.at[2], link.at(dz=6))
    yield
    to_7.wait_recv()
    to_5 = link.send(buf.at[7], buf.at[5], link.at(dz=2))
    on_arrival(7)
    yield
    to_1.wait_recv()
    to_3 = link.send(buf.at[1], buf.at[3], link.at(dz=6))
    on_arrival(1)
    yield
    to_6.wait_recv()
    if split is None:
        to_4 = [link.send(buf.at[6], buf.at[4], link.at(dz=2))]
    else:
        to_4 = [link.send(buf.at[6, :split], buf.at[4, :split], link.at(dz=2))]
    on_arrival(6)
    yield
    to_2.wait_recv()
    if split is not None:
        to_4.append(link.send(buf.at[2, split:], buf.at[4, split:], link.at(dz=6)))
    on_arrival(2)
    yield
    to_5.wait_recv()
    on_arrival(5)
    to_3.wait_recv()
    on_arrival(3)
    wait_all(to_4)
    on_arrival(4)


def gather_plane(link, buf):
    steps = (1, 3, 2)
    top, low = pl.ds(0, HALF), pl.ds(HALF, HALF)
    got = link.group(buf.at[1:, 1:])
    got_x = [link.send(buf.at[0, 0], buf.at[NX - i, 0], link.at(dx=i)) for i in steps]
    got_y = [link.send(buf.at[0, 0], buf.at[0, NY - j], link.at(dy=j)) for j in steps]
    yield
    for copy_x, copy_y, k in zip(got_x, got_y, steps):
        a = NX - k
        copy_x.wait_recv()
        for j in steps:
            got.send(buf.at[a, 0, top], buf.at[a, NY - j, top], link.at(dy=j))
        copy_y.wait_recv()
        for i in steps:
            got.send(buf.at[0, a, low], buf.at[NX - i, a, low], link.at(dx=i))
        yield
    got.wait_recv()


def interleave(*parts):
    parts = list(parts)
    while parts:
        for part in list(parts):
            try:
                next(part)
            except StopIteration:
                parts.remove(part)


def reduce_z_start(link, part, sent, got, split):
    for i, k in enumerate((3, 5, 4)):
        sent[i] = part(k).astype(BF16)
    return [
        link.send(sent.at[0], got.at[0], link.at(dz=2)),
        link.send(sent.at[1], got.at[1], link.at(dz=6)),
        link.send(sent.at[2, :split], got.at[2, :split], link.at(dz=2)),
        link.send(sent.at[2, split:], got.at[2, split:], link.at(dz=6)),
    ]


def reduce_z_finish(link, part, sent, got, split, first, over_cores=False):
    def onward(i, k):
        if not over_cores:
            return link.send(sent.at[i], got.at[i], link.at(dz=k))
        copies = link.group(got.at[i])
        for e in range(2):
            copies.send(sent.at[i, link.cs[e]], got.at[i, e], link.at(dz=k, dc=e))
        return copies

    first[0].wait_recv()
    sent[3] = (part(1) + got[0].astype(F32)).astype(BF16)
    last = [onward(3, 1)]
    first[1].wait_recv()
    sent[4] = (part(7) + got[1].astype(F32)).astype(BF16)
    last.append(onward(4, 7))
    first[2].wait_recv()
    term = part(2)
    sent[5, :split] = (term[:split] + got[2, :split].astype(F32)).astype(BF16)
    sent[5, split:] = term[split:].astype(BF16)
    last.append(onward(5, 2))
    first[3].wait_recv()
    term = part(6)
    sent[6, :split] = term[:split].astype(BF16)
    sent[6, split:] = (term[split:] + got[2, split:].astype(F32)).astype(BF16)
    last.append(onward(6, 6))
    return last


def reduce_z_sum(part, got, last):
    total = part(0)
    for k, copy in enumerate(last):
        copy.wait_recv()
        total = total + got[3 + k].astype(F32)
    return total


def kernel(
    f_img, f_txt, w_img, w_txt, b_img, b_txt, log_scale, logit_bias,
    rf, ow, o_sums,
    fs, fk, wk, po, pk, rp0, rp, unit, inv, ia, ta, wt, tg, tgx, tgs, tz_sent, tz_got,
    ig0, ig_x32, ig_y32, ig_top, ig_low, r_top, r_low, ig2_top, ig2_low, r2_top, r2_low,
    d16, dk, bp, bx, by, bz, bs, dfs, g32, gy, ry, gz32, gz_sent, gz_got, gz_own,
    send_sems, recv_sems,
):
    link = Links(send_sems, recv_sems)
    x, y, z, c = link.x, link.y, link.z, link.c

    peers = [(0, 0, 0, 1)]
    peers += [(i, 0, 0, e) for i in range(1, NX) for e in range(2)]
    peers += [(0, j, 0, 0) for j in range(1, NY)]
    peers += [(0, 0, k, e) for k in (1, 2, 6, 7) for e in range(2)]
    barrier = pltpu.get_barrier_semaphore()
    for p in peers:
        pl.semaphore_signal(barrier, inc=1, device_id=link.at(*p), device_id_type=MESH)

    shard = link.y_mp[0]

    for t, head in enumerate((w_img, w_txt)):

        @pl.when(c == t)
        def _():
            for k in range(CHUNKS):
                wk[k, shard] = head[:, COLS * k : COLS * (k + 1)]

    for k in range(NX):
        fs[0, k] = f_img[:, KX * k : KX * (k + 1)]
        fs[1, k] = f_txt[:, KX * k : KX * (k + 1)]
    pl.semaphore_wait(barrier, len(peers))

    odd = y - 2 * shard
    ahead, behind = link.at(dy=1), link.at(dy=3)
    partner = tuple(jnp.where(odd == 1, u, v) for u, v in zip(ahead, behind))
    got_f = link.group(fk.at[1:])
    for r in range(NX):
        for e in range(2):
            if (r, e) == (0, 0):
                fk[0] = fs[c, x]
                continue
            got_f.send(
                fs.at[link.cs[e], link.xs[r]],
                fk.at[((NX - r) % NX) * 2 + e],
                link.at(dx=r, dc=e),
            )
    got_w = [link.send(wk.at[k, shard], wk.at[k, shard], partner) for k in range(CHUNKS)]
    got_f.wait_recv()

    rows = fk[...].reshape(8 * ROWS, KX)
    got_p = []
    for k in range(CHUNKS):
        got_w[k].wait_recv()
        part = matmul(rows, wk[k].reshape(KX, COLS))
        rp0[k, 0] = part[:ROWS]
        po[k] = part[ROWS : 2 * ROWS]
        pk[k] = part[2 * ROWS :].astype(BF16).reshape(6, ROWS, COLS)
        got = link.group(rp.at[k])
        got_p.append([link.send(po.at[k], rp0.at[k, 1], link.at(dc=1)), got])
        for r in (2, 1, 3):
            for e in range(2):
                got.send(pk.at[k, (r - 1) * 2 + e], rp.at[k, e, NX - r - 1], link.at(dx=r, dc=e))
    squares = [0.0, 0.0]
    for k in range(CHUNKS):
        wait_all(got_p[k])
        cols = slice(COLS * k, COLS * (k + 1))
        for t, bias in enumerate((b_img, b_txt)):
            e = link.cs[t]
            pre = rp0[k, e] + bias[cols].reshape(1, COLS)
            for r in range(NX - 1):
                pre = pre + rp[k, e, r].astype(F32)
            unit[t, :, cols] = pre
            squares[t] = squares[t] + jnp.sum(pre * pre, axis=1, keepdims=True)
    for t in range(2):
        inverse = lax.rsqrt(squares[t] + EPSILON)
        unit[t] = unit[t] * inverse
        inv[t] = jnp.broadcast_to(inverse, (ROWS, 128))
    ia[0, 0] = unit[0].astype(BF16)
    ta[0, 0] = unit[1].astype(BF16)

    got_s = link.group(ta.at[1])
    got_s.send(ta.at[0, 0], ta.at[1, 0], link.at(dc=1))

    def forward(k):
        got_s.send(ta.at[0, k], ta.at[1, k], link.at(dc=1))

    interleave(gather_z(link, ta.at[0], HALF, forward), gather_plane(link, ia))

    half = NZ * ROWS
    scale = jnp.exp(log_scale[...].reshape(1, 1))
    shift = logit_bias[...].reshape(1, 1)
    images = ia[...].reshape(16 * ROWS, E)
    stats = []
    for h in range(2):
        if h == 1:
            got_s.wait_recv()
        texts = ta[h].reshape(half, E)
        scaled = scale * matmul_bt(texts, images)
        logits = scaled + shift
        signed = logits
        if h == 0:
            row = lax.broadcasted_iota(jnp.int32, logits.shape, 0)
            col = lax.broadcasted_iota(jnp.int32, logits.shape, 1)
            match = jnp.logical_and(row == col, col < ROWS)
            signed = jnp.where(match, -logits, logits)
        small = jnp.exp(-jnp.abs(logits))
        loss = jnp.maximum(signed, 0.0) + jnp.log1p(small)
        errors = jnp.where(logits >= 0.0, 1.0, small) / (1.0 + small)
        if h == 0:
            errors = errors - match.astype(F32)
        weights = (LOSS_FACTOR * errors).astype(BF16)
        sums = (loss, LOSS_FACTOR * errors * scaled, LOSS_FACTOR * errors)
        stats.append([jnp.sum(v, axis=0, keepdims=True) for v in sums])
        wt[:, half * h : half * (h + 1)] = weights.T
        grad = matmul(weights, images)
        if h == 0:
            tg[...] = grad.reshape(NZ, ROWS, E)
        else:
            tgx[...] = grad.reshape(NZ, ROWS, E)
    got_x = [
        link.send(tgx.at[k], tgs.at[k], link.at(dc=1))
        for k in (pl.ds(3, 3), pl.ds(0, 3), pl.ds(6, 2))
    ]

    def txt_part(k):
        return tg[k] + tgs[k]

    top, low = pl.ds(0, HALF), pl.ds(HALF, HALF)
    texts = ta[...].reshape(16 * ROWS, E)
    got_low, got_top = link.group(r_low), link.group(r_top)
    for i, a in enumerate((2, 1, 3, 0)):
        grad = matmul(wt[128 * a : 128 * (a + 1), :], texts).reshape(NY, ROWS, E)
        ig_top[:, a] = grad[:, :HALF].astype(BF16)
        ig_low[a] = grad[:, HALF:].astype(BF16)
        if a:
            ig_x32[a - 1] = grad[0, :HALF]
            got_low.send(ig_low.at[a], r_low.at[a - 1], link.at(dx=a))
        else:
            ig0[...] = grad[0]
            ig_y32[...] = grad[1:, HALF:]
        if i == 0:
            got_x[0].wait_recv()
            first = reduce_z_start(link, txt_part, tz_sent, tz_got, HALF)
    for j in (2, 1, 3):
        got_top.send(ig_top.at[j], r_top.at[j - 1], link.at(dy=j))
    wait_all(got_x[1:])
    got_tg = reduce_z_finish(link, txt_part, tz_sent, tz_got, HALF, first)

    got_low.wait_recv()
    got_low2 = link.group(r2_low)
    for j in (2, 1, 3):
        total = ig_y32[j - 1]
        for i in range(NX - 1):
            total = total + r_low[i, j].astype(F32)
        ig2_low[j - 1] = total.astype(BF16)
        got_low2.send(ig2_low.at[j - 1], r2_low.at[j - 1], link.at(dy=j))
    got_top.wait_recv()
    got_top2 = link.group(r2_top)
    for i in (2, 1, 3):
        total = ig_x32[i - 1]
        for j in range(NY - 1):
            total = total + r_top[j, i].astype(F32)
        ig2_top[i - 1] = total.astype(BF16)
        got_top2.send(ig2_top.at[i - 1], r2_top.at[i - 1], link.at(dx=i))

    grad_txt = reduce_z_sum(txt_part, tz_got, got_tg)
    got_low2.wait_recv()
    got_top2.wait_recv()
    halves = []
    for rows, first_got, second_got in ((top, r_top, r2_top), (low, r_low, r2_low)):
        total = ig0[rows, :]
        for k in range(3):
            total = total + first_got[k, 0].astype(F32) + second_got[k].astype(F32)
        halves.append(total)
    grad_img = jnp.concatenate(halves, axis=0)
    for t, grad in enumerate((grad_img, grad_txt)):
        grad = scale * grad
        delta = inv[t, :, 0:1] * (grad - unit[t] * jnp.sum(unit[t] * grad, axis=1, keepdims=True))
        d16[t] = delta.astype(BF16)
        total = jnp.sum(delta, axis=0, keepdims=True)
        for k in range(9):
            bp[9 * t + k : 9 * t + k + 1, :] = total[:, 128 * k : 128 * (k + 1)]
    for k in range(3):
        lanes = stats[0][k] + stats[1][k]
        bp[18 + k : 19 + k, :] = (
            lanes[:, 0:128] + lanes[:, 128:256] + lanes[:, 256:384] + lanes[:, 384:512]
        )
    bp[21:24, :] = jnp.zeros((3, 128), F32)

    got_b = link.group(bx)
    for r in range(1, NX):
        got_b.send(bp, bx.at[r - 1], link.at(dx=r))
    got_d = link.group(dk.at[1:])
    for r in range(NX):
        for e in range(2):
            if (r, e) == (0, 0):
                dk[0] = d16[c]
                continue
            got_d.send(d16.at[link.cs[e]], dk.at[((NX - r) % NX) * 2 + e], link.at(dx=r, dc=e))
    got_b.wait_recv()
    by[0] = bp[...] + bx[0] + bx[1] + bx[2]
    got_b = link.group(by.at[1:])
    for j in range(1, NY):
        got_b.send(by.at[0], by.at[j], link.at(dy=j))
    got_d.wait_recv()

    deltas = dk[...].reshape(8 * ROWS, E)
    grad_w = matmul_at(fk[...].reshape(8 * ROWS, KX), deltas)
    for j in range(NY):
        part = grad_w[SHARD * (j // 2) : SHARD * (j // 2 + 1), (E // 2) * (j % 2) : (E // 2) * (j % 2 + 1)]
        g32[j] = part
        gy[j] = part.astype(BF16)
    got_y = link.group(ry)
    for j in (2, 1, 3):
        got_y.send(gy.at[link.ys[j]], ry.at[j - 1], link.at(dy=j))

    grad_f = 0.0
    for k in range(CHUNKS):
        grad_f = grad_f + matmul_bt(deltas[:, COLS * k : COLS * (k + 1)], wk[k].reshape(KX, COLS))
    dfs[...] = grad_f.astype(BF16).reshape(8, ROWS, KX)
    got_df = link.group(dfs.at[1:])
    for r in range(NX):
        for e in range(2):
            if (r, e) == (0, 0):
                rf[0, x] = dfs[0]
                continue
            got_df.send(dfs.at[r * 2 + e], rf.at[e, x], link.at(dx=r, dc=e))

    got_b.wait_recv()
    bz[0] = by[0] + by[1] + by[2] + by[3]
    interleave(gather_z(link, bz, None, lambda k: None))
    bias_sum = bz[0]
    for k in range(1, NZ):
        bias_sum = bias_sum + bz[k]
    bs[0] = bias_sum
    got_b = link.send(bs.at[0], bs.at[1], link.at(dc=1))

    got_y.wait_recv()
    total = g32[y]
    for j in range(NY - 1):
        total = total + ry[j].astype(F32)
    for k in range(NZ):
        for e in range(2):
            col = 72 * k + 36 * e
            block = total[:, col : col + 36]
            gz32[k, e] = jnp.concatenate([block[:CUT], block[CUT : 2 * CUT], block[2 * CUT :]], axis=1)

    def head_part(k):
        return gz32[link.zs[k]]

    first = reduce_z_start(link, head_part, gz_sent, gz_got, 1)
    got_own = link.send(gz32.at[z, link.cs[1]], gz_own, link.at(dc=1))
    last = reduce_z_finish(link, head_part, gz_sent, gz_got, 1, first, over_cores=True)
    got_own.wait_recv()
    wait_all(last)
    for e, total in enumerate((gz32[z, c], gz_own[...])):
        for i in range(4):
            total = total + gz_got[3 + i, e].astype(F32)
        ow[e] = total
    got_b.wait_recv()
    o_sums[...] = bs[0] + bs[1]
    got_df.wait_recv()

    for copy in link.started:
        copy.wait_send()


def finish(rf, ow, sums, o_loss, o_scale, o_fi, o_ft, o_wi, o_wt, o_bias):
    c = lax.axis_index("dp") % 2
    for t, (out_f, out_w) in enumerate(((o_fi, o_wi), (o_ft, o_wt))):
        e = jnp.where(c == t, 0, 1)
        for k in range(NX):
            out_f[:, KX * k : KX * (k + 1)] = rf[e, k]
        for k in range(3):
            out_w[:, CUT * k : CUT * (k + 1)] = ow[e][:, 36 * k : 36 * (k + 1)].T
        for k in range(9):
            o_bias[t : t + 1, 128 * k : 128 * (k + 1)] = sums[9 * t + k : 9 * t + k + 1, :]
    o_loss[0] = jnp.sum(sums[18:19, :]) * (1.0 / 8192.0)
    o_scale[0] = jnp.sum(sums[19:20, :])
    o_scale[1] = jnp.sum(sums[20:21, :])


def per_device(f_img, f_txt, w_img, w_txt, b_img, b_txt, log_scale, logit_bias):
    vmem = pl.BlockSpec(memory_space=pltpu.VMEM)
    smem = pl.BlockSpec(memory_space=pltpu.SMEM)
    scratch = [
        ((2, NX, ROWS, KX), BF16),
        ((8, ROWS, KX), BF16),
        ((CHUNKS, 2, SHARD, COLS), BF16),
        ((CHUNKS, ROWS, COLS), F32),
        ((CHUNKS, 6, ROWS, COLS), BF16),
        ((CHUNKS, 2, ROWS, COLS), F32),
        ((CHUNKS, 2, NX - 1, ROWS, COLS), BF16),
        ((2, ROWS, E), F32),
        ((2, ROWS, 128), F32),
        ((NX, NY, ROWS, E), BF16),
        ((2, NZ, ROWS, E), BF16),
        ((512, 512), BF16),
        ((NZ, ROWS, E), F32),
        ((NZ, ROWS, E), F32),
        ((NZ, ROWS, E), F32),
        ((7, ROWS, E), BF16),
        ((7, ROWS, E), BF16),
        ((ROWS, E), F32),
        ((NX - 1, HALF, E), F32),
        ((NY - 1, HALF, E), F32),
        ((NY, NX, HALF, E), BF16),
        ((NX, NY, HALF, E), BF16),
        ((NY - 1, NX, HALF, E), BF16),
        ((NX - 1, NY, HALF, E), BF16),
        ((NX - 1, HALF, E), BF16),
        ((NY - 1, HALF, E), BF16),
        ((NX - 1, HALF, E), BF16),
        ((NY - 1, HALF, E), BF16),
        ((2, ROWS, E), BF16),
        ((8, ROWS, E), BF16),
        ((24, 128), F32),
        ((3, 24, 128), F32),
        ((4, 24, 128), F32),
        ((8, 24, 128), F32),
        ((2, 24, 128), F32),
        ((8, ROWS, KX), BF16),
        ((NY, SHARD, E // 2), F32),
        ((NY, SHARD, E // 2), BF16),
        ((NY - 1, SHARD, E // 2), BF16),
        ((NZ, 2, CUT, 108), F32),
        ((7, 2, CUT, 108), BF16),
        ((7, 2, CUT, 108), BF16),
        ((CUT, 108), F32),
    ]
    parts = pl.pallas_call(
        kernel,
        out_shape=(
            jax.ShapeDtypeStruct((2, NX, ROWS, KX), BF16),
            jax.ShapeDtypeStruct((2, CUT, 108), F32),
            jax.ShapeDtypeStruct((24, 128), F32),
        ),
        in_specs=[vmem] * 8,
        out_specs=(vmem, vmem, vmem),
        scratch_shapes=[pltpu.VMEM(shape, dtype) for shape, dtype in scratch]
        + [pltpu.SemaphoreType.DMA((N_GROUPS,))] * 2,
        compiler_params=pltpu.CompilerParams(
            collective_id=0, has_side_effects=True, vmem_limit_bytes=56 * 2**20
        ),
    )(f_img, f_txt, w_img, w_txt, b_img, b_txt, log_scale, logit_bias)
    loss, scale, fi, ft, wi, wt, bias = pl.pallas_call(
        finish,
        out_shape=(
            jax.ShapeDtypeStruct((1,), F32),
            jax.ShapeDtypeStruct((2,), F32),
            jax.ShapeDtypeStruct((ROWS, D), BF16),
            jax.ShapeDtypeStruct((ROWS, D), BF16),
            jax.ShapeDtypeStruct((36, SHARD), F32),
            jax.ShapeDtypeStruct((36, SHARD), F32),
            jax.ShapeDtypeStruct((2, E), F32),
        ),
        in_specs=[vmem] * 3,
        out_specs=(smem, smem, vmem, vmem, vmem, vmem, vmem),
    )(*parts)
    return loss, scale, fi, ft, wi.T, wt.T, bias


def solution(mesh):
    rows = P(("dp", "mp"), None)
    return jax.shard_map(
        per_device,
        mesh=mesh,
        in_specs=(rows, rows, P("mp", None), P("mp", None), P(), P(), P(), P()),
        out_specs=(P(), P(), rows, rows, P("mp", "dp"), P("mp", "dp"), P()),
        check_vma=False,
    )
```

```python
import functools

import jax
import jax.numpy as jnp
from jax import lax
from jax.experimental import pallas as pl
from jax.experimental.pallas import tpu as pltpu
from jax.sharding import PartitionSpec as P

EPSILON = 1e-06
LOSS_FACTOR = 32.0
NX, NY, NZ = 4, 4, 8
ROWS = 32
HALF = ROWS // 2
D = 1152
E = 1152
SHARD = 144
KX = 2 * SHARD
CHUNKS = 3
COLS = E // CHUNKS
CUT = SHARD // 3
QUARTER = E // 4
MESH = pl.DeviceIdType.MESH
F32 = jnp.float32
BF16 = jnp.bfloat16

N_GROUPS = 65


def ring(place, size):
    steps = [place + k for k in range(size)]
    return [place] + [jnp.where(v >= size, v - size, v) for v in steps[1:]]


class Links:
    def __init__(self, send_sems, recv_sems):
        dp, mp = lax.axis_index("dp"), lax.axis_index("mp")
        self.x, self.y = mp // 2, (mp % 2) * 2 + dp // 16
        self.z, self.c = (dp // 2) % NZ, dp % 2
        self.send_sems, self.recv_sems = send_sems, recv_sems
        self.started = []
        self.xs = ring(self.x, NX)
        self.ys = ring(self.y, NY)
        self.zs = ring(self.z, NZ)
        self.cs = ring(self.c, 2)
        self.x_mp = [2 * v for v in self.xs]
        self.y_mp = [v // 2 for v in self.ys]
        self.y_dp = [(v - 2 * h) * 16 for v, h in zip(self.ys, self.y_mp)]
        self.z_dp = [2 * v for v in self.zs]

    def at(self, dx=0, dy=0, dz=0, dc=0):
        return (self.y_dp[dy] + self.z_dp[dz] + self.cs[dc], self.x_mp[dx] + self.y_mp[dy])

    def group(self, region):
        copies = Group(self, len(self.started), region)
        self.started.append(copies)
        return copies

    def send(self, src, dst, device):
        copies = self.group(dst)
        copies.send(src, dst, device)
        return copies


class Group:
    def __init__(self, link, k, region):
        self.link, self.region = link, region
        self.sems = (link.send_sems.at[k], link.recv_sems.at[k])

    def copy(self, src, dst, device):
        return pltpu.make_async_remote_copy(
            src_ref=src,
            dst_ref=dst,
            send_sem=self.sems[0],
            recv_sem=self.sems[1],
            device_id=device,
            device_id_type=MESH,
        )

    def send(self, src, dst, device):
        self.copy(src, dst, device).start()

    def wait_recv(self):
        self.copy(self.region, self.region, self.link.at(dc=1)).wait_recv()

    def wait_send(self):
        self.copy(self.region, self.region, self.link.at(dc=1)).wait_send()


def matmul(a, b):
    return lax.dot_general(a, b, (((1,), (0,)), ((), ())), preferred_element_type=F32)


def matmul_bt(a, b):
    return lax.dot_general(a, b, (((1,), (1,)), ((), ())), preferred_element_type=F32)


def matmul_at(a, b):
    return lax.dot_general(a, b, (((0,), (0,)), ((), ())), preferred_element_type=F32)


def wait_all(copies):
    for copy in copies:
        copy.wait_recv()


def gather_z(link, buf, split, on_arrival):
    to_7 = link.send(buf.at[0], buf.at[7], link.at(dz=1))
    to_1 = link.send(buf.at[0], buf.at[1], link.at(dz=7))
    to_6 = link.send(buf.at[0], buf.at[6], link.at(dz=2))
    to_2 = link.send(buf.at[0], buf.at[2], link.at(dz=6))
    yield
    to_7.wait_recv()
    to_5 = link.send(buf.at[7], buf.at[5], link.at(dz=2))
    on_arrival(7)
    yield
    to_1.wait_recv()
    to_3 = link.send(buf.at[1], buf.at[3], link.at(dz=6))
    on_arrival(1)
    yield
    to_6.wait_recv()
    if split is None:
        to_4 = [link.send(buf.at[6], buf.at[4], link.at(dz=2))]
    else:
        to_4 = [link.send(buf.at[6, :split], buf.at[4, :split], link.at(dz=2))]
    on_arrival(6)
    yield
    to_2.wait_recv()
    if split is not None:
        to_4.append(link.send(buf.at[2, split:], buf.at[4, split:], link.at(dz=6)))
    on_arrival(2)
    yield
    to_5.wait_recv()
    on_arrival(5)
    to_3.wait_recv()
    on_arrival(3)
    wait_all(to_4)
    on_arrival(4)


def gather_plane(link, buf):
    steps = (1, 3, 2)
    top, low = pl.ds(0, HALF), pl.ds(HALF, HALF)
    got = link.group(buf.at[1:, 1:])
    got_x = [link.send(buf.at[0, 0], buf.at[NX - i, 0], link.at(dx=i)) for i in steps]
    got_y = [link.send(buf.at[0, 0], buf.at[0, NY - j], link.at(dy=j)) for j in steps]
    yield
    for copy_x, copy_y, k in zip(got_x, got_y, steps):
        a = NX - k
        copy_x.wait_recv()
        for j in steps:
            got.send(buf.at[a, 0, top], buf.at[a, NY - j, top], link.at(dy=j))
        copy_y.wait_recv()
        for i in steps:
            got.send(buf.at[0, a, low], buf.at[NX - i, a, low], link.at(dx=i))
        yield
    got.wait_recv()


def interleave(*parts):
    parts = list(parts)
    while parts:
        for part in list(parts):
            try:
                next(part)
            except StopIteration:
                parts.remove(part)


def reduce_z_start(link, part, sent, got, split):
    for i, k in enumerate((3, 5, 4)):
        sent[i] = part(k).astype(BF16)
    return [
        link.send(sent.at[0], got.at[0], link.at(dz=2)),
        link.send(sent.at[1], got.at[1], link.at(dz=6)),
        link.send(sent.at[2, :split], got.at[2, :split], link.at(dz=2)),
        link.send(sent.at[2, split:], got.at[2, split:], link.at(dz=6)),
    ]


def reduce_z_finish(link, part, sent, got, split, first, over_cores=False):
    def onward(i, k):
        if not over_cores:
            return link.send(sent.at[i], got.at[i], link.at(dz=k))
        copies = link.group(got.at[i])
        for e in range(2):
            copies.send(sent.at[i, link.cs[e]], got.at[i, e], link.at(dz=k, dc=e))
        return copies

    first[0].wait_recv()
    sent[3] = (part(1) + got[0].astype(F32)).astype(BF16)
    last = [onward(3, 1)]
    first[1].wait_recv()
    sent[4] = (part(7) + got[1].astype(F32)).astype(BF16)
    last.append(onward(4, 7))
    first[2].wait_recv()
    term = part(2)
    sent[5, :split] = (term[:split] + got[2, :split].astype(F32)).astype(BF16)
    sent[5, split:] = term[split:].astype(BF16)
    last.append(onward(5, 2))
    first[3].wait_recv()
    term = part(6)
    sent[6, :split] = term[:split].astype(BF16)
    sent[6, split:] = (term[split:] + got[2, split:].astype(F32)).astype(BF16)
    last.append(onward(6, 6))
    return last


def reduce_z_sum(part, got, last):
    total = part(0)
    for k, copy in enumerate(last):
        copy.wait_recv()
        total = total + got[3 + k].astype(F32)
    return total


def kernel(
    f_img, f_txt, w_img, w_txt, b_img, b_txt, log_scale, logit_bias,
    rf, ow, o_sums,
    fs, fk, wk, po, pk, rp0, rp, unit, inv, ia, ta, wt, wn, tg, tgx, tgs, tz_sent, tz_got,
    ig0, ig_x32, ig_y32, ig_top, ig_low, r_top, r_low, ig2_top, ig2_low, r2_top, r2_low,
    d16, dk, bp, bx, by, bz, bs, dfs, g32, gy, ry, gz32, gz_sent, gz_got, gz_own,
    send_sems, recv_sems,
):
    link = Links(send_sems, recv_sems)
    x, y, z, c = link.x, link.y, link.z, link.c

    peers = [(0, 0, 0, 1)]
    peers += [(i, 0, 0, e) for i in range(1, NX) for e in range(2)]
    peers += [(0, j, 0, 0) for j in range(1, NY)]
    peers += [(0, 0, k, e) for k in (1, 2, 6, 7) for e in range(2)]
    barrier = pltpu.get_barrier_semaphore()
    for p in peers:
        pl.semaphore_signal(barrier, inc=1, device_id=link.at(*p), device_id_type=MESH)

    shard = link.y_mp[0]

    for t, head in enumerate((w_img, w_txt)):

        @pl.when(c == t)
        def _():
            for k in range(CHUNKS):
                wk[k, shard] = head[:, COLS * k : COLS * (k + 1)]

    for k in range(NX):
        fs[0, k] = f_img[:, KX * k : KX * (k + 1)]
        fs[1, k] = f_txt[:, KX * k : KX * (k + 1)]
    pl.semaphore_wait(barrier, len(peers))

    odd = y - 2 * shard
    ahead, behind = link.at(dy=1), link.at(dy=3)
    partner = tuple(jnp.where(odd == 1, u, v) for u, v in zip(ahead, behind))
    got_f = link.group(fk.at[1:])
    for r in range(NX):
        for e in range(2):
            if (r, e) == (0, 0):
                fk[0] = fs[c, x]
                continue
            got_f.send(
                fs.at[link.cs[e], link.xs[r]],
                fk.at[((NX - r) % NX) * 2 + e],
                link.at(dx=r, dc=e),
            )
    got_w = [link.send(wk.at[k, shard], wk.at[k, shard], partner) for k in range(CHUNKS)]
    got_f.wait_recv()

    rows = fk[...].reshape(8 * ROWS, KX)
    got_p = []
    for k in range(CHUNKS):
        got_w[k].wait_recv()
        part = matmul(rows, wk[k].reshape(KX, COLS))
        rp0[k, 0] = part[:ROWS]
        po[k] = part[ROWS : 2 * ROWS]
        pk[k] = part[2 * ROWS :].astype(BF16).reshape(6, ROWS, COLS)
        got = link.group(rp.at[k])
        got_p.append([link.send(po.at[k], rp0.at[k, 1], link.at(dc=1)), got])
        for r in (2, 1, 3):
            for e in range(2):
                got.send(pk.at[k, (r - 1) * 2 + e], rp.at[k, e, NX - r - 1], link.at(dx=r, dc=e))
    squares = [0.0, 0.0]
    for k in range(CHUNKS):
        wait_all(got_p[k])
        cols = slice(COLS * k, COLS * (k + 1))
        for t, bias in enumerate((b_img, b_txt)):
            e = link.cs[t]
            pre = rp0[k, e] + bias[cols].reshape(1, COLS)
            for r in range(NX - 1):
                pre = pre + rp[k, e, r].astype(F32)
            unit[t, :, cols] = pre
            squares[t] = squares[t] + jnp.sum(pre * pre, axis=1, keepdims=True)
    for t in range(2):
        inverse = lax.rsqrt(squares[t] + EPSILON)
        unit[t] = unit[t] * inverse
        inv[t] = jnp.broadcast_to(inverse, (ROWS, 128))
    ia[0, 0] = unit[0].astype(BF16)
    ta[0, 0] = unit[1].astype(BF16)

    got_s = link.group(ta.at[1])
    got_s.send(ta.at[0, 0], ta.at[1, 0], link.at(dc=1))

    def forward(k):
        got_s.send(ta.at[0, k], ta.at[1, k], link.at(dc=1))

    interleave(gather_z(link, ta.at[0], HALF, forward), gather_plane(link, ia))

    half = NZ * ROWS
    scale = jnp.exp(log_scale[...].reshape(1, 1))
    shift = logit_bias[...].reshape(1, 1)
    images = ia[...].reshape(16 * ROWS, E)
    stats = []
    for h in range(2):
        if h == 1:
            got_s.wait_recv()
        texts = ta[h].reshape(half, E)
        scaled = scale * matmul_bt(texts, images)
        logits = scaled + shift
        signed = logits
        if h == 0:
            row = lax.broadcasted_iota(jnp.int32, logits.shape, 0)
            col = lax.broadcasted_iota(jnp.int32, logits.shape, 1)
            match = jnp.logical_and(row == col, col < ROWS)
            signed = jnp.where(match, -logits, logits)
        small = jnp.exp(-jnp.abs(logits))
        loss = jnp.maximum(signed, 0.0) + jnp.log1p(small)
        errors = jnp.where(logits >= 0.0, 1.0, small) / (1.0 + small)
        if h == 0:
            errors = errors - match.astype(F32)
        weights = (LOSS_FACTOR * errors).astype(BF16)
        sums = (loss, LOSS_FACTOR * errors * scaled, LOSS_FACTOR * errors)
        stats.append([jnp.sum(v, axis=0, keepdims=True) for v in sums])
        wt[:, half * h : half * (h + 1)] = weights.T
        if h == 0:
            wn[...] = weights
    tgx[...] = matmul(weights, images).reshape(NZ, ROWS, E)
    got_x = [
        link.send(tgx.at[k], tgs.at[k], link.at(dc=1))
        for k in (pl.ds(3, 3), pl.ds(0, 3), pl.ds(6, 2))
    ]

    def txt_part(k):
        return tg[k] + tgs[k]

    top, low = pl.ds(0, HALF), pl.ds(HALF, HALF)
    texts = ta[...].reshape(16 * ROWS, E)
    got_low, got_top = link.group(r_low), link.group(r_top)
    for i, a in enumerate((2, 1, 3, 0)):
        grad = matmul(wt[128 * a : 128 * (a + 1), :], texts).reshape(NY, ROWS, E)
        ig_top[:, a] = grad[:, :HALF].astype(BF16)
        ig_low[a] = grad[:, HALF:].astype(BF16)
        if a:
            ig_x32[a - 1] = grad[0, :HALF]
            got_low.send(ig_low.at[a], r_low.at[a - 1], link.at(dx=a))
        else:
            ig0[...] = grad[0]
            ig_y32[...] = grad[1:, HALF:]
        if i == 0:
            tg[...] = matmul(wn[...], images).reshape(NZ, ROWS, E)
            got_x[0].wait_recv()
            first = reduce_z_start(link, txt_part, tz_sent, tz_got, HALF)
    for j in (2, 1, 3):
        got_top.send(ig_top.at[j], r_top.at[j - 1], link.at(dy=j))
    wait_all(got_x[1:])
    got_tg = reduce_z_finish(link, txt_part, tz_sent, tz_got, HALF, first)

    got_low.wait_recv()
    got_low2 = link.group(r2_low)
    for j in (2, 1, 3):
        total = ig_y32[j - 1]
        for i in range(NX - 1):
            total = total + r_low[i, j].astype(F32)
        ig2_low[j - 1] = total.astype(BF16)
        got_low2.send(ig2_low.at[j - 1], r2_low.at[j - 1], link.at(dy=j))
    got_top.wait_recv()
    got_top2 = link.group(r2_top)
    for i in (2, 1, 3):
        total = ig_x32[i - 1]
        for j in range(NY - 1):
            total = total + r_top[j, i].astype(F32)
        ig2_top[i - 1] = total.astype(BF16)
        got_top2.send(ig2_top.at[i - 1], r2_top.at[i - 1], link.at(dx=i))

    grad_txt = reduce_z_sum(txt_part, tz_got, got_tg)
    got_low2.wait_recv()
    got_top2.wait_recv()
    halves = []
    for rows, first_got, second_got in ((top, r_top, r2_top), (low, r_low, r2_low)):
        total = ig0[rows, :]
        for k in range(3):
            total = total + first_got[k, 0].astype(F32) + second_got[k].astype(F32)
        halves.append(total)
    grad_img = jnp.concatenate(halves, axis=0)
    for t, grad in enumerate((grad_img, grad_txt)):
        grad = scale * grad
        delta = inv[t, :, 0:1] * (grad - unit[t] * jnp.sum(unit[t] * grad, axis=1, keepdims=True))
        for h in range(2):
            for q in range(2):
                col = 2 * QUARTER * q + QUARTER * h
                d16[h, t, :, QUARTER * q : QUARTER * (q + 1)] = delta[:, col : col + QUARTER].astype(BF16)
        total = jnp.sum(delta, axis=0, keepdims=True)
        for k in range(9):
            bp[9 * t + k : 9 * t + k + 1, :] = total[:, 128 * k : 128 * (k + 1)]
    for k in range(3):
        lanes = stats[0][k] + stats[1][k]
        bp[18 + k : 19 + k, :] = (
            lanes[:, 0:128] + lanes[:, 128:256] + lanes[:, 256:384] + lanes[:, 384:512]
        )
    bp[21:24, :] = jnp.zeros((3, 128), F32)

    got_b = link.group(bx)
    for r in range(1, NX):
        got_b.send(bp, bx.at[r - 1], link.at(dx=r))
    got_d = []
    for h in range(2):
        got_d.append(link.group(dk.at[h, 1:]))
        for r in (0, 2, 1, 3):
            for e in range(2):
                if (r, e) == (0, 0):
                    dk[h, 0] = d16[h, c]
                    continue
                got_d[h].send(
                    d16.at[h, link.cs[e]], dk.at[h, ((NX - r) % NX) * 2 + e], link.at(dx=r, dc=e)
                )
    got_b.wait_recv()
    by[0] = bp[...] + bx[0] + bx[1] + bx[2]
    got_b = link.group(by.at[1:])
    for j in range(1, NY):
        got_b.send(by.at[0], by.at[j], link.at(dy=j))

    rows = fk[...].reshape(8 * ROWS, KX)
    got_y, deltas = [], []
    for h in range(2):
        got_d[h].wait_recv()
        half_deltas = dk[h].reshape(8 * ROWS, 2 * QUARTER)
        deltas.append(half_deltas)
        grad_w = matmul_at(rows, half_deltas)
        for j in range(NY):
            block = grad_w[SHARD * (j // 2) : SHARD * (j // 2 + 1), QUARTER * (j % 2) : QUARTER * (j % 2 + 1)]
            block = jnp.concatenate([block[:CUT], block[CUT : 2 * CUT], block[2 * CUT :]], axis=1)
            g32[h, j] = block
            gy[h, j] = block.astype(BF16)
        got_y.append(link.group(ry.at[h]))
        for j in (2, 1, 3):
            got_y[h].send(gy.at[h, link.ys[j]], ry.at[h, j - 1], link.at(dy=j))

    deltas = jnp.concatenate([d[:, QUARTER * q : QUARTER * (q + 1)] for q in range(2) for d in deltas], axis=1)
    grad_f = 0.0
    for k in range(CHUNKS):
        grad_f = grad_f + matmul_bt(deltas[:, COLS * k : COLS * (k + 1)], wk[k].reshape(KX, COLS))
    dfs[...] = grad_f.astype(BF16).reshape(8, ROWS, KX)
    got_df = link.group(dfs.at[1:])
    for r in range(NX):
        for e in range(2):
            if (r, e) == (0, 0):
                rf[0, x] = dfs[0]
                continue
            got_df.send(dfs.at[r * 2 + e], rf.at[e, x], link.at(dx=r, dc=e))

    got_b.wait_recv()
    bz[0] = by[0] + by[1] + by[2] + by[3]
    interleave(gather_z(link, bz, None, lambda k: None))
    bias_sum = bz[0]
    for k in range(1, NZ):
        bias_sum = bias_sum + bz[k]
    bs[0] = bias_sum
    got_b = link.send(bs.at[0], bs.at[1], link.at(dc=1))

    for h in range(2):
        got_y[h].wait_recv()
        total = g32[h, y]
        for j in range(NY - 1):
            total = total + ry[h, j].astype(F32)
        for k in range(NZ // 2):
            for e in range(2):
                col = 72 * k + 36 * e
                block = [total[:, QUARTER * i + col : QUARTER * i + col + 36] for i in range(3)]
                gz32[NZ // 2 * h + k, e] = jnp.concatenate(block, axis=1)

    def head_part(k):
        return gz32[link.zs[k]]

    first = reduce_z_start(link, head_part, gz_sent, gz_got, 1)
    got_own = link.send(gz32.at[z, link.cs[1]], gz_own, link.at(dc=1))
    last = reduce_z_finish(link, head_part, gz_sent, gz_got, 1, first, over_cores=True)
    got_own.wait_recv()
    wait_all(last)
    for e, total in enumerate((gz32[z, c], gz_own[...])):
        for i in range(4):
            total = total + gz_got[3 + i, e].astype(F32)
        ow[e] = total
    got_b.wait_recv()
    o_sums[...] = bs[0] + bs[1]
    got_df.wait_recv()

    for copy in link.started:
        copy.wait_send()


def finish(rf, ow, sums, o_loss, o_scale, o_fi, o_ft, o_wi, o_wt, o_bias):
    c = lax.axis_index("dp") % 2
    for t, (out_f, out_w) in enumerate(((o_fi, o_wi), (o_ft, o_wt))):
        e = jnp.where(c == t, 0, 1)
        for k in range(NX):
            out_f[:, KX * k : KX * (k + 1)] = rf[e, k]
        for k in range(3):
            out_w[:, CUT * k : CUT * (k + 1)] = ow[e][:, 36 * k : 36 * (k + 1)].T
        for k in range(9):
            o_bias[t : t + 1, 128 * k : 128 * (k + 1)] = sums[9 * t + k : 9 * t + k + 1, :]
    o_loss[0] = jnp.sum(sums[18:19, :]) * (1.0 / 8192.0)
    o_scale[0] = jnp.sum(sums[19:20, :])
    o_scale[1] = jnp.sum(sums[20:21, :])


def per_device(f_img, f_txt, w_img, w_txt, b_img, b_txt, log_scale, logit_bias):
    vmem = pl.BlockSpec(memory_space=pltpu.VMEM)
    smem = pl.BlockSpec(memory_space=pltpu.SMEM)
    scratch = [
        ((2, NX, ROWS, KX), BF16),
        ((8, ROWS, KX), BF16),
        ((CHUNKS, 2, SHARD, COLS), BF16),
        ((CHUNKS, ROWS, COLS), F32),
        ((CHUNKS, 6, ROWS, COLS), BF16),
        ((CHUNKS, 2, ROWS, COLS), F32),
        ((CHUNKS, 2, NX - 1, ROWS, COLS), BF16),
        ((2, ROWS, E), F32),
        ((2, ROWS, 128), F32),
        ((NX, NY, ROWS, E), BF16),
        ((2, NZ, ROWS, E), BF16),
        ((512, 512), BF16),
        ((256, 512), BF16),
        ((NZ, ROWS, E), F32),
        ((NZ, ROWS, E), F32),
        ((NZ, ROWS, E), F32),
        ((7, ROWS, E), BF16),
        ((7, ROWS, E), BF16),
        ((ROWS, E), F32),
        ((NX - 1, HALF, E), F32),
        ((NY - 1, HALF, E), F32),
        ((NY, NX, HALF, E), BF16),
        ((NX, NY, HALF, E), BF16),
        ((NY - 1, NX, HALF, E), BF16),
        ((NX - 1, NY, HALF, E), BF16),
        ((NX - 1, HALF, E), BF16),
        ((NY - 1, HALF, E), BF16),
        ((NX - 1, HALF, E), BF16),
        ((NY - 1, HALF, E), BF16),
        ((2, 2, ROWS, 2 * QUARTER), BF16),
        ((2, 8, ROWS, 2 * QUARTER), BF16),
        ((24, 128), F32),
        ((3, 24, 128), F32),
        ((4, 24, 128), F32),
        ((8, 24, 128), F32),
        ((2, 24, 128), F32),
        ((8, ROWS, KX), BF16),
        ((2, NY, CUT, 3 * QUARTER), F32),
        ((2, NY, CUT, 3 * QUARTER), BF16),
        ((2, NY - 1, CUT, 3 * QUARTER), BF16),
        ((NZ, 2, CUT, 108), F32),
        ((7, 2, CUT, 108), BF16),
        ((7, 2, CUT, 108), BF16),
        ((CUT, 108), F32),
    ]
    parts = pl.pallas_call(
        kernel,
        out_shape=(
            jax.ShapeDtypeStruct((2, NX, ROWS, KX), BF16),
            jax.ShapeDtypeStruct((2, CUT, 108), F32),
            jax.ShapeDtypeStruct((24, 128), F32),
        ),
        in_specs=[vmem] * 8,
        out_specs=(vmem, vmem, vmem),
        scratch_shapes=[pltpu.VMEM(shape, dtype) for shape, dtype in scratch]
        + [pltpu.SemaphoreType.DMA((N_GROUPS,))] * 2,
        compiler_params=pltpu.CompilerParams(
            collective_id=0, has_side_effects=True, vmem_limit_bytes=56 * 2**20
        ),
    )(f_img, f_txt, w_img, w_txt, b_img, b_txt, log_scale, logit_bias)
    loss, scale, fi, ft, wi, wt, bias = pl.pallas_call(
        finish,
        out_shape=(
            jax.ShapeDtypeStruct((1,), F32),
            jax.ShapeDtypeStruct((2,), F32),
            jax.ShapeDtypeStruct((ROWS, D), BF16),
            jax.ShapeDtypeStruct((ROWS, D), BF16),
            jax.ShapeDtypeStruct((36, SHARD), F32),
            jax.ShapeDtypeStruct((36, SHARD), F32),
            jax.ShapeDtypeStruct((2, E), F32),
        ),
        in_specs=[vmem] * 3,
        out_specs=(smem, smem, vmem, vmem, vmem, vmem, vmem),
    )(*parts)
    return loss, scale, fi, ft, wi.T, wt.T, bias


def solution(mesh):
    rows = P(("dp", "mp"), None)
    return jax.shard_map(
        per_device,
        mesh=mesh,
        in_specs=(rows, rows, P("mp", None), P("mp", None), P(), P(), P(), P()),
        out_specs=(P(), P(), rows, rows, P("mp", "dp"), P("mp", "dp"), P()),
        check_vma=False,
    )
```

```python
import functools

import jax
import jax.numpy as jnp
from jax import lax
from jax.experimental import pallas as pl
from jax.experimental.pallas import tpu as pltpu
from jax.sharding import PartitionSpec as P

EPSILON = 1e-06
LOSS_FACTOR = 32.0
NX, NY, NZ = 4, 4, 8
ROWS = 32
HALF = ROWS // 2
D = 1152
E = 1152
SHARD = 144
KX = 2 * SHARD
CHUNKS = 3
COLS = E // CHUNKS
CUT = SHARD // 3
QUARTER = E // 4
MESH = pl.DeviceIdType.MESH
F32 = jnp.float32
BF16 = jnp.bfloat16

N_GROUPS = 65


def ring(place, size):
    steps = [place + k for k in range(size)]
    return [place] + [jnp.where(v >= size, v - size, v) for v in steps[1:]]


class Links:
    def __init__(self, send_sems, recv_sems):
        dp, mp = lax.axis_index("dp"), lax.axis_index("mp")
        self.x, self.y = mp // 2, (mp % 2) * 2 + dp // 16
        self.z, self.c = (dp // 2) % NZ, dp % 2
        self.send_sems, self.recv_sems = send_sems, recv_sems
        self.started = []
        self.xs = ring(self.x, NX)
        self.ys = ring(self.y, NY)
        self.zs = ring(self.z, NZ)
        self.cs = ring(self.c, 2)
        self.x_mp = [2 * v for v in self.xs]
        self.y_mp = [v // 2 for v in self.ys]
        self.y_dp = [(v - 2 * h) * 16 for v, h in zip(self.ys, self.y_mp)]
        self.z_dp = [2 * v for v in self.zs]

    def at(self, dx=0, dy=0, dz=0, dc=0):
        return (self.y_dp[dy] + self.z_dp[dz] + self.cs[dc], self.x_mp[dx] + self.y_mp[dy])

    def group(self, region):
        copies = Group(self, len(self.started), region)
        self.started.append(copies)
        return copies

    def send(self, src, dst, device):
        copies = self.group(dst)
        copies.send(src, dst, device)
        return copies


class Group:
    def __init__(self, link, k, region):
        self.link, self.region = link, region
        self.sems = (link.send_sems.at[k], link.recv_sems.at[k])

    def copy(self, src, dst, device):
        return pltpu.make_async_remote_copy(
            src_ref=src,
            dst_ref=dst,
            send_sem=self.sems[0],
            recv_sem=self.sems[1],
            device_id=device,
            device_id_type=MESH,
        )

    def send(self, src, dst, device):
        self.copy(src, dst, device).start()

    def wait_recv(self):
        self.copy(self.region, self.region, self.link.at(dc=1)).wait_recv()

    def wait_send(self):
        self.copy(self.region, self.region, self.link.at(dc=1)).wait_send()


def matmul(a, b):
    return lax.dot_general(a, b, (((1,), (0,)), ((), ())), preferred_element_type=F32)


def matmul_bt(a, b):
    return lax.dot_general(a, b, (((1,), (1,)), ((), ())), preferred_element_type=F32)


def matmul_at(a, b):
    return lax.dot_general(a, b, (((0,), (0,)), ((), ())), preferred_element_type=F32)


def wait_all(copies):
    for copy in copies:
        copy.wait_recv()


def gather_z(link, buf, split, on_arrival):
    to_6 = link.send(buf.at[0], buf.at[6], link.at(dz=2))
    to_2 = link.send(buf.at[0], buf.at[2], link.at(dz=6))
    to_7 = link.send(buf.at[0], buf.at[7], link.at(dz=1))
    to_1 = link.send(buf.at[0], buf.at[1], link.at(dz=7))
    yield
    to_6.wait_recv()
    to_5 = link.send(buf.at[6], buf.at[5], link.at(dz=1))
    if split is None:
        to_4 = [link.send(buf.at[6], buf.at[4], link.at(dz=2))]
    else:
        to_4 = [link.send(buf.at[6, :split], buf.at[4, :split], link.at(dz=2))]
    on_arrival(6)
    yield
    to_2.wait_recv()
    to_3 = link.send(buf.at[2], buf.at[3], link.at(dz=7))
    if split is not None:
        to_4.append(link.send(buf.at[2, split:], buf.at[4, split:], link.at(dz=6)))
    on_arrival(2)
    yield
    to_7.wait_recv()
    on_arrival(7)
    yield
    to_1.wait_recv()
    on_arrival(1)
    yield
    to_5.wait_recv()
    on_arrival(5)
    to_3.wait_recv()
    on_arrival(3)
    wait_all(to_4)
    on_arrival(4)


def gather_plane(link, buf):
    steps = (1, 3, 2)
    top, low = pl.ds(0, HALF), pl.ds(HALF, HALF)
    got = link.group(buf.at[1:, 1:])
    got_x = [link.send(buf.at[0, 0], buf.at[NX - i, 0], link.at(dx=i)) for i in steps]
    got_y = [link.send(buf.at[0, 0], buf.at[0, NY - j], link.at(dy=j)) for j in steps]
    yield
    for copy_x, copy_y, k in zip(got_x, got_y, steps):
        a = NX - k
        copy_x.wait_recv()
        for j in steps:
            got.send(buf.at[a, 0, top], buf.at[a, NY - j, top], link.at(dy=j))
        copy_y.wait_recv()
        for i in steps:
            got.send(buf.at[0, a, low], buf.at[NX - i, a, low], link.at(dx=i))
        yield
    got.wait_recv()


def interleave(*parts):
    parts = list(parts)
    while parts:
        for part in list(parts):
            try:
                next(part)
            except StopIteration:
                parts.remove(part)


def reduce_z_start(link, part, sent, got, split):
    for i, k in enumerate((4, 3, 5)):
        sent[i] = part(k).astype(BF16)
    return [
        link.send(sent.at[0, :split], got.at[0, :split], link.at(dz=2)),
        link.send(sent.at[0, split:], got.at[0, split:], link.at(dz=6)),
        link.send(sent.at[1], got.at[1], link.at(dz=1)),
        link.send(sent.at[2], got.at[2], link.at(dz=7)),
    ]


def reduce_z_finish(link, part, sent, got, split, first, over_cores=False):
    def onward(i, k):
        if not over_cores:
            return link.send(sent.at[i], got.at[i], link.at(dz=k))
        copies = link.group(got.at[i])
        for e in range(2):
            copies.send(sent.at[i, link.cs[e]], got.at[i, e], link.at(dz=k, dc=e))
        return copies

    last = []
    for i, k in ((3, 1), (4, 7)):
        sent[i] = part(k).astype(BF16)
        last.append(onward(i, k))
    first[0].wait_recv()
    first[2].wait_recv()
    term = part(2) + got[1].astype(F32)
    sent[5, :split] = (term[:split] + got[0, :split].astype(F32)).astype(BF16)
    sent[5, split:] = term[split:].astype(BF16)
    last.append(onward(5, 2))
    first[1].wait_recv()
    first[3].wait_recv()
    term = part(6) + got[2].astype(F32)
    sent[6, :split] = term[:split].astype(BF16)
    sent[6, split:] = (term[split:] + got[0, split:].astype(F32)).astype(BF16)
    last.append(onward(6, 6))
    return last


def reduce_z_sum(part, got, last):
    total = part(0)
    for k, copy in enumerate(last):
        copy.wait_recv()
        total = total + got[3 + k].astype(F32)
    return total


def kernel(
    f_img, f_txt, w_img, w_txt, b_img, b_txt, log_scale, logit_bias,
    rf, ow, o_sums,
    fv, fs, fk, wk, po, pk, rp0, rp, unit, inv, ia, ta, wt, wn, tg, tgx, tgs, tz_sent, tz_got,
    ig0, ig_x32, ig_y32, ig_top, ig_low, r_top, r_low, ig2_top, ig2_low, r2_top, r2_low,
    d16, dk, bp, bx, by, bz, bs, dfs, g32, gy, ry, gz32, gz_sent, gz_got, gz_own,
    send_sems, recv_sems, load_sems,
):
    link = Links(send_sems, recv_sems)
    x, y, z, c = link.x, link.y, link.z, link.c

    shard = link.y_mp[0]
    for t, head in enumerate((w_img, w_txt)):

        @pl.when(c == t)
        def _():
            for k in range(CHUNKS):
                cols = pl.ds(COLS * k, COLS)
                pltpu.make_async_copy(head.at[:, cols], wk.at[k, shard], load_sems.at[0]).start()

    loads = [
        pltpu.make_async_copy(f, fv.at[t], load_sems.at[1 + t]) for t, f in enumerate((f_img, f_txt))
    ]
    for load in loads:
        load.start()

    peers = [(0, 0, 0, 1)]
    peers += [(i, 0, 0, e) for i in range(1, NX) for e in range(2)]
    peers += [(0, j, 0, 0) for j in range(1, NY)]
    peers += [(0, 0, k, e) for k in (1, 2, 6, 7) for e in range(2)]
    barrier = pltpu.get_barrier_semaphore()
    for p in peers:
        pl.semaphore_signal(barrier, inc=1, device_id=link.at(*p), device_id_type=MESH)

    for t, load in enumerate(loads):
        load.wait()
        for k in range(NX):
            fs[t, k] = fv[t, :, KX * k : KX * (k + 1)]
    own_head = wk.at[:, shard]
    pltpu.make_async_copy(own_head, own_head, load_sems.at[0]).wait()
    pl.semaphore_wait(barrier, len(peers))

    odd = y - 2 * shard
    ahead, behind = link.at(dy=1), link.at(dy=3)
    partner = tuple(jnp.where(odd == 1, u, v) for u, v in zip(ahead, behind))
    got_f = link.group(fk.at[1:])
    for r in range(NX):
        for e in range(2):
            if (r, e) == (0, 0):
                fk[0] = fs[c, x]
                continue
            got_f.send(
                fs.at[link.cs[e], link.xs[r]],
                fk.at[((NX - r) % NX) * 2 + e],
                link.at(dx=r, dc=e),
            )
    got_w = [link.send(wk.at[k, shard], wk.at[k, shard], partner) for k in range(CHUNKS)]
    got_f.wait_recv()

    rows = fk[...].reshape(8 * ROWS, KX)
    got_p = []
    for k in range(CHUNKS):
        got_w[k].wait_recv()
        part = matmul(rows, wk[k].reshape(KX, COLS))
        rp0[k, 0] = part[:ROWS]
        po[k] = part[ROWS : 2 * ROWS]
        pk[k] = part[2 * ROWS :].astype(BF16).reshape(6, ROWS, COLS)
        got = link.group(rp.at[k])
        got_p.append([link.send(po.at[k], rp0.at[k, 1], link.at(dc=1)), got])
        for r in (2, 1, 3):
            for e in range(2):
                got.send(pk.at[k, (r - 1) * 2 + e], rp.at[k, e, NX - r - 1], link.at(dx=r, dc=e))
    squares = [0.0, 0.0]
    for k in range(CHUNKS):
        wait_all(got_p[k])
        cols = slice(COLS * k, COLS * (k + 1))
        for t, bias in enumerate((b_img, b_txt)):
            e = link.cs[t]
            pre = rp0[k, e] + bias[cols].reshape(1, COLS)
            for r in range(NX - 1):
                pre = pre + rp[k, e, r].astype(F32)
            unit[t, :, cols] = pre
            squares[t] = squares[t] + jnp.sum(pre * pre, axis=1, keepdims=True)
    for t in range(2):
        inverse = lax.rsqrt(squares[t] + EPSILON)
        unit[t] = unit[t] * inverse
        inv[t] = jnp.broadcast_to(inverse, (ROWS, 128))
    ia[0, 0] = unit[0].astype(BF16)
    ta[0, 0] = unit[1].astype(BF16)

    got_s = link.group(ta.at[1])
    got_s.send(ta.at[0, 0], ta.at[1, 0], link.at(dc=1))

    def forward(k):
        got_s.send(ta.at[0, k], ta.at[1, k], link.at(dc=1))

    interleave(gather_z(link, ta.at[0], HALF, forward), gather_plane(link, ia))

    half = NZ * ROWS
    scale = jnp.exp(log_scale[...].reshape(1, 1))
    shift = logit_bias[...].reshape(1, 1)
    images = ia[...].reshape(16 * ROWS, E)
    stats = []
    for h in range(2):
        if h == 1:
            got_s.wait_recv()
        texts = ta[h].reshape(half, E)
        scaled = scale * matmul_bt(texts, images)
        logits = scaled + shift
        signed = logits
        if h == 0:
            row = lax.broadcasted_iota(jnp.int32, logits.shape, 0)
            col = lax.broadcasted_iota(jnp.int32, logits.shape, 1)
            match = jnp.logical_and(row == col, col < ROWS)
            signed = jnp.where(match, -logits, logits)
        small = jnp.exp(-jnp.abs(logits))
        loss = jnp.maximum(signed, 0.0) + jnp.log1p(small)
        errors = jnp.where(logits >= 0.0, 1.0, small) / (1.0 + small)
        if h == 0:
            errors = errors - match.astype(F32)
        weights = (LOSS_FACTOR * errors).astype(BF16)
        sums = (loss, LOSS_FACTOR * errors * scaled, LOSS_FACTOR * errors)
        stats.append([jnp.sum(v, axis=0, keepdims=True) for v in sums])
        wt[:, half * h : half * (h + 1)] = weights.T
        if h == 0:
            wn[...] = weights
    tgx[...] = matmul(weights, images).reshape(NZ, ROWS, E)
    got_x = [
        link.send(tgx.at[k], tgs.at[k], link.at(dc=1))
        for k in (pl.ds(3, 3), pl.ds(0, 3), pl.ds(6, 2))
    ]

    def txt_part(k):
        return tg[k] + tgs[k]

    top, low = pl.ds(0, HALF), pl.ds(HALF, HALF)
    texts = ta[...].reshape(16 * ROWS, E)
    got_low, got_top = link.group(r_low), link.group(r_top)
    for i, a in enumerate((2, 1, 3, 0)):
        grad = matmul(wt[128 * a : 128 * (a + 1), :], texts).reshape(NY, ROWS, E)
        ig_top[:, a] = grad[:, :HALF].astype(BF16)
        ig_low[a] = grad[:, HALF:].astype(BF16)
        if a:
            ig_x32[a - 1] = grad[0, :HALF]
            got_low.send(ig_low.at[a], r_low.at[a - 1], link.at(dx=a))
        else:
            ig0[...] = grad[0]
            ig_y32[...] = grad[1:, HALF:]
        if i == 0:
            tg[...] = matmul(wn[...], images).reshape(NZ, ROWS, E)
            got_x[0].wait_recv()
            first = reduce_z_start(link, txt_part, tz_sent, tz_got, HALF)
    for j in (2, 1, 3):
        got_top.send(ig_top.at[j], r_top.at[j - 1], link.at(dy=j))
    wait_all(got_x[1:])
    got_tg = reduce_z_finish(link, txt_part, tz_sent, tz_got, HALF, first)

    got_low.wait_recv()
    got_low2 = link.group(r2_low)
    for j in (2, 1, 3):
        total = ig_y32[j - 1]
        for i in range(NX - 1):
            total = total + r_low[i, j].astype(F32)
        ig2_low[j - 1] = total.astype(BF16)
        got_low2.send(ig2_low.at[j - 1], r2_low.at[j - 1], link.at(dy=j))
    got_top.wait_recv()
    got_top2 = link.group(r2_top)
    for i in (2, 1, 3):
        total = ig_x32[i - 1]
        for j in range(NY - 1):
            total = total + r_top[j, i].astype(F32)
        ig2_top[i - 1] = total.astype(BF16)
        got_top2.send(ig2_top.at[i - 1], r2_top.at[i - 1], link.at(dx=i))

    grad_txt = reduce_z_sum(txt_part, tz_got, got_tg)
    got_low2.wait_recv()
    got_top2.wait_recv()
    halves = []
    for rows, first_got, second_got in ((top, r_top, r2_top), (low, r_low, r2_low)):
        total = ig0[rows, :]
        for k in range(3):
            total = total + first_got[k, 0].astype(F32) + second_got[k].astype(F32)
        halves.append(total)
    grad_img = jnp.concatenate(halves, axis=0)
    for t, grad in enumerate((grad_img, grad_txt)):
        grad = scale * grad
        delta = inv[t, :, 0:1] * (grad - unit[t] * jnp.sum(unit[t] * grad, axis=1, keepdims=True))
        for h in range(2):
            for q in range(2):
                col = 2 * QUARTER * q + QUARTER * h
                d16[h, t, :, QUARTER * q : QUARTER * (q + 1)] = delta[:, col : col + QUARTER].astype(BF16)
        total = jnp.sum(delta, axis=0, keepdims=True)
        for k in range(9):
            bp[9 * t + k : 9 * t + k + 1, :] = total[:, 128 * k : 128 * (k + 1)]
    for k in range(3):
        lanes = stats[0][k] + stats[1][k]
        bp[18 + k : 19 + k, :] = (
            lanes[:, 0:128] + lanes[:, 128:256] + lanes[:, 256:384] + lanes[:, 384:512]
        )
    bp[21:24, :] = jnp.zeros((3, 128), F32)

    got_b = link.group(bx)
    for r in range(1, NX):
        got_b.send(bp, bx.at[r - 1], link.at(dx=r))
    got_d = []
    for h in range(2):
        got_d.append(link.group(dk.at[h, 1:]))
        for r in (0, 2, 1, 3):
            for e in range(2):
                if (r, e) == (0, 0):
                    dk[h, 0] = d16[h, c]
                    continue
                got_d[h].send(
                    d16.at[h, link.cs[e]], dk.at[h, ((NX - r) % NX) * 2 + e], link.at(dx=r, dc=e)
                )
    got_b.wait_recv()
    by[0] = bp[...] + bx[0] + bx[1] + bx[2]
    got_b = link.group(by.at[1:])
    for j in range(1, NY):
        got_b.send(by.at[0], by.at[j], link.at(dy=j))

    rows = fk[...].reshape(8 * ROWS, KX)
    got_y, deltas = [], []
    for h in range(2):
        got_d[h].wait_recv()
        half_deltas = dk[h].reshape(8 * ROWS, 2 * QUARTER)
        deltas.append(half_deltas)
        grad_w = matmul_at(rows, half_deltas)
        for j in range(NY):
            block = grad_w[SHARD * (j // 2) : SHARD * (j // 2 + 1), QUARTER * (j % 2) : QUARTER * (j % 2 + 1)]
            block = jnp.concatenate([block[:CUT], block[CUT : 2 * CUT], block[2 * CUT :]], axis=1)
            g32[h, j] = block
            gy[h, j] = block.astype(BF16)
        got_y.append(link.group(ry.at[h]))
        for j in (2, 1, 3):
            got_y[h].send(gy.at[h, link.ys[j]], ry.at[h, j - 1], link.at(dy=j))

    deltas = jnp.concatenate([d[:, QUARTER * q : QUARTER * (q + 1)] for q in range(2) for d in deltas], axis=1)
    grad_f = 0.0
    for k in range(CHUNKS):
        grad_f = grad_f + matmul_bt(deltas[:, COLS * k : COLS * (k + 1)], wk[k].reshape(KX, COLS))
    dfs[...] = grad_f.astype(BF16).reshape(8, ROWS, KX)
    got_df = link.group(dfs.at[1:])
    for r in range(NX):
        for e in range(2):
            if (r, e) == (0, 0):
                rf[0, x] = dfs[0]
                continue
            got_df.send(dfs.at[r * 2 + e], rf.at[e, x], link.at(dx=r, dc=e))

    got_b.wait_recv()
    bz[0] = by[0] + by[1] + by[2] + by[3]
    interleave(gather_z(link, bz, None, lambda k: None))
    bias_sum = bz[0]
    for k in range(1, NZ):
        bias_sum = bias_sum + bz[k]
    bs[0] = bias_sum
    got_b = link.send(bs.at[0], bs.at[1], link.at(dc=1))

    for h in range(2):
        got_y[h].wait_recv()
        total = g32[h, y]
        for j in range(NY - 1):
            total = total + ry[h, j].astype(F32)
        for k in range(NZ // 2):
            for e in range(2):
                col = 72 * k + 36 * e
                block = [total[:, QUARTER * i + col : QUARTER * i + col + 36] for i in range(3)]
                gz32[NZ // 2 * h + k, e] = jnp.concatenate(block, axis=1)

    def head_part(k):
        return gz32[link.zs[k]]

    first = reduce_z_start(link, head_part, gz_sent, gz_got, 1)
    got_own = link.send(gz32.at[z, link.cs[1]], gz_own, link.at(dc=1))
    last = reduce_z_finish(link, head_part, gz_sent, gz_got, 1, first, over_cores=True)
    got_own.wait_recv()
    wait_all(last)
    for e, total in enumerate((gz32[z, c], gz_own[...])):
        for i in range(4):
            total = total + gz_got[3 + i, e].astype(F32)
        ow[e] = total
    got_b.wait_recv()
    o_sums[...] = bs[0] + bs[1]
    got_df.wait_recv()

    for copy in link.started:
        copy.wait_send()


def finish(rf, ow, sums, o_loss, o_scale, o_fi, o_ft, o_wi, o_wt, o_bias):
    c = lax.axis_index("dp") % 2
    for t, (out_f, out_w) in enumerate(((o_fi, o_wi), (o_ft, o_wt))):
        e = jnp.where(c == t, 0, 1)
        for k in range(NX):
            out_f[:, KX * k : KX * (k + 1)] = rf[e, k]
        for k in range(3):
            out_w[:, CUT * k : CUT * (k + 1)] = ow[e][:, 36 * k : 36 * (k + 1)].T
        for k in range(9):
            o_bias[t : t + 1, 128 * k : 128 * (k + 1)] = sums[9 * t + k : 9 * t + k + 1, :]
    o_loss[0] = jnp.sum(sums[18:19, :]) * (1.0 / 8192.0)
    o_scale[0] = jnp.sum(sums[19:20, :])
    o_scale[1] = jnp.sum(sums[20:21, :])


def per_device(f_img, f_txt, w_img, w_txt, b_img, b_txt, log_scale, logit_bias):
    vmem = pl.BlockSpec(memory_space=pltpu.VMEM)
    smem = pl.BlockSpec(memory_space=pltpu.SMEM)
    scratch = [
        ((2, ROWS, D), BF16),
        ((2, NX, ROWS, KX), BF16),
        ((8, ROWS, KX), BF16),
        ((CHUNKS, 2, SHARD, COLS), BF16),
        ((CHUNKS, ROWS, COLS), F32),
        ((CHUNKS, 6, ROWS, COLS), BF16),
        ((CHUNKS, 2, ROWS, COLS), F32),
        ((CHUNKS, 2, NX - 1, ROWS, COLS), BF16),
        ((2, ROWS, E), F32),
        ((2, ROWS, 128), F32),
        ((NX, NY, ROWS, E), BF16),
        ((2, NZ, ROWS, E), BF16),
        ((512, 512), BF16),
        ((256, 512), BF16),
        ((NZ, ROWS, E), F32),
        ((NZ, ROWS, E), F32),
        ((NZ, ROWS, E), F32),
        ((7, ROWS, E), BF16),
        ((7, ROWS, E), BF16),
        ((ROWS, E), F32),
        ((NX - 1, HALF, E), F32),
        ((NY - 1, HALF, E), F32),
        ((NY, NX, HALF, E), BF16),
        ((NX, NY, HALF, E), BF16),
        ((NY - 1, NX, HALF, E), BF16),
        ((NX - 1, NY, HALF, E), BF16),
        ((NX - 1, HALF, E), BF16),
        ((NY - 1, HALF, E), BF16),
        ((NX - 1, HALF, E), BF16),
        ((NY - 1, HALF, E), BF16),
        ((2, 2, ROWS, 2 * QUARTER), BF16),
        ((2, 8, ROWS, 2 * QUARTER), BF16),
        ((24, 128), F32),
        ((3, 24, 128), F32),
        ((4, 24, 128), F32),
        ((8, 24, 128), F32),
        ((2, 24, 128), F32),
        ((8, ROWS, KX), BF16),
        ((2, NY, CUT, 3 * QUARTER), F32),
        ((2, NY, CUT, 3 * QUARTER), BF16),
        ((2, NY - 1, CUT, 3 * QUARTER), BF16),
        ((NZ, 2, CUT, 108), F32),
        ((7, 2, CUT, 108), BF16),
        ((7, 2, CUT, 108), BF16),
        ((CUT, 108), F32),
    ]
    parts = pl.pallas_call(
        kernel,
        out_shape=(
            jax.ShapeDtypeStruct((2, NX, ROWS, KX), BF16),
            jax.ShapeDtypeStruct((2, CUT, 108), F32),
            jax.ShapeDtypeStruct((24, 128), F32),
        ),
        in_specs=[pl.BlockSpec(memory_space=pl.ANY)] * 4 + [vmem] * 4,
        out_specs=(vmem, vmem, vmem),
        scratch_shapes=[pltpu.VMEM(shape, dtype) for shape, dtype in scratch]
        + [pltpu.SemaphoreType.DMA((N_GROUPS,))] * 2
        + [pltpu.SemaphoreType.DMA((3,))],
        compiler_params=pltpu.CompilerParams(
            collective_id=0, has_side_effects=True, vmem_limit_bytes=56 * 2**20
        ),
    )(f_img, f_txt, w_img, w_txt, b_img, b_txt, log_scale, logit_bias)
    loss, scale, fi, ft, wi, wt, bias = pl.pallas_call(
        finish,
        out_shape=(
            jax.ShapeDtypeStruct((1,), F32),
            jax.ShapeDtypeStruct((2,), F32),
            jax.ShapeDtypeStruct((ROWS, D), BF16),
            jax.ShapeDtypeStruct((ROWS, D), BF16),
            jax.ShapeDtypeStruct((36, SHARD), F32),
            jax.ShapeDtypeStruct((36, SHARD), F32),
            jax.ShapeDtypeStruct((2, E), F32),
        ),
        in_specs=[vmem] * 3,
        out_specs=(smem, smem, vmem, vmem, vmem, vmem, vmem),
    )(*parts)
    return loss, scale, fi, ft, wi.T, wt.T, bias


def solution(mesh):
    rows = P(("dp", "mp"), None)
    return jax.shard_map(
        per_device,
        mesh=mesh,
        in_specs=(rows, rows, P("mp", None), P("mp", None), P(), P(), P(), P()),
        out_specs=(P(), P(), rows, rows, P("mp", "dp"), P("mp", "dp"), P()),
        check_vma=False,
    )
```

```python
import functools

import jax
import jax.numpy as jnp
from jax import lax
from jax.experimental import pallas as pl
from jax.experimental.pallas import tpu as pltpu
from jax.sharding import PartitionSpec as P

EPSILON = 1e-06
LOSS_FACTOR = 32.0
NX, NY, NZ = 4, 4, 8
ROWS = 32
HALF = ROWS // 2
D = 1152
E = 1152
SHARD = 144
KX = 2 * SHARD
CHUNKS = 3
COLS = E // CHUNKS
CUT = SHARD // 3
QUARTER = E // 4
MESH = pl.DeviceIdType.MESH
F32 = jnp.float32
BF16 = jnp.bfloat16

N_GROUPS = 65


def ring(place, size):
    steps = [place + k for k in range(size)]
    return [place] + [jnp.where(v >= size, v - size, v) for v in steps[1:]]


class Links:
    def __init__(self, send_sems, recv_sems):
        dp, mp = lax.axis_index("dp"), lax.axis_index("mp")
        self.x, self.y = mp // 2, (mp % 2) * 2 + dp // 16
        self.z, self.c = (dp // 2) % NZ, dp % 2
        self.send_sems, self.recv_sems = send_sems, recv_sems
        self.started = []
        self.xs = ring(self.x, NX)
        self.ys = ring(self.y, NY)
        self.zs = ring(self.z, NZ)
        self.cs = ring(self.c, 2)
        self.x_mp = [2 * v for v in self.xs]
        self.y_mp = [v // 2 for v in self.ys]
        self.y_dp = [(v - 2 * h) * 16 for v, h in zip(self.ys, self.y_mp)]
        self.z_dp = [2 * v for v in self.zs]

    def at(self, dx=0, dy=0, dz=0, dc=0, core=None):
        core = self.cs[dc] if core is None else core
        return (self.y_dp[dy] + self.z_dp[dz] + core, self.x_mp[dx] + self.y_mp[dy])

    def group(self, region):
        copies = Group(self, len(self.started), region)
        self.started.append(copies)
        return copies

    def send(self, src, dst, device):
        copies = self.group(dst)
        copies.send(src, dst, device)
        return copies


class Group:
    def __init__(self, link, k, region):
        self.link, self.region = link, region
        self.sems = (link.send_sems.at[k], link.recv_sems.at[k])

    def copy(self, src, dst, device):
        return pltpu.make_async_remote_copy(
            src_ref=src,
            dst_ref=dst,
            send_sem=self.sems[0],
            recv_sem=self.sems[1],
            device_id=device,
            device_id_type=MESH,
        )

    def send(self, src, dst, device):
        self.copy(src, dst, device).start()

    def wait_recv(self):
        self.copy(self.region, self.region, self.link.at(dc=1)).wait_recv()

    def wait_send(self):
        self.copy(self.region, self.region, self.link.at(dc=1)).wait_send()


def matmul(a, b):
    return lax.dot_general(a, b, (((1,), (0,)), ((), ())), preferred_element_type=F32)


def matmul_bt(a, b):
    return lax.dot_general(a, b, (((1,), (1,)), ((), ())), preferred_element_type=F32)


def matmul_at(a, b):
    return lax.dot_general(a, b, (((0,), (0,)), ((), ())), preferred_element_type=F32)


def wait_all(copies):
    for copy in copies:
        copy.wait_recv()


def gather_z(link, buf, split, on_arrival):
    to_6 = link.send(buf.at[0], buf.at[6], link.at(dz=2))
    to_2 = link.send(buf.at[0], buf.at[2], link.at(dz=6))
    to_7 = link.send(buf.at[0], buf.at[7], link.at(dz=1))
    to_1 = link.send(buf.at[0], buf.at[1], link.at(dz=7))
    yield
    to_6.wait_recv()
    to_5 = link.send(buf.at[6], buf.at[5], link.at(dz=1))
    if split is None:
        to_4 = [link.send(buf.at[6], buf.at[4], link.at(dz=2))]
    else:
        to_4 = [link.send(buf.at[6, :split], buf.at[4, :split], link.at(dz=2))]
    on_arrival(6)
    yield
    to_2.wait_recv()
    to_3 = link.send(buf.at[2], buf.at[3], link.at(dz=7))
    if split is not None:
        to_4.append(link.send(buf.at[2, split:], buf.at[4, split:], link.at(dz=6)))
    on_arrival(2)
    yield
    to_7.wait_recv()
    on_arrival(7)
    yield
    to_1.wait_recv()
    on_arrival(1)
    yield
    to_5.wait_recv()
    on_arrival(5)
    to_3.wait_recv()
    on_arrival(3)
    wait_all(to_4)
    on_arrival(4)


def gather_plane(link, buf):
    steps = (1, 3, 2)
    top, low = pl.ds(0, HALF), pl.ds(HALF, HALF)
    got = link.group(buf.at[1:, 1:])
    got_x = [link.send(buf.at[0, 0], buf.at[NX - i, 0], link.at(dx=i)) for i in steps]
    got_y = [link.send(buf.at[0, 0], buf.at[0, NY - j], link.at(dy=j)) for j in steps]
    yield
    for copy_x, copy_y, k in zip(got_x, got_y, steps):
        a = NX - k
        copy_x.wait_recv()
        for j in steps:
            got.send(buf.at[a, 0, top], buf.at[a, NY - j, top], link.at(dy=j))
        copy_y.wait_recv()
        for i in steps:
            got.send(buf.at[0, a, low], buf.at[NX - i, a, low], link.at(dx=i))
        yield
    got.wait_recv()


def interleave(*parts):
    parts = list(parts)
    while parts:
        for part in list(parts):
            try:
                next(part)
            except StopIteration:
                parts.remove(part)


def reduce_z_start(link, part, sent, got, split):
    for i, k in enumerate((4, 3, 5)):
        sent[i] = part(k).astype(BF16)
    return [
        link.send(sent.at[0, :split], got.at[0, :split], link.at(dz=2)),
        link.send(sent.at[0, split:], got.at[0, split:], link.at(dz=6)),
        link.send(sent.at[1], got.at[1], link.at(dz=1)),
        link.send(sent.at[2], got.at[2], link.at(dz=7)),
    ]


def reduce_z_finish(link, part, sent, got, split, first, over_cores=False):
    def onward(i, k):
        if not over_cores:
            return link.send(sent.at[i], got.at[i], link.at(dz=k))
        copies = link.group(got.at[i])
        for e in range(2):
            copies.send(sent.at[i, link.cs[e]], got.at[i, e], link.at(dz=k, dc=e))
        return copies

    last = []
    for i, k in ((3, 1), (4, 7)):
        sent[i] = part(k).astype(BF16)
        last.append(onward(i, k))
    first[0].wait_recv()
    first[2].wait_recv()
    term = part(2) + got[1].astype(F32)
    sent[5, :split] = (term[:split] + got[0, :split].astype(F32)).astype(BF16)
    sent[5, split:] = term[split:].astype(BF16)
    last.append(onward(5, 2))
    first[1].wait_recv()
    first[3].wait_recv()
    term = part(6) + got[2].astype(F32)
    sent[6, :split] = term[:split].astype(BF16)
    sent[6, split:] = (term[split:] + got[0, split:].astype(F32)).astype(BF16)
    last.append(onward(6, 6))
    return last


def reduce_z_sum(part, got, last):
    total = part(0)
    for k, copy in enumerate(last):
        copy.wait_recv()
        total = total + got[3 + k].astype(F32)
    return total


def kernel(
    f_img, f_txt, w_img, w_txt, b_img, b_txt, log_scale, logit_bias,
    rf, ow, o_sums,
    fv, bv_img, bv_txt, fs, fk, wk, po, pk, rp0, rp, unit, inv, ia, ta, wt, wn, tg, tgx, tgs, tz_sent, tz_got,
    ig0, ig_x32, ig_y32, ig_top, ig_low, r_top, r_low, ig2_top, ig2_low, r2_top, r2_low,
    d16, dk, bp, bx, by, bz, bs, dfs, g32, gy, ry, gz32, gz_sent, gz_got, gz_own,
    send_sems, recv_sems, load_sems, scalars,
):
    link = Links(send_sems, recv_sems)
    x, y, z, c = link.x, link.y, link.z, link.c

    shard = link.y_mp[0]
    for t, head in enumerate((w_img, w_txt)):

        @pl.when(c == t)
        def _():
            for k in range(CHUNKS):
                cols = pl.ds(COLS * k, COLS)
                pltpu.make_async_copy(head.at[:, cols], wk.at[k, shard], load_sems.at[0]).start()

    loads = [
        pltpu.make_async_copy(f, fv.at[t], load_sems.at[1 + t]) for t, f in enumerate((f_img, f_txt))
    ]
    small = ((log_scale, scalars.at[0]), (logit_bias, scalars.at[1]), (b_img, bv_img), (b_txt, bv_txt))
    small_loads = [
        pltpu.make_async_copy(v, place, load_sems.at[3 + k]) for k, (v, place) in enumerate(small)
    ]
    loads += small_loads
    for load in loads:
        load.start()

    peers = [(0, 0, 0, 1)]
    peers += [(i, 0, 0, e) for i in range(1, NX) for e in range(2)]
    peers += [(0, j, 0, 0) for j in range(1, NY)]
    peers += [(0, 0, k, e) for k in (1, 2, 6, 7) for e in range(2)]
    barrier = pltpu.get_barrier_semaphore()
    for p in peers:
        pl.semaphore_signal(barrier, inc=1, device_id=link.at(*p), device_id_type=MESH)

    for t in range(2):
        loads[t].wait()
        for k in range(NX):
            fs[t, k] = fv[t, :, KX * k : KX * (k + 1)]
    own_head = wk.at[:, shard]
    pltpu.make_async_copy(own_head, own_head, load_sems.at[0]).wait()
    for load in small_loads:
        load.wait()
    pl.semaphore_wait(barrier, len(peers))

    odd = y - 2 * shard
    ahead, behind = link.at(dy=1), link.at(dy=3)
    partner = tuple(jnp.where(odd == 1, u, v) for u, v in zip(ahead, behind))
    got_f = link.group(fk.at[1:])
    for r in range(NX):
        for e in range(2):
            if (r, e) == (0, 0):
                fk[0] = fs[c, x]
                continue
            got_f.send(
                fs.at[link.cs[e], link.xs[r]],
                fk.at[((NX - r) % NX) * 2 + e],
                link.at(dx=r, dc=e),
            )
    got_w = [link.send(wk.at[k, shard], wk.at[k, shard], partner) for k in range(CHUNKS)]
    got_f.wait_recv()

    rows = fk[...].reshape(8 * ROWS, KX)
    got_p = []
    for k in range(CHUNKS):
        got_w[k].wait_recv()
        part = matmul(rows, wk[k].reshape(KX, COLS))
        rp0[k, 0] = part[:ROWS]
        po[k] = part[ROWS : 2 * ROWS]
        pk[k] = part[2 * ROWS :].astype(BF16).reshape(6, ROWS, COLS)
        got = link.group(rp.at[k])
        got_p.append([link.send(po.at[k], rp0.at[k, 1], link.at(dc=1)), got])
        for r in (2, 1, 3):
            for e in range(2):
                got.send(pk.at[k, (r - 1) * 2 + e], rp.at[k, e, NX - r - 1], link.at(dx=r, dc=e))
    squares = [0.0, 0.0]
    for k in range(CHUNKS):
        wait_all(got_p[k])
        cols = slice(COLS * k, COLS * (k + 1))
        for t, bias in enumerate((bv_img, bv_txt)):
            e = link.cs[t]
            pre = rp0[k, e] + bias[cols].reshape(1, COLS)
            for r in range(NX - 1):
                pre = pre + rp[k, e, r].astype(F32)
            unit[t, :, cols] = pre
            squares[t] = squares[t] + jnp.sum(pre * pre, axis=1, keepdims=True)
    for t in range(2):
        inverse = lax.rsqrt(squares[t] + EPSILON)
        unit[t] = unit[t] * inverse
        inv[t] = jnp.broadcast_to(inverse, (ROWS, 128))
    ia[0, 0] = unit[0].astype(BF16)
    ta[0, 0] = unit[1].astype(BF16)

    got_s = link.group(ta.at[1])
    got_s.send(ta.at[0, 0], ta.at[1, 0], link.at(dc=1))

    def forward(k):
        got_s.send(ta.at[0, k], ta.at[1, k], link.at(dc=1))

    interleave(gather_z(link, ta.at[0], HALF, forward), gather_plane(link, ia))

    half = NZ * ROWS
    scale = jnp.exp(jnp.full((1, 1), scalars[0, 0], F32))
    shift = scalars[1, 0]
    images = ia[...].reshape(16 * ROWS, E)
    stats = []
    for h in range(2):
        if h == 1:
            got_s.wait_recv()
        texts = ta[h].reshape(half, E)
        scaled = scale * matmul_bt(texts, images)
        logits = scaled + shift
        signed = logits
        if h == 0:
            row = lax.broadcasted_iota(jnp.int32, logits.shape, 0)
            col = lax.broadcasted_iota(jnp.int32, logits.shape, 1)
            match = jnp.logical_and(row == col, col < ROWS)
            signed = jnp.where(match, -logits, logits)
        small = jnp.exp(-jnp.abs(logits))
        loss = jnp.maximum(signed, 0.0) + jnp.log1p(small)
        errors = jnp.where(logits >= 0.0, 1.0, small) / (1.0 + small)
        if h == 0:
            errors = errors - match.astype(F32)
        weights = (LOSS_FACTOR * errors).astype(BF16)
        sums = (loss, LOSS_FACTOR * errors * scaled, LOSS_FACTOR * errors)
        stats.append([jnp.sum(v, axis=0, keepdims=True) for v in sums])
        wt[:, half * h : half * (h + 1)] = weights.T
        if h == 0:
            wn[...] = weights
    tgx[...] = matmul(weights, images).reshape(NZ, ROWS, E)
    got_x = [
        link.send(tgx.at[k], tgs.at[k], link.at(dc=1))
        for k in (pl.ds(3, 3), pl.ds(0, 3), pl.ds(6, 2))
    ]

    def txt_part(k):
        return tg[k] + tgs[k]

    top, low = pl.ds(0, HALF), pl.ds(HALF, HALF)
    texts = ta[...].reshape(16 * ROWS, E)
    got_low, got_top = link.group(r_low), link.group(r_top)
    for i, a in enumerate((2, 1, 3, 0)):
        grad = matmul(wt[128 * a : 128 * (a + 1), :], texts).reshape(NY, ROWS, E)
        ig_top[:, a] = grad[:, :HALF].astype(BF16)
        ig_low[a] = grad[:, HALF:].astype(BF16)
        if a:
            ig_x32[a - 1] = grad[0, :HALF]
            got_low.send(ig_low.at[a], r_low.at[a - 1], link.at(dx=a))
        else:
            ig0[...] = grad[0]
            ig_y32[...] = grad[1:, HALF:]
        if i == 0:
            tg[...] = matmul(wn[...], images).reshape(NZ, ROWS, E)
            got_x[0].wait_recv()
            first = reduce_z_start(link, txt_part, tz_sent, tz_got, HALF)
    for j in (2, 1, 3):
        got_top.send(ig_top.at[j], r_top.at[j - 1], link.at(dy=j))
    wait_all(got_x[1:])
    got_tg = reduce_z_finish(link, txt_part, tz_sent, tz_got, HALF, first)

    got_low.wait_recv()
    got_low2 = link.group(r2_low)
    for j in (2, 1, 3):
        total = ig_y32[j - 1]
        for i in range(NX - 1):
            total = total + r_low[i, j].astype(F32)
        ig2_low[j - 1] = total.astype(BF16)
        got_low2.send(ig2_low.at[j - 1], r2_low.at[j - 1], link.at(dy=j))
    got_top.wait_recv()
    got_top2 = link.group(r2_top)
    for i in (2, 1, 3):
        total = ig_x32[i - 1]
        for j in range(NY - 1):
            total = total + r_top[j, i].astype(F32)
        ig2_top[i - 1] = total.astype(BF16)
        got_top2.send(ig2_top.at[i - 1], r2_top.at[i - 1], link.at(dx=i))

    got_b = link.group(bx)
    got_d = [link.group(dk.at[h, 1:]) for h in range(2)]

    def norm_backward(t, grad):
        grad = scale * grad
        delta = inv[t, :, 0:1] * (grad - unit[t] * jnp.sum(unit[t] * grad, axis=1, keepdims=True))
        for h in range(2):
            for q in range(2):
                col = 2 * QUARTER * q + QUARTER * h
                d16[h, t, :, QUARTER * q : QUARTER * (q + 1)] = delta[:, col : col + QUARTER].astype(BF16)
        total = jnp.sum(delta, axis=0, keepdims=True)
        for k in range(9):
            bp[9 * t + k : 9 * t + k + 1, :] = total[:, 128 * k : 128 * (k + 1)]

    def send_deltas(t):
        for h in range(2):
            for r in (2, 1, 3):
                slot = (NX - r) * 2 + link.cs[t]
                got_d[h].send(d16.at[h, t], dk.at[h, slot], link.at(dx=r, core=t))

            @pl.when(c == t)
            def _():
                dk[h, 0] = d16[h, t]

            @pl.when(c != t)
            def _():
                got_d[h].send(d16.at[h, t], dk.at[h, 1], link.at(dc=1))

    norm_backward(1, reduce_z_sum(txt_part, tz_got, got_tg))
    send_deltas(1)
    got_low2.wait_recv()
    got_top2.wait_recv()
    halves = []
    for rows, first_got, second_got in ((top, r_top, r2_top), (low, r_low, r2_low)):
        total = ig0[rows, :]
        for k in range(3):
            total = total + first_got[k, 0].astype(F32) + second_got[k].astype(F32)
        halves.append(total)
    norm_backward(0, jnp.concatenate(halves, axis=0))
    for k in range(3):
        lanes = stats[0][k] + stats[1][k]
        bp[18 + k : 19 + k, :] = (
            lanes[:, 0:128] + lanes[:, 128:256] + lanes[:, 256:384] + lanes[:, 384:512]
        )
    bp[21:24, :] = jnp.zeros((3, 128), F32)
    for r in range(1, NX):
        got_b.send(bp, bx.at[r - 1], link.at(dx=r))
    send_deltas(0)
    got_b.wait_recv()
    by[0] = bp[...] + bx[0] + bx[1] + bx[2]
    got_b = link.group(by.at[1:])
    for j in range(1, NY):
        got_b.send(by.at[0], by.at[j], link.at(dy=j))

    rows = fk[...].reshape(8 * ROWS, KX)
    got_y, deltas = [], []
    for h in range(2):
        got_d[h].wait_recv()
        half_deltas = dk[h].reshape(8 * ROWS, 2 * QUARTER)
        deltas.append(half_deltas)
        grad_w = matmul_at(rows, half_deltas)
        for j in range(NY):
            block = grad_w[SHARD * (j // 2) : SHARD * (j // 2 + 1), QUARTER * (j % 2) : QUARTER * (j % 2 + 1)]
            block = jnp.concatenate([block[:CUT], block[CUT : 2 * CUT], block[2 * CUT :]], axis=1)
            g32[h, j] = block
            gy[h, j] = block.astype(BF16)
        got_y.append(link.group(ry.at[h]))
        for j in (2, 1, 3):
            got_y[h].send(gy.at[h, link.ys[j]], ry.at[h, j - 1], link.at(dy=j))

    deltas = jnp.concatenate([d[:, QUARTER * q : QUARTER * (q + 1)] for q in range(2) for d in deltas], axis=1)
    grad_f = 0.0
    for k in range(CHUNKS):
        grad_f = grad_f + matmul_bt(deltas[:, COLS * k : COLS * (k + 1)], wk[k].reshape(KX, COLS))
    dfs[...] = grad_f.astype(BF16).reshape(8, ROWS, KX)
    got_df = link.group(dfs.at[1:])
    for r in range(NX):
        for e in range(2):
            if (r, e) == (0, 0):
                rf[0, x] = dfs[0]
                continue
            got_df.send(dfs.at[r * 2 + e], rf.at[e, x], link.at(dx=r, dc=e))

    got_b.wait_recv()
    bz[0] = by[0] + by[1] + by[2] + by[3]
    interleave(gather_z(link, bz, None, lambda k: None))
    bias_sum = bz[0]
    for k in range(1, NZ):
        bias_sum = bias_sum + bz[k]
    bs[0] = bias_sum
    got_b = link.send(bs.at[0], bs.at[1], link.at(dc=1))

    for h in range(2):
        got_y[h].wait_recv()
        total = g32[h, y]
        for j in range(NY - 1):
            total = total + ry[h, j].astype(F32)
        for k in range(NZ // 2):
            for e in range(2):
                col = 72 * k + 36 * e
                block = [total[:, QUARTER * i + col : QUARTER * i + col + 36] for i in range(3)]
                gz32[NZ // 2 * h + k, e] = jnp.concatenate(block, axis=1)

    def head_part(k):
        return gz32[link.zs[k]]

    first = reduce_z_start(link, head_part, gz_sent, gz_got, 1)
    got_own = link.send(gz32.at[z, link.cs[1]], gz_own, link.at(dc=1))
    last = reduce_z_finish(link, head_part, gz_sent, gz_got, 1, first, over_cores=True)
    got_own.wait_recv()
    wait_all(last)
    for e, total in enumerate((gz32[z, c], gz_own[...])):
        for i in range(4):
            total = total + gz_got[3 + i, e].astype(F32)
        ow[e] = total
    got_b.wait_recv()
    o_sums[...] = bs[0] + bs[1]
    got_df.wait_recv()

    for copy in link.started:
        copy.wait_send()


def finish(rf, ow, sums, o_loss, o_scale, o_fi, o_ft, o_wi, o_wt, o_bias):
    c = lax.axis_index("dp") % 2
    for t, (out_f, out_w) in enumerate(((o_fi, o_wi), (o_ft, o_wt))):
        e = jnp.where(c == t, 0, 1)
        for k in range(NX):
            out_f[:, KX * k : KX * (k + 1)] = rf[e, k]
        for k in range(3):
            out_w[:, CUT * k : CUT * (k + 1)] = ow[e][:, 36 * k : 36 * (k + 1)].T
        for k in range(9):
            o_bias[t : t + 1, 128 * k : 128 * (k + 1)] = sums[9 * t + k : 9 * t + k + 1, :]
    o_loss[0] = jnp.sum(sums[18:19, :]) * (1.0 / 8192.0)
    o_scale[0] = jnp.sum(sums[19:20, :])
    o_scale[1] = jnp.sum(sums[20:21, :])


def per_device(f_img, f_txt, w_img, w_txt, b_img, b_txt, log_scale, logit_bias):
    hbm = pl.BlockSpec(memory_space=pl.ANY)
    vmem = pl.BlockSpec(memory_space=pltpu.VMEM)
    smem = pl.BlockSpec(memory_space=pltpu.SMEM)
    scratch = [
        ((2, ROWS, D), BF16),
        ((E,), F32),
        ((E,), F32),
        ((2, NX, ROWS, KX), BF16),
        ((8, ROWS, KX), BF16),
        ((CHUNKS, 2, SHARD, COLS), BF16),
        ((CHUNKS, ROWS, COLS), F32),
        ((CHUNKS, 6, ROWS, COLS), BF16),
        ((CHUNKS, 2, ROWS, COLS), F32),
        ((CHUNKS, 2, NX - 1, ROWS, COLS), BF16),
        ((2, ROWS, E), F32),
        ((2, ROWS, 128), F32),
        ((NX, NY, ROWS, E), BF16),
        ((2, NZ, ROWS, E), BF16),
        ((512, 512), BF16),
        ((256, 512), BF16),
        ((NZ, ROWS, E), F32),
        ((NZ, ROWS, E), F32),
        ((NZ, ROWS, E), F32),
        ((7, ROWS, E), BF16),
        ((7, ROWS, E), BF16),
        ((ROWS, E), F32),
        ((NX - 1, HALF, E), F32),
        ((NY - 1, HALF, E), F32),
        ((NY, NX, HALF, E), BF16),
        ((NX, NY, HALF, E), BF16),
        ((NY - 1, NX, HALF, E), BF16),
        ((NX - 1, NY, HALF, E), BF16),
        ((NX - 1, HALF, E), BF16),
        ((NY - 1, HALF, E), BF16),
        ((NX - 1, HALF, E), BF16),
        ((NY - 1, HALF, E), BF16),
        ((2, 2, ROWS, 2 * QUARTER), BF16),
        ((2, 8, ROWS, 2 * QUARTER), BF16),
        ((24, 128), F32),
        ((3, 24, 128), F32),
        ((4, 24, 128), F32),
        ((8, 24, 128), F32),
        ((2, 24, 128), F32),
        ((8, ROWS, KX), BF16),
        ((2, NY, CUT, 3 * QUARTER), F32),
        ((2, NY, CUT, 3 * QUARTER), BF16),
        ((2, NY - 1, CUT, 3 * QUARTER), BF16),
        ((NZ, 2, CUT, 108), F32),
        ((7, 2, CUT, 108), BF16),
        ((7, 2, CUT, 108), BF16),
        ((CUT, 108), F32),
    ]
    parts = pl.pallas_call(
        kernel,
        out_shape=(
            jax.ShapeDtypeStruct((2, NX, ROWS, KX), BF16),
            jax.ShapeDtypeStruct((2, CUT, 108), F32),
            jax.ShapeDtypeStruct((24, 128), F32),
        ),
        in_specs=[hbm] * 8,
        out_specs=(vmem, vmem, vmem),
        scratch_shapes=[pltpu.VMEM(shape, dtype) for shape, dtype in scratch]
        + [pltpu.SemaphoreType.DMA((N_GROUPS,))] * 2
        + [pltpu.SemaphoreType.DMA((7,)), pltpu.SMEM((2, 1), F32)],
        compiler_params=pltpu.CompilerParams(
            collective_id=0, has_side_effects=True, vmem_limit_bytes=56 * 2**20
        ),
    )(f_img, f_txt, w_img, w_txt, b_img, b_txt, log_scale, logit_bias)
    loss, scale, fi, ft, wi, wt, bias = pl.pallas_call(
        finish,
        out_shape=(
            jax.ShapeDtypeStruct((1,), F32),
            jax.ShapeDtypeStruct((2,), F32),
            jax.ShapeDtypeStruct((ROWS, D), BF16),
            jax.ShapeDtypeStruct((ROWS, D), BF16),
            jax.ShapeDtypeStruct((36, SHARD), F32),
            jax.ShapeDtypeStruct((36, SHARD), F32),
            jax.ShapeDtypeStruct((2, E), F32),
        ),
        in_specs=[vmem] * 3,
        out_specs=(smem, smem, vmem, vmem, vmem, vmem, vmem),
    )(*parts)
    return loss, scale, fi, ft, wi.T, wt.T, bias


def solution(mesh):
    rows = P(("dp", "mp"), None)
    return jax.shard_map(
        per_device,
        mesh=mesh,
        in_specs=(rows, rows, P("mp", None), P("mp", None), P(), P(), P(), P()),
        out_specs=(P(), P(), rows, rows, P("mp", "dp"), P("mp", "dp"), P()),
        check_vma=False,
    )
```

```python
import functools

import jax
import jax.numpy as jnp
from jax import lax
from jax.experimental import pallas as pl
from jax.experimental.pallas import tpu as pltpu
from jax.sharding import PartitionSpec as P

EPSILON = 1e-06
LOSS_FACTOR = 32.0
NX, NY, NZ = 4, 4, 8
ROWS = 32
HALF = ROWS // 2
D = 1152
E = 1152
SHARD = 144
KX = 2 * SHARD
CHUNKS = 3
COLS = E // CHUNKS
CUT = SHARD // 3
QUARTER = E // 4
MESH = pl.DeviceIdType.MESH
F32 = jnp.float32
BF16 = jnp.bfloat16

N_GROUPS = 65


def ring(place, size):
    steps = [place + k for k in range(size)]
    return [place] + [jnp.where(v >= size, v - size, v) for v in steps[1:]]


class Links:
    def __init__(self, send_sems, recv_sems):
        dp, mp = lax.axis_index("dp"), lax.axis_index("mp")
        self.x, self.y = mp // 2, (mp % 2) * 2 + dp // 16
        self.z, self.c = (dp // 2) % NZ, dp % 2
        self.send_sems, self.recv_sems = send_sems, recv_sems
        self.started = []
        self.xs = ring(self.x, NX)
        self.ys = ring(self.y, NY)
        self.zs = ring(self.z, NZ)
        self.cs = ring(self.c, 2)
        self.x_mp = [2 * v for v in self.xs]
        self.y_mp = [v // 2 for v in self.ys]
        self.y_dp = [(v - 2 * h) * 16 for v, h in zip(self.ys, self.y_mp)]
        self.z_dp = [2 * v for v in self.zs]

    def at(self, dx=0, dy=0, dz=0, dc=0, core=None):
        core = self.cs[dc] if core is None else core
        return (self.y_dp[dy] + self.z_dp[dz] + core, self.x_mp[dx] + self.y_mp[dy])

    def group(self, region):
        copies = Group(self, len(self.started), region)
        self.started.append(copies)
        return copies

    def send(self, src, dst, device):
        copies = self.group(dst)
        copies.send(src, dst, device)
        return copies


class Group:
    def __init__(self, link, k, region):
        self.link, self.region = link, region
        self.sems = (link.send_sems.at[k], link.recv_sems.at[k])

    def copy(self, src, dst, device):
        return pltpu.make_async_remote_copy(
            src_ref=src,
            dst_ref=dst,
            send_sem=self.sems[0],
            recv_sem=self.sems[1],
            device_id=device,
            device_id_type=MESH,
        )

    def send(self, src, dst, device):
        self.copy(src, dst, device).start()

    def wait_recv(self):
        self.copy(self.region, self.region, self.link.at(dc=1)).wait_recv()

    def wait_send(self):
        self.copy(self.region, self.region, self.link.at(dc=1)).wait_send()


def matmul(a, b):
    return lax.dot_general(a, b, (((1,), (0,)), ((), ())), preferred_element_type=F32)


def matmul_bt(a, b):
    return lax.dot_general(a, b, (((1,), (1,)), ((), ())), preferred_element_type=F32)


def matmul_at(a, b):
    return lax.dot_general(a, b, (((0,), (0,)), ((), ())), preferred_element_type=F32)


def wait_all(copies):
    for copy in copies:
        copy.wait_recv()


def gather_z(link, buf, split, on_arrival):
    to_6 = link.send(buf.at[0], buf.at[6], link.at(dz=2))
    to_2 = link.send(buf.at[0], buf.at[2], link.at(dz=6))
    to_7 = link.send(buf.at[0], buf.at[7], link.at(dz=1))
    to_1 = link.send(buf.at[0], buf.at[1], link.at(dz=7))
    yield
    to_6.wait_recv()
    to_5 = link.send(buf.at[6], buf.at[5], link.at(dz=1))
    if split is None:
        to_4 = [link.send(buf.at[6], buf.at[4], link.at(dz=2))]
    else:
        to_4 = [link.send(buf.at[6, :split], buf.at[4, :split], link.at(dz=2))]
    on_arrival(6)
    yield
    to_2.wait_recv()
    to_3 = link.send(buf.at[2], buf.at[3], link.at(dz=7))
    if split is not None:
        to_4.append(link.send(buf.at[2, split:], buf.at[4, split:], link.at(dz=6)))
    on_arrival(2)
    yield
    to_7.wait_recv()
    on_arrival(7)
    yield
    to_1.wait_recv()
    on_arrival(1)
    yield
    to_5.wait_recv()
    on_arrival(5)
    to_3.wait_recv()
    on_arrival(3)
    wait_all(to_4)
    on_arrival(4)


def gather_plane(link, buf):
    steps = (1, 3, 2)
    top, low = pl.ds(0, HALF), pl.ds(HALF, HALF)
    got = link.group(buf.at[1:, 1:])
    got_x = [link.send(buf.at[0, 0], buf.at[NX - i, 0], link.at(dx=i)) for i in steps]
    got_y = [link.send(buf.at[0, 0], buf.at[0, NY - j], link.at(dy=j)) for j in steps]
    yield
    for copy_x, copy_y, k in zip(got_x, got_y, steps):
        a = NX - k
        copy_x.wait_recv()
        for j in steps:
            got.send(buf.at[a, 0, top], buf.at[a, NY - j, top], link.at(dy=j))
        copy_y.wait_recv()
        for i in steps:
            got.send(buf.at[0, a, low], buf.at[NX - i, a, low], link.at(dx=i))
        yield
    got.wait_recv()


def interleave(*parts):
    parts = list(parts)
    while parts:
        for part in list(parts):
            try:
                next(part)
            except StopIteration:
                parts.remove(part)


def reduce_z_start(link, part, sent, got, split):
    for i, k in enumerate((4, 3, 5)):
        sent[i] = part(k).astype(BF16)
    return [
        link.send(sent.at[0, :split], got.at[0, :split], link.at(dz=2)),
        link.send(sent.at[0, split:], got.at[0, split:], link.at(dz=6)),
        link.send(sent.at[1], got.at[1], link.at(dz=1)),
        link.send(sent.at[2], got.at[2], link.at(dz=7)),
    ]


def reduce_z_finish(link, part, sent, got, split, first, over_cores=False):
    def onward(i, k):
        if not over_cores:
            return link.send(sent.at[i], got.at[i], link.at(dz=k))
        copies = link.group(got.at[i])
        for e in range(2):
            copies.send(sent.at[i, link.cs[e]], got.at[i, e], link.at(dz=k, dc=e))
        return copies

    last = []
    for i, k in ((3, 1), (4, 7)):
        sent[i] = part(k).astype(BF16)
        last.append(onward(i, k))
    first[0].wait_recv()
    first[2].wait_recv()
    term = part(2) + got[1].astype(F32)
    sent[5, :split] = (term[:split] + got[0, :split].astype(F32)).astype(BF16)
    sent[5, split:] = term[split:].astype(BF16)
    last.append(onward(5, 2))
    first[1].wait_recv()
    first[3].wait_recv()
    term = part(6) + got[2].astype(F32)
    sent[6, :split] = term[:split].astype(BF16)
    sent[6, split:] = (term[split:] + got[0, split:].astype(F32)).astype(BF16)
    last.append(onward(6, 6))
    return last


def reduce_z_sum(part, got, last):
    total = part(0)
    for k, copy in enumerate(last):
        copy.wait_recv()
        total = total + got[3 + k].astype(F32)
    return total


def kernel(
    f_img, f_txt, w_img, w_txt, b_img, b_txt, log_scale, logit_bias,
    o_loss, o_scale, o_fi, o_ft, o_wi, o_wt, o_bias,
    rf, ow, fv, bv_img, bv_txt, fs, fk, wk, po, pk, rp0, rp, unit, inv, ia, ta, wt, wn, tg, tgx, tgs, tz_sent, tz_got,
    ig0, ig_x32, ig_y32, ig_top, ig_low, r_top, r_low, ig2_top, ig2_low, r2_top, r2_low,
    d16, dk, bp, bx, by, bz, bs, dfs, g32, gy, ry, gz32, gz_sent, gz_got, gz_own,
    send_sems, recv_sems, load_sems, scalars,
):
    link = Links(send_sems, recv_sems)
    x, y, z, c = link.x, link.y, link.z, link.c

    shard = link.y_mp[0]
    for t, head in enumerate((w_img, w_txt)):

        @pl.when(c == t)
        def _():
            for k in range(CHUNKS):
                cols = pl.ds(COLS * k, COLS)
                pltpu.make_async_copy(head.at[:, cols], wk.at[k, shard], load_sems.at[0]).start()

    loads = [
        pltpu.make_async_copy(f, fv.at[t], load_sems.at[1 + t]) for t, f in enumerate((f_img, f_txt))
    ]
    small = ((log_scale, scalars.at[0]), (logit_bias, scalars.at[1]), (b_img, bv_img), (b_txt, bv_txt))
    small_loads = [
        pltpu.make_async_copy(v, place, load_sems.at[3 + k]) for k, (v, place) in enumerate(small)
    ]
    loads += small_loads
    for load in loads:
        load.start()

    peers = [(0, 0, 0, 1)]
    peers += [(i, 0, 0, e) for i in range(1, NX) for e in range(2)]
    peers += [(0, j, 0, 0) for j in range(1, NY)]
    peers += [(0, 0, k, e) for k in (1, 2, 6, 7) for e in range(2)]
    barrier = pltpu.get_barrier_semaphore()
    for p in peers:
        pl.semaphore_signal(barrier, inc=1, device_id=link.at(*p), device_id_type=MESH)

    for t in range(2):
        loads[t].wait()
        for k in range(NX):
            fs[t, k] = fv[t, :, KX * k : KX * (k + 1)]
    own_head = wk.at[:, shard]
    pltpu.make_async_copy(own_head, own_head, load_sems.at[0]).wait()
    for load in small_loads:
        load.wait()
    pl.semaphore_wait(barrier, len(peers))

    odd = y - 2 * shard
    ahead, behind = link.at(dy=1), link.at(dy=3)
    partner = tuple(jnp.where(odd == 1, u, v) for u, v in zip(ahead, behind))
    got_f = link.group(fk.at[1:])
    for r in range(NX):
        for e in range(2):
            if (r, e) == (0, 0):
                fk[0] = fs[c, x]
                continue
            got_f.send(
                fs.at[link.cs[e], link.xs[r]],
                fk.at[((NX - r) % NX) * 2 + e],
                link.at(dx=r, dc=e),
            )
    got_w = [link.send(wk.at[k, shard], wk.at[k, shard], partner) for k in range(CHUNKS)]
    got_f.wait_recv()

    rows = fk[...].reshape(8 * ROWS, KX)
    got_p = []
    for k in range(CHUNKS):
        got_w[k].wait_recv()
        part = matmul(rows, wk[k].reshape(KX, COLS))
        rp0[k, 0] = part[:ROWS]
        po[k] = part[ROWS : 2 * ROWS]
        pk[k] = part[2 * ROWS :].astype(BF16).reshape(6, ROWS, COLS)
        got = link.group(rp.at[k])
        got_p.append([link.send(po.at[k], rp0.at[k, 1], link.at(dc=1)), got])
        for r in (2, 1, 3):
            for e in range(2):
                got.send(pk.at[k, (r - 1) * 2 + e], rp.at[k, e, NX - r - 1], link.at(dx=r, dc=e))
    squares = [0.0, 0.0]
    for k in range(CHUNKS):
        wait_all(got_p[k])
        cols = slice(COLS * k, COLS * (k + 1))
        for t, bias in enumerate((bv_img, bv_txt)):
            e = link.cs[t]
            pre = rp0[k, e] + bias[cols].reshape(1, COLS)
            for r in range(NX - 1):
                pre = pre + rp[k, e, r].astype(F32)
            unit[t, :, cols] = pre
            squares[t] = squares[t] + jnp.sum(pre * pre, axis=1, keepdims=True)
    for t in range(2):
        inverse = lax.rsqrt(squares[t] + EPSILON)
        unit[t] = unit[t] * inverse
        inv[t] = jnp.broadcast_to(inverse, (ROWS, 128))
    ia[0, 0] = unit[0].astype(BF16)
    ta[0, 0] = unit[1].astype(BF16)

    got_s = link.group(ta.at[1])
    got_s.send(ta.at[0, 0], ta.at[1, 0], link.at(dc=1))

    def forward(k):
        got_s.send(ta.at[0, k], ta.at[1, k], link.at(dc=1))

    interleave(gather_z(link, ta.at[0], HALF, forward), gather_plane(link, ia))

    half = NZ * ROWS
    scale = jnp.exp(jnp.full((1, 1), scalars[0, 0], F32))
    shift = scalars[1, 0]
    images = ia[...].reshape(16 * ROWS, E)
    stats = []
    for h in range(2):
        if h == 1:
            got_s.wait_recv()
        texts = ta[h].reshape(half, E)
        scaled = scale * matmul_bt(texts, images)
        logits = scaled + shift
        signed = logits
        if h == 0:
            row = lax.broadcasted_iota(jnp.int32, logits.shape, 0)
            col = lax.broadcasted_iota(jnp.int32, logits.shape, 1)
            match = jnp.logical_and(row == col, col < ROWS)
            signed = jnp.where(match, -logits, logits)
        small = jnp.exp(-jnp.abs(logits))
        loss = jnp.maximum(signed, 0.0) + jnp.log1p(small)
        errors = jnp.where(logits >= 0.0, 1.0, small) / (1.0 + small)
        if h == 0:
            errors = errors - match.astype(F32)
        weights = (LOSS_FACTOR * errors).astype(BF16)
        sums = (loss, LOSS_FACTOR * errors * scaled, LOSS_FACTOR * errors)
        stats.append([jnp.sum(v, axis=0, keepdims=True) for v in sums])
        wt[:, half * h : half * (h + 1)] = weights.T
        if h == 0:
            wn[...] = weights
    tgx[...] = matmul(weights, images).reshape(NZ, ROWS, E)
    got_x = [
        link.send(tgx.at[k], tgs.at[k], link.at(dc=1))
        for k in (pl.ds(3, 3), pl.ds(0, 3), pl.ds(6, 2))
    ]

    def txt_part(k):
        return tg[k] + tgs[k]

    top, low = pl.ds(0, HALF), pl.ds(HALF, HALF)
    texts = ta[...].reshape(16 * ROWS, E)
    got_low, got_top = link.group(r_low), link.group(r_top)
    for pair in ((1, 2), (3, 0)):
        w_rows = [wt[NY * ROWS * a : NY * ROWS * (a + 1), :] for a in pair]
        grads = matmul(jnp.concatenate(w_rows, axis=0), texts).reshape(2, NY, ROWS, E)
        for a, grad in zip(pair, (grads[0], grads[1])):
            ig_top[:, a] = grad[:, :HALF].astype(BF16)
            ig_low[a] = grad[:, HALF:].astype(BF16)
            if a:
                ig_x32[a - 1] = grad[0, :HALF]
                got_low.send(ig_low.at[a], r_low.at[a - 1], link.at(dx=a))
            else:
                ig0[...] = grad[0]
                ig_y32[...] = grad[1:, HALF:]
        if 0 not in pair:
            tg[...] = matmul(wn[...], images).reshape(NZ, ROWS, E)
            got_x[0].wait_recv()
            first = reduce_z_start(link, txt_part, tz_sent, tz_got, HALF)
    for j in (2, 1, 3):
        got_top.send(ig_top.at[j], r_top.at[j - 1], link.at(dy=j))
    wait_all(got_x[1:])
    got_tg = reduce_z_finish(link, txt_part, tz_sent, tz_got, HALF, first)

    got_low.wait_recv()
    got_low2 = link.group(r2_low)
    for j in (2, 1, 3):
        total = ig_y32[j - 1]
        for i in range(NX - 1):
            total = total + r_low[i, j].astype(F32)
        ig2_low[j - 1] = total.astype(BF16)
        got_low2.send(ig2_low.at[j - 1], r2_low.at[j - 1], link.at(dy=j))
    got_top.wait_recv()
    got_top2 = link.group(r2_top)
    for i in (2, 1, 3):
        total = ig_x32[i - 1]
        for j in range(NY - 1):
            total = total + r_top[j, i].astype(F32)
        ig2_top[i - 1] = total.astype(BF16)
        got_top2.send(ig2_top.at[i - 1], r2_top.at[i - 1], link.at(dx=i))

    got_b = link.group(bx)
    got_d = [link.group(dk.at[h, 1:]) for h in range(2)]

    def norm_backward(t, grad):
        grad = scale * grad
        delta = inv[t, :, 0:1] * (grad - unit[t] * jnp.sum(unit[t] * grad, axis=1, keepdims=True))
        for h in range(2):
            for q in range(2):
                col = 2 * QUARTER * q + QUARTER * h
                d16[h, t, :, QUARTER * q : QUARTER * (q + 1)] = delta[:, col : col + QUARTER].astype(BF16)
        total = jnp.sum(delta, axis=0, keepdims=True)
        for k in range(9):
            bp[9 * t + k : 9 * t + k + 1, :] = total[:, 128 * k : 128 * (k + 1)]

    def send_deltas(t):
        for h in range(2):
            for r in (2, 1, 3):
                slot = (NX - r) * 2 + link.cs[t]
                got_d[h].send(d16.at[h, t], dk.at[h, slot], link.at(dx=r, core=t))

            @pl.when(c == t)
            def _():
                dk[h, 0] = d16[h, t]

            @pl.when(c != t)
            def _():
                got_d[h].send(d16.at[h, t], dk.at[h, 1], link.at(dc=1))

    norm_backward(1, reduce_z_sum(txt_part, tz_got, got_tg))
    send_deltas(1)
    got_low2.wait_recv()
    got_top2.wait_recv()
    halves = []
    for rows, first_got, second_got in ((top, r_top, r2_top), (low, r_low, r2_low)):
        total = ig0[rows, :]
        for k in range(3):
            total = total + first_got[k, 0].astype(F32) + second_got[k].astype(F32)
        halves.append(total)
    norm_backward(0, jnp.concatenate(halves, axis=0))
    for k in range(3):
        lanes = stats[0][k] + stats[1][k]
        bp[18 + k : 19 + k, :] = (
            lanes[:, 0:128] + lanes[:, 128:256] + lanes[:, 256:384] + lanes[:, 384:512]
        )
    bp[21:24, :] = jnp.zeros((3, 128), F32)
    for r in range(1, NX):
        got_b.send(bp, bx.at[r - 1], link.at(dx=r))
    send_deltas(0)
    got_b.wait_recv()
    by[0] = bp[...] + bx[0] + bx[1] + bx[2]
    got_b = link.group(by.at[1:])
    for j in range(1, NY):
        got_b.send(by.at[0], by.at[j], link.at(dy=j))

    rows = fk[...].reshape(8 * ROWS, KX)
    got_y, deltas = [], []
    for h in range(2):
        got_d[h].wait_recv()
        half_deltas = dk[h].reshape(8 * ROWS, 2 * QUARTER)
        deltas.append(half_deltas)
        grad_w = matmul_at(rows, half_deltas)
        for j in range(NY):
            block = grad_w[SHARD * (j // 2) : SHARD * (j // 2 + 1), QUARTER * (j % 2) : QUARTER * (j % 2 + 1)]
            block = jnp.concatenate([block[:CUT], block[CUT : 2 * CUT], block[2 * CUT :]], axis=1)
            g32[h, j] = block
            gy[h, j] = block.astype(BF16)
        got_y.append(link.group(ry.at[h]))
        for j in (2, 1, 3):
            got_y[h].send(gy.at[h, link.ys[j]], ry.at[h, j - 1], link.at(dy=j))
        if h == 0:
            got_b.wait_recv()
            bz[0] = by[0] + by[1] + by[2] + by[3]
            sums = gather_z(link, bz, None, lambda k: None)
            next(sums)
    next(sums)
    next(sums)

    deltas = jnp.concatenate([d[:, QUARTER * q : QUARTER * (q + 1)] for q in range(2) for d in deltas], axis=1)
    grad_f = 0.0
    for k in range(CHUNKS):
        grad_f = grad_f + matmul_bt(deltas[:, COLS * k : COLS * (k + 1)], wk[k].reshape(KX, COLS))
    dfs[...] = grad_f.astype(BF16).reshape(8, ROWS, KX)
    got_df = link.group(dfs.at[1:])
    for r in range(NX):
        for e in range(2):
            if (r, e) == (0, 0):
                rf[0, x] = dfs[0]
                continue
            got_df.send(dfs.at[r * 2 + e], rf.at[e, x], link.at(dx=r, dc=e))


    for h in range(2):
        got_y[h].wait_recv()
        total = g32[h, y]
        for j in range(NY - 1):
            total = total + ry[h, j].astype(F32)
        for k in range(NZ // 2):
            for e in range(2):
                col = 72 * k + 36 * e
                block = [total[:, QUARTER * i + col : QUARTER * i + col + 36] for i in range(3)]
                gz32[NZ // 2 * h + k, e] = jnp.concatenate(block, axis=1)
        if h == 0:
            interleave(sums)
            bias_sum = bz[0]
            for k in range(1, NZ):
                bias_sum = bias_sum + bz[k]
            bs[0] = bias_sum
            got_b = link.send(bs.at[0], bs.at[1], link.at(dc=1))

    def head_part(k):
        return gz32[link.zs[k]]

    first = reduce_z_start(link, head_part, gz_sent, gz_got, 1)
    got_own = link.send(gz32.at[z, link.cs[1]], gz_own, link.at(dc=1))
    got_df.wait_recv()
    for t, out in enumerate((o_fi, o_ft)):
        for k in range(NX):
            out[:, KX * k : KX * (k + 1)] = rf[link.cs[t], k]
    last = reduce_z_finish(link, head_part, gz_sent, gz_got, 1, first, over_cores=True)
    got_b.wait_recv()
    sums = bs[0] + bs[1]
    for t in range(2):
        for k in range(9):
            o_bias[t : t + 1, 128 * k : 128 * (k + 1)] = sums[9 * t + k : 9 * t + k + 1, :]
    o_loss[0] = jnp.sum(sums[18:19, :]) * (1.0 / 8192.0)
    o_scale[0] = jnp.sum(sums[19:20, :])
    o_scale[1] = jnp.sum(sums[20:21, :])
    got_own.wait_recv()
    wait_all(last)
    for e, total in enumerate((gz32[z, c], gz_own[...])):
        for i in range(4):
            total = total + gz_got[3 + i, e].astype(F32)
        ow[e] = total
    for t, out in enumerate((o_wi, o_wt)):
        block = ow[link.cs[t]]
        for k in range(3):
            out[:, CUT * k : CUT * (k + 1)] = block[:, 36 * k : 36 * (k + 1)].T

    for copy in link.started:
        copy.wait_send()


def finish(*refs):
    parts, outs, sems = refs[:7], refs[7:14], refs[14]
    copies = [
        pltpu.make_async_copy(part, out, sems.at[k]) for k, (part, out) in enumerate(zip(parts, outs))
    ]
    for copy in copies:
        copy.start()
    for copy in copies:
        copy.wait()


def per_device(f_img, f_txt, w_img, w_txt, b_img, b_txt, log_scale, logit_bias):
    hbm = pl.BlockSpec(memory_space=pl.ANY)
    vmem = pl.BlockSpec(memory_space=pltpu.VMEM)
    smem = pl.BlockSpec(memory_space=pltpu.SMEM)
    scratch = [
        ((2, NX, ROWS, KX), BF16),
        ((2, CUT, 108), F32),
        ((2, ROWS, D), BF16),
        ((E,), F32),
        ((E,), F32),
        ((2, NX, ROWS, KX), BF16),
        ((8, ROWS, KX), BF16),
        ((CHUNKS, 2, SHARD, COLS), BF16),
        ((CHUNKS, ROWS, COLS), F32),
        ((CHUNKS, 6, ROWS, COLS), BF16),
        ((CHUNKS, 2, ROWS, COLS), F32),
        ((CHUNKS, 2, NX - 1, ROWS, COLS), BF16),
        ((2, ROWS, E), F32),
        ((2, ROWS, 128), F32),
        ((NX, NY, ROWS, E), BF16),
        ((2, NZ, ROWS, E), BF16),
        ((512, 512), BF16),
        ((256, 512), BF16),
        ((NZ, ROWS, E), F32),
        ((NZ, ROWS, E), F32),
        ((NZ, ROWS, E), F32),
        ((7, ROWS, E), BF16),
        ((7, ROWS, E), BF16),
        ((ROWS, E), F32),
        ((NX - 1, HALF, E), F32),
        ((NY - 1, HALF, E), F32),
        ((NY, NX, HALF, E), BF16),
        ((NX, NY, HALF, E), BF16),
        ((NY - 1, NX, HALF, E), BF16),
        ((NX - 1, NY, HALF, E), BF16),
        ((NX - 1, HALF, E), BF16),
        ((NY - 1, HALF, E), BF16),
        ((NX - 1, HALF, E), BF16),
        ((NY - 1, HALF, E), BF16),
        ((2, 2, ROWS, 2 * QUARTER), BF16),
        ((2, 8, ROWS, 2 * QUARTER), BF16),
        ((24, 128), F32),
        ((3, 24, 128), F32),
        ((4, 24, 128), F32),
        ((8, 24, 128), F32),
        ((2, 24, 128), F32),
        ((8, ROWS, KX), BF16),
        ((2, NY, CUT, 3 * QUARTER), F32),
        ((2, NY, CUT, 3 * QUARTER), BF16),
        ((2, NY - 1, CUT, 3 * QUARTER), BF16),
        ((NZ, 2, CUT, 108), F32),
        ((7, 2, CUT, 108), BF16),
        ((7, 2, CUT, 108), BF16),
        ((CUT, 108), F32),
    ]
    shapes = (
        jax.ShapeDtypeStruct((1,), F32),
        jax.ShapeDtypeStruct((2,), F32),
        jax.ShapeDtypeStruct((ROWS, D), BF16),
        jax.ShapeDtypeStruct((ROWS, D), BF16),
        jax.ShapeDtypeStruct((36, SHARD), F32),
        jax.ShapeDtypeStruct((36, SHARD), F32),
        jax.ShapeDtypeStruct((2, E), F32),
    )
    parts = pl.pallas_call(
        kernel,
        out_shape=shapes,
        in_specs=[hbm] * 8,
        out_specs=(smem, smem, vmem, vmem, vmem, vmem, vmem),
        scratch_shapes=[pltpu.VMEM(shape, dtype) for shape, dtype in scratch]
        + [pltpu.SemaphoreType.DMA((N_GROUPS,))] * 2
        + [pltpu.SemaphoreType.DMA((7,)), pltpu.SMEM((2, 1), F32)],
        compiler_params=pltpu.CompilerParams(
            collective_id=0, has_side_effects=True, vmem_limit_bytes=56 * 2**20
        ),
    )(f_img, f_txt, w_img, w_txt, b_img, b_txt, log_scale, logit_bias)
    loss, scale, fi, ft, wi, wt, bias = pl.pallas_call(
        finish,
        out_shape=shapes,
        in_specs=[hbm] * 7,
        out_specs=(hbm,) * 7,
        scratch_shapes=[pltpu.SemaphoreType.DMA((7,))],
    )(*parts)
    return loss, scale, fi, ft, wi.T, wt.T, bias


def solution(mesh):
    rows = P(("dp", "mp"), None)
    return jax.shard_map(
        per_device,
        mesh=mesh,
        in_specs=(rows, rows, P("mp", None), P("mp", None), P(), P(), P(), P()),
        out_specs=(P(), P(), rows, rows, P("mp", "dp"), P("mp", "dp"), P()),
        check_vma=False,
    )
```

```python
import functools

import jax
import jax.numpy as jnp
from jax import lax
from jax.experimental import pallas as pl
from jax.experimental.pallas import tpu as pltpu
from jax.sharding import PartitionSpec as P

EPSILON = 1e-06
LOSS_FACTOR = 32.0
NX, NY, NZ = 4, 4, 8
ROWS = 32
HALF = ROWS // 2
D = 1152
E = 1152
SHARD = 144
KX = 2 * SHARD
CHUNKS = 3
COLS = E // CHUNKS
CUT = SHARD // 3
QUARTER = E // 4
MESH = pl.DeviceIdType.MESH
F32 = jnp.float32
BF16 = jnp.bfloat16

N_GROUPS = 65


def ring(place, size):
    steps = [place + k for k in range(size)]
    return [place] + [jnp.where(v >= size, v - size, v) for v in steps[1:]]


class Links:
    def __init__(self, send_sems, recv_sems):
        dp, mp = lax.axis_index("dp"), lax.axis_index("mp")
        self.x, self.y = mp // 2, (mp % 2) * 2 + dp // 16
        self.z, self.c = (dp // 2) % NZ, dp % 2
        self.send_sems, self.recv_sems = send_sems, recv_sems
        self.started = []
        self.xs = ring(self.x, NX)
        self.ys = ring(self.y, NY)
        self.zs = ring(self.z, NZ)
        self.cs = ring(self.c, 2)
        self.x_mp = [2 * v for v in self.xs]
        self.y_mp = [v // 2 for v in self.ys]
        self.y_dp = [(v - 2 * h) * 16 for v, h in zip(self.ys, self.y_mp)]
        self.z_dp = [2 * v for v in self.zs]

    def at(self, dx=0, dy=0, dz=0, dc=0, core=None):
        core = self.cs[dc] if core is None else core
        return (self.y_dp[dy] + self.z_dp[dz] + core, self.x_mp[dx] + self.y_mp[dy])

    def group(self, region):
        copies = Group(self, len(self.started), region)
        self.started.append(copies)
        return copies

    def send(self, src, dst, device):
        copies = self.group(dst)
        copies.send(src, dst, device)
        return copies


class Group:
    def __init__(self, link, k, region):
        self.link, self.region = link, region
        self.sems = (link.send_sems.at[k], link.recv_sems.at[k])

    def copy(self, src, dst, device):
        return pltpu.make_async_remote_copy(
            src_ref=src,
            dst_ref=dst,
            send_sem=self.sems[0],
            recv_sem=self.sems[1],
            device_id=device,
            device_id_type=MESH,
        )

    def send(self, src, dst, device):
        self.copy(src, dst, device).start()

    def wait_recv(self):
        self.copy(self.region, self.region, self.link.at(dc=1)).wait_recv()

    def wait_send(self):
        self.copy(self.region, self.region, self.link.at(dc=1)).wait_send()


def matmul(a, b):
    return lax.dot_general(a, b, (((1,), (0,)), ((), ())), preferred_element_type=F32)


def matmul_bt(a, b):
    return lax.dot_general(a, b, (((1,), (1,)), ((), ())), preferred_element_type=F32)


def matmul_at(a, b):
    return lax.dot_general(a, b, (((0,), (0,)), ((), ())), preferred_element_type=F32)


def wait_all(copies):
    for copy in copies:
        copy.wait_recv()


def gather_z(link, buf, split, on_arrival):
    to_6 = link.send(buf.at[0], buf.at[6], link.at(dz=2))
    to_2 = link.send(buf.at[0], buf.at[2], link.at(dz=6))
    to_7 = link.send(buf.at[0], buf.at[7], link.at(dz=1))
    to_1 = link.send(buf.at[0], buf.at[1], link.at(dz=7))
    yield
    to_6.wait_recv()
    to_5 = link.send(buf.at[6], buf.at[5], link.at(dz=1))
    if split is None:
        to_4 = [link.send(buf.at[6], buf.at[4], link.at(dz=2))]
    else:
        to_4 = [link.send(buf.at[6, :split], buf.at[4, :split], link.at(dz=2))]
    on_arrival(6)
    yield
    to_2.wait_recv()
    to_3 = link.send(buf.at[2], buf.at[3], link.at(dz=7))
    if split is not None:
        to_4.append(link.send(buf.at[2, split:], buf.at[4, split:], link.at(dz=6)))
    on_arrival(2)
    yield
    to_7.wait_recv()
    on_arrival(7)
    yield
    to_1.wait_recv()
    on_arrival(1)
    yield
    to_5.wait_recv()
    on_arrival(5)
    to_3.wait_recv()
    on_arrival(3)
    wait_all(to_4)
    on_arrival(4)


def gather_plane(link, buf):
    steps = (1, 3, 2)
    top, low = pl.ds(0, HALF), pl.ds(HALF, HALF)
    got = link.group(buf.at[1:, 1:])
    got_x = [link.send(buf.at[0, 0], buf.at[NX - i, 0], link.at(dx=i)) for i in steps]
    got_y = [link.send(buf.at[0, 0], buf.at[0, NY - j], link.at(dy=j)) for j in steps]
    yield
    for copy_x, copy_y, k in zip(got_x, got_y, steps):
        a = NX - k
        copy_x.wait_recv()
        for j in steps:
            got.send(buf.at[a, 0, top], buf.at[a, NY - j, top], link.at(dy=j))
        copy_y.wait_recv()
        for i in steps:
            got.send(buf.at[0, a, low], buf.at[NX - i, a, low], link.at(dx=i))
        yield
    got.wait_recv()


def interleave(*parts):
    parts = list(parts)
    while parts:
        for part in list(parts):
            try:
                next(part)
            except StopIteration:
                parts.remove(part)


def reduce_z_start(link, part, sent, got, split):
    for i, k in enumerate((4, 3, 5)):
        sent[i] = part(k).astype(BF16)
    return [
        link.send(sent.at[0, :split], got.at[0, :split], link.at(dz=2)),
        link.send(sent.at[0, split:], got.at[0, split:], link.at(dz=6)),
        link.send(sent.at[1], got.at[1], link.at(dz=1)),
        link.send(sent.at[2], got.at[2], link.at(dz=7)),
    ]


def reduce_z_finish(link, part, sent, got, split, first, over_cores=False):
    def onward(i, k):
        if not over_cores:
            return link.send(sent.at[i], got.at[i], link.at(dz=k))
        copies = link.group(got.at[i])
        for e in range(2):
            copies.send(sent.at[i, link.cs[e]], got.at[i, e], link.at(dz=k, dc=e))
        return copies

    last = []
    for i, k in ((3, 1), (4, 7)):
        sent[i] = part(k).astype(BF16)
        last.append(onward(i, k))
    first[0].wait_recv()
    first[2].wait_recv()
    term = part(2) + got[1].astype(F32)
    sent[5, :split] = (term[:split] + got[0, :split].astype(F32)).astype(BF16)
    sent[5, split:] = term[split:].astype(BF16)
    last.append(onward(5, 2))
    first[1].wait_recv()
    first[3].wait_recv()
    term = part(6) + got[2].astype(F32)
    sent[6, :split] = term[:split].astype(BF16)
    sent[6, split:] = (term[split:] + got[0, split:].astype(F32)).astype(BF16)
    last.append(onward(6, 6))
    return last


def reduce_z_sum(part, got, last):
    total = part(0)
    for k, copy in enumerate(last):
        copy.wait_recv()
        total = total + got[3 + k].astype(F32)
    return total


def kernel(
    f_img, f_txt, w_img, w_txt, b_img, b_txt, log_scale, logit_bias,
    rf, ow, o_sums,
    fv, bv_img, bv_txt, fs, fk, wk, po, pk, rp0, rp, unit, inv, ia, ta, wt, wn, tg, tgx, tgs, tz_sent, tz_got,
    ig0, ig_x32, ig_y32, ig_top, ig_low, r_top, r_low, ig2_top, ig2_low, r2_top, r2_low,
    d16, dk, bp, bx, by, bz, bs, dfs, g32, gy, ry, gz32, gz_sent, gz_got, gz_own,
    send_sems, recv_sems, load_sems, scalars,
):
    link = Links(send_sems, recv_sems)
    x, y, z, c = link.x, link.y, link.z, link.c

    shard = link.y_mp[0]
    for t, head in enumerate((w_img, w_txt)):

        @pl.when(c == t)
        def _():
            for k in range(CHUNKS):
                cols = pl.ds(COLS * k, COLS)
                pltpu.make_async_copy(head.at[:, cols], wk.at[k, shard], load_sems.at[0]).start()

    loads = [
        pltpu.make_async_copy(f, fv.at[t], load_sems.at[1 + t]) for t, f in enumerate((f_img, f_txt))
    ]
    small = ((log_scale, scalars.at[0]), (logit_bias, scalars.at[1]), (b_img, bv_img), (b_txt, bv_txt))
    small_loads = [
        pltpu.make_async_copy(v, place, load_sems.at[3 + k]) for k, (v, place) in enumerate(small)
    ]
    loads += small_loads
    for load in loads:
        load.start()

    peers = [(0, 0, 0, 1)]
    peers += [(i, 0, 0, e) for i in range(1, NX) for e in range(2)]
    peers += [(0, j, 0, 0) for j in range(1, NY)]
    peers += [(0, 0, k, e) for k in (1, 2, 6, 7) for e in range(2)]
    barrier = pltpu.get_barrier_semaphore()
    for p in peers:
        pl.semaphore_signal(barrier, inc=1, device_id=link.at(*p), device_id_type=MESH)

    for t in range(2):
        loads[t].wait()
        for k in range(NX):
            fs[t, k] = fv[t, :, KX * k : KX * (k + 1)]
    own_head = wk.at[:, shard]
    pltpu.make_async_copy(own_head, own_head, load_sems.at[0]).wait()
    for load in small_loads:
        load.wait()
    pl.semaphore_wait(barrier, len(peers))

    odd = y - 2 * shard
    ahead, behind = link.at(dy=1), link.at(dy=3)
    partner = tuple(jnp.where(odd == 1, u, v) for u, v in zip(ahead, behind))
    got_f = link.group(fk.at[1:])
    for r in range(NX):
        for e in range(2):
            if (r, e) == (0, 0):
                fk[0] = fs[c, x]
                continue
            got_f.send(
                fs.at[link.cs[e], link.xs[r]],
                fk.at[((NX - r) % NX) * 2 + e],
                link.at(dx=r, dc=e),
            )
    got_w = [link.send(wk.at[k, shard], wk.at[k, shard], partner) for k in range(CHUNKS)]
    got_f.wait_recv()

    rows = fk[...].reshape(8 * ROWS, KX)
    got_p = []
    for k in range(CHUNKS):
        got_w[k].wait_recv()
        part = matmul(rows, wk[k].reshape(KX, COLS))
        rp0[k, 0] = part[:ROWS]
        po[k] = part[ROWS : 2 * ROWS]
        pk[k] = part[2 * ROWS :].astype(BF16).reshape(6, ROWS, COLS)
        got = link.group(rp.at[k])
        got_p.append([link.send(po.at[k], rp0.at[k, 1], link.at(dc=1)), got])
        for r in (2, 1, 3):
            for e in range(2):
                got.send(pk.at[k, (r - 1) * 2 + e], rp.at[k, e, NX - r - 1], link.at(dx=r, dc=e))
    squares = [0.0, 0.0]
    for k in range(CHUNKS):
        wait_all(got_p[k])
        cols = slice(COLS * k, COLS * (k + 1))
        for t, bias in enumerate((bv_img, bv_txt)):
            e = link.cs[t]
            pre = rp0[k, e] + bias[cols].reshape(1, COLS)
            for r in range(NX - 1):
                pre = pre + rp[k, e, r].astype(F32)
            unit[t, :, cols] = pre
            squares[t] = squares[t] + jnp.sum(pre * pre, axis=1, keepdims=True)
    for t in range(2):
        inverse = lax.rsqrt(squares[t] + EPSILON)
        unit[t] = unit[t] * inverse
        inv[t] = jnp.broadcast_to(inverse, (ROWS, 128))
    ia[0, 0] = unit[0].astype(BF16)
    ta[0, 0] = unit[1].astype(BF16)

    got_s = link.group(ta.at[1])
    got_s.send(ta.at[0, 0], ta.at[1, 0], link.at(dc=1))

    def forward(k):
        got_s.send(ta.at[0, k], ta.at[1, k], link.at(dc=1))

    interleave(gather_z(link, ta.at[0], HALF, forward), gather_plane(link, ia))

    half = NZ * ROWS
    scale = jnp.exp(jnp.full((1, 1), scalars[0, 0], F32))
    shift = scalars[1, 0]
    images = ia[...].reshape(16 * ROWS, E)
    stats = []
    for h in range(2):
        if h == 1:
            got_s.wait_recv()
        texts = ta[h].reshape(half, E)
        scaled = scale * matmul_bt(texts, images)
        logits = scaled + shift
        signed = logits
        if h == 0:
            row = lax.broadcasted_iota(jnp.int32, logits.shape, 0)
            col = lax.broadcasted_iota(jnp.int32, logits.shape, 1)
            match = jnp.logical_and(row == col, col < ROWS)
            signed = jnp.where(match, -logits, logits)
        small = jnp.exp(-jnp.abs(logits))
        loss = jnp.maximum(signed, 0.0) + jnp.log1p(small)
        errors = jnp.where(logits >= 0.0, 1.0, small) / (1.0 + small)
        if h == 0:
            errors = errors - match.astype(F32)
        weights = (LOSS_FACTOR * errors).astype(BF16)
        sums = (loss, LOSS_FACTOR * errors * scaled, LOSS_FACTOR * errors)
        stats.append([jnp.sum(v, axis=0, keepdims=True) for v in sums])
        wt[:, half * h : half * (h + 1)] = weights.T
        if h == 0:
            wn[...] = weights
    tgx[...] = matmul(weights, images).astype(BF16).reshape(NZ, ROWS, E)
    got_x = [
        link.send(tgx.at[k], tgs.at[k], link.at(dc=1))
        for k in (pl.ds(3, 3), pl.ds(0, 3), pl.ds(6, 2))
    ]

    def txt_part(k):
        return tg[k] + tgs[k].astype(F32)

    top, low = pl.ds(0, HALF), pl.ds(HALF, HALF)
    texts = ta[...].reshape(16 * ROWS, E)
    got_low, got_top = link.group(r_low), link.group(r_top)
    for pair in ((1, 2), (3, 0)):
        w_rows = [wt[NY * ROWS * a : NY * ROWS * (a + 1), :] for a in pair]
        grads = matmul(jnp.concatenate(w_rows, axis=0), texts).reshape(2, NY, ROWS, E)
        for a, grad in zip(pair, (grads[0], grads[1])):
            ig_top[:, a] = grad[:, :HALF].astype(BF16)
            ig_low[a] = grad[:, HALF:].astype(BF16)
            if a:
                ig_x32[a - 1] = grad[0, :HALF]
                got_low.send(ig_low.at[a], r_low.at[a - 1], link.at(dx=a))
            else:
                ig0[...] = grad[0]
                ig_y32[...] = grad[1:, HALF:]
        if 0 not in pair:
            tg[...] = matmul(wn[...], images).reshape(NZ, ROWS, E)
            got_x[0].wait_recv()
            first = reduce_z_start(link, txt_part, tz_sent, tz_got, HALF)
    for j in (2, 1, 3):
        got_top.send(ig_top.at[j], r_top.at[j - 1], link.at(dy=j))
    wait_all(got_x[1:])
    got_tg = reduce_z_finish(link, txt_part, tz_sent, tz_got, HALF, first)

    got_low.wait_recv()
    got_low2 = link.group(r2_low)
    for j in (2, 1, 3):
        total = ig_y32[j - 1]
        for i in range(NX - 1):
            total = total + r_low[i, j].astype(F32)
        ig2_low[j - 1] = total.astype(BF16)
        got_low2.send(ig2_low.at[j - 1], r2_low.at[j - 1], link.at(dy=j))
    got_top.wait_recv()
    got_top2 = link.group(r2_top)
    for i in (2, 1, 3):
        total = ig_x32[i - 1]
        for j in range(NY - 1):
            total = total + r_top[j, i].astype(F32)
        ig2_top[i - 1] = total.astype(BF16)
        got_top2.send(ig2_top.at[i - 1], r2_top.at[i - 1], link.at(dx=i))

    got_b = link.group(bx)
    got_d = [link.group(dk.at[h, 1:]) for h in range(2)]

    def norm_backward(t, grad):
        grad = scale * grad
        delta = inv[t, :, 0:1] * (grad - unit[t] * jnp.sum(unit[t] * grad, axis=1, keepdims=True))
        for h in range(2):
            for q in range(2):
                col = 2 * QUARTER * q + QUARTER * h
                d16[h, t, :, QUARTER * q : QUARTER * (q + 1)] = delta[:, col : col + QUARTER].astype(BF16)
        total = jnp.sum(delta, axis=0, keepdims=True)
        for k in range(9):
            bp[9 * t + k : 9 * t + k + 1, :] = total[:, 128 * k : 128 * (k + 1)]

    def send_deltas(t):
        for h in range(2):
            for r in (2, 1, 3):
                slot = (NX - r) * 2 + link.cs[t]
                got_d[h].send(d16.at[h, t], dk.at[h, slot], link.at(dx=r, core=t))

            @pl.when(c == t)
            def _():
                dk[h, 0] = d16[h, t]

            @pl.when(c != t)
            def _():
                got_d[h].send(d16.at[h, t], dk.at[h, 1], link.at(dc=1))

    norm_backward(1, reduce_z_sum(txt_part, tz_got, got_tg))
    send_deltas(1)
    got_low2.wait_recv()
    got_top2.wait_recv()
    halves = []
    for rows, first_got, second_got in ((top, r_top, r2_top), (low, r_low, r2_low)):
        total = ig0[rows, :]
        for k in range(3):
            total = total + first_got[k, 0].astype(F32) + second_got[k].astype(F32)
        halves.append(total)
    norm_backward(0, jnp.concatenate(halves, axis=0))
    for k in range(3):
        lanes = stats[0][k] + stats[1][k]
        bp[18 + k : 19 + k, :] = (
            lanes[:, 0:128] + lanes[:, 128:256] + lanes[:, 256:384] + lanes[:, 384:512]
        )
    bp[21:24, :] = jnp.zeros((3, 128), F32)
    for r in range(1, NX):
        got_b.send(bp, bx.at[r - 1], link.at(dx=r))
    send_deltas(0)
    got_b.wait_recv()
    by[0] = bp[...] + bx[0] + bx[1] + bx[2]
    got_b = link.group(by.at[1:])
    for j in range(1, NY):
        got_b.send(by.at[0], by.at[j], link.at(dy=j))

    rows = fk[...].reshape(8 * ROWS, KX)
    got_y, deltas = [], []
    for h in range(2):
        got_d[h].wait_recv()
        half_deltas = dk[h].reshape(8 * ROWS, 2 * QUARTER)
        deltas.append(half_deltas)
        grad_w = matmul_at(rows, half_deltas)
        for j in range(NY):
            block = grad_w[SHARD * (j // 2) : SHARD * (j // 2 + 1), QUARTER * (j % 2) : QUARTER * (j % 2 + 1)]
            block = jnp.concatenate([block[:CUT], block[CUT : 2 * CUT], block[2 * CUT :]], axis=1)
            g32[h, j] = block
            gy[h, j] = block.astype(BF16)
        got_y.append(link.group(ry.at[h]))
        for j in (2, 1, 3):
            got_y[h].send(gy.at[h, link.ys[j]], ry.at[h, j - 1], link.at(dy=j))
        if h == 0:
            got_b.wait_recv()
            bz[0] = by[0] + by[1] + by[2] + by[3]
            sums = gather_z(link, bz, None, lambda k: None)
            next(sums)
    next(sums)
    next(sums)

    deltas = jnp.concatenate([d[:, QUARTER * q : QUARTER * (q + 1)] for q in range(2) for d in deltas], axis=1)
    grad_f = 0.0
    for k in range(CHUNKS):
        grad_f = grad_f + matmul_bt(deltas[:, COLS * k : COLS * (k + 1)], wk[k].reshape(KX, COLS))
    dfs[...] = grad_f.astype(BF16).reshape(8, ROWS, KX)
    got_df = link.group(dfs.at[1:])
    for r in range(NX):
        for e in range(2):
            if (r, e) == (0, 0):
                rf[0, x] = dfs[0]
                continue
            got_df.send(dfs.at[r * 2 + e], rf.at[e, x], link.at(dx=r, dc=e))


    for h in range(2):
        got_y[h].wait_recv()
        total = g32[h, y]
        for j in range(NY - 1):
            total = total + ry[h, j].astype(F32)
        for k in range(NZ // 2):
            for e in range(2):
                col = 72 * k + 36 * e
                block = [total[:, QUARTER * i + col : QUARTER * i + col + 36] for i in range(3)]
                gz32[NZ // 2 * h + k, e] = jnp.concatenate(block, axis=1)
        if h == 0:
            interleave(sums)
            bias_sum = bz[0]
            for k in range(1, NZ):
                bias_sum = bias_sum + bz[k]
            bs[0] = bias_sum
            got_b = link.send(bs.at[0], bs.at[1], link.at(dc=1))

    def head_part(k):
        return gz32[link.zs[k]]

    first = reduce_z_start(link, head_part, gz_sent, gz_got, 1)
    got_own = link.send(gz32.at[z, link.cs[1]], gz_own, link.at(dc=1))
    last = reduce_z_finish(link, head_part, gz_sent, gz_got, 1, first, over_cores=True)
    got_own.wait_recv()
    wait_all(last)
    for e, total in enumerate((gz32[z, c], gz_own[...])):
        for i in range(4):
            total = total + gz_got[3 + i, e].astype(F32)
        ow[e] = total
    got_b.wait_recv()
    o_sums[...] = bs[0] + bs[1]
    got_df.wait_recv()

    for copy in link.started:
        copy.wait_send()


def finish(rf, ow, sums, o_loss, o_scale, o_fi, o_ft, o_wi, o_wt, o_bias):
    c = lax.axis_index("dp") % 2
    for t, (out_f, out_w) in enumerate(((o_fi, o_wi), (o_ft, o_wt))):
        e = jnp.where(c == t, 0, 1)
        for k in range(NX):
            out_f[:, KX * k : KX * (k + 1)] = rf[e, k]
        for k in range(3):
            out_w[:, CUT * k : CUT * (k + 1)] = ow[e][:, 36 * k : 36 * (k + 1)].T
        for k in range(9):
            o_bias[t : t + 1, 128 * k : 128 * (k + 1)] = sums[9 * t + k : 9 * t + k + 1, :]
    o_loss[0] = jnp.sum(sums[18:19, :]) * (1.0 / 8192.0)
    o_scale[0] = jnp.sum(sums[19:20, :])
    o_scale[1] = jnp.sum(sums[20:21, :])


def per_device(f_img, f_txt, w_img, w_txt, b_img, b_txt, log_scale, logit_bias):
    hbm = pl.BlockSpec(memory_space=pl.ANY)
    vmem = pl.BlockSpec(memory_space=pltpu.VMEM)
    smem = pl.BlockSpec(memory_space=pltpu.SMEM)
    scratch = [
        ((2, ROWS, D), BF16),
        ((E,), F32),
        ((E,), F32),
        ((2, NX, ROWS, KX), BF16),
        ((8, ROWS, KX), BF16),
        ((CHUNKS, 2, SHARD, COLS), BF16),
        ((CHUNKS, ROWS, COLS), F32),
        ((CHUNKS, 6, ROWS, COLS), BF16),
        ((CHUNKS, 2, ROWS, COLS), F32),
        ((CHUNKS, 2, NX - 1, ROWS, COLS), BF16),
        ((2, ROWS, E), F32),
        ((2, ROWS, 128), F32),
        ((NX, NY, ROWS, E), BF16),
        ((2, NZ, ROWS, E), BF16),
        ((512, 512), BF16),
        ((256, 512), BF16),
        ((NZ, ROWS, E), F32),
        ((NZ, ROWS, E), BF16),
        ((NZ, ROWS, E), BF16),
        ((7, ROWS, E), BF16),
        ((7, ROWS, E), BF16),
        ((ROWS, E), F32),
        ((NX - 1, HALF, E), F32),
        ((NY - 1, HALF, E), F32),
        ((NY, NX, HALF, E), BF16),
        ((NX, NY, HALF, E), BF16),
        ((NY - 1, NX, HALF, E), BF16),
        ((NX - 1, NY, HALF, E), BF16),
        ((NX - 1, HALF, E), BF16),
        ((NY - 1, HALF, E), BF16),
        ((NX - 1, HALF, E), BF16),
        ((NY - 1, HALF, E), BF16),
        ((2, 2, ROWS, 2 * QUARTER), BF16),
        ((2, 8, ROWS, 2 * QUARTER), BF16),
        ((24, 128), F32),
        ((3, 24, 128), F32),
        ((4, 24, 128), F32),
        ((8, 24, 128), F32),
        ((2, 24, 128), F32),
        ((8, ROWS, KX), BF16),
        ((2, NY, CUT, 3 * QUARTER), F32),
        ((2, NY, CUT, 3 * QUARTER), BF16),
        ((2, NY - 1, CUT, 3 * QUARTER), BF16),
        ((NZ, 2, CUT, 108), F32),
        ((7, 2, CUT, 108), BF16),
        ((7, 2, CUT, 108), BF16),
        ((CUT, 108), F32),
    ]
    parts = pl.pallas_call(
        kernel,
        out_shape=(
            jax.ShapeDtypeStruct((2, NX, ROWS, KX), BF16),
            jax.ShapeDtypeStruct((2, CUT, 108), F32),
            jax.ShapeDtypeStruct((24, 128), F32),
        ),
        in_specs=[hbm] * 8,
        out_specs=(vmem, vmem, vmem),
        scratch_shapes=[pltpu.VMEM(shape, dtype) for shape, dtype in scratch]
        + [pltpu.SemaphoreType.DMA((N_GROUPS,))] * 2
        + [pltpu.SemaphoreType.DMA((7,)), pltpu.SMEM((2, 1), F32)],
        compiler_params=pltpu.CompilerParams(
            collective_id=0, has_side_effects=True, vmem_limit_bytes=56 * 2**20
        ),
    )(f_img, f_txt, w_img, w_txt, b_img, b_txt, log_scale, logit_bias)
    loss, scale, fi, ft, wi, wt, bias = pl.pallas_call(
        finish,
        out_shape=(
            jax.ShapeDtypeStruct((1,), F32),
            jax.ShapeDtypeStruct((2,), F32),
            jax.ShapeDtypeStruct((ROWS, D), BF16),
            jax.ShapeDtypeStruct((ROWS, D), BF16),
            jax.ShapeDtypeStruct((36, SHARD), F32),
            jax.ShapeDtypeStruct((36, SHARD), F32),
            jax.ShapeDtypeStruct((2, E), F32),
        ),
        in_specs=[vmem] * 3,
        out_specs=(smem, smem, vmem, vmem, vmem, vmem, vmem),
    )(*parts)
    return loss, scale, fi, ft, wi.T, wt.T, bias


def solution(mesh):
    rows = P(("dp", "mp"), None)
    return jax.shard_map(
        per_device,
        mesh=mesh,
        in_specs=(rows, rows, P("mp", None), P("mp", None), P(), P(), P(), P()),
        out_specs=(P(), P(), rows, rows, P("mp", "dp"), P("mp", "dp"), P()),
        check_vma=False,
    )
```
